32 devices in a mesh: pb: 4 (over z), ka: 4 (over x, core), ha: 2 (over y).
Axes of the slice: x: 2, y: 2, z: 4, core: 2. Of those that a mesh axis runs over, the one named last changes fastest.
Arguments:
- tokens: bfloat16 [2, 3072, 768], P(None, ('pb', 'ka')), may hold values from -6 to 6
- cotangent: bfloat16 [2, 3072, 768], P(None, ('pb', 'ka')), may hold values from -6 to 6
- seq_lengths: int32 [2, 2], replicated, may hold values from 1024 to 2048, as said below
- slot_token: int32 [2, 3072], replicated, may hold values from 0 to 3071, each once within a row
- w_qkv: float32 [768, 3, 768], P(('pb', 'ka'), None, 'ha'), may hold values from -0.21875 to 0.21875
- w_proj: float32 [768, 768], P('ha', ('pb', 'ka')), may hold values from -6 to 6
- w_inner: float32 [768, 3072], P(('pb', 'ka'), 'ha'), may hold values from -0.21875 to 0.21875
- w_outer: float32 [3072, 768], P('ha', ('pb', 'ka')), may hold values from -0.109375 to 0.109375
- norm_gains: float32 [2, 768], P(None, ('pb', 'ka')), may hold values from 0.5 to 1.5
- norm_biases: float32 [2, 768], P(None, ('pb', 'ka')), may hold values from -1.75 to 1.75
- qkv_first: float32 [768, 3, 768], P(('pb', 'ka'), None, 'ha'), may hold values from -28 to 28
- qkv_second: float32 [768, 3, 768], P(('pb', 'ka'), None, 'ha'), may hold values from 39.936 to 645.12
- proj_first: float32 [768, 768], P('ha', ('pb', 'ka')), may hold values from -1 to 1
- proj_second: float32 [768, 768], P('ha', ('pb', 'ka')), may hold values from 0.075 to 1.2
- inner_first: float32 [768, 3072], P(('pb', 'ka'), 'ha'), may hold values from -8 to 8
- inner_second: float32 [768, 3072], P(('pb', 'ka'), 'ha'), may hold values from 3.5328 to 58.368
- outer_first: float32 [3072, 768], P('ha', ('pb', 'ka')), may hold values from -16 to 16
- outer_second: float32 [3072, 768], P('ha', ('pb', 'ka')), may hold values from 14.4384 to 230.4
- norm_first: float32 [4, 768], P(None, ('pb', 'ka')), may hold values from -28 to 28
- norm_second: float32 [4, 768], P(None, ('pb', 'ka')), may hold values from 39.936 to 645.12
Outputs:
- layer_out: bfloat16 [2, 3072, 768], P(None, ('pb', 'ka'))
- input_grad: float32 [2, 3072, 768], P(None, ('pb', 'ka'))
- qkv_first_new: float32 [768, 3, 768], P(('pb', 'ka'), None, 'ha')
- qkv_second_new: float32 [768, 3, 768], P(('pb', 'ka'), None, 'ha')
- qkv_new: float32 [768, 3, 768], P(('pb', 'ka'), None, 'ha')
- proj_first_new: float32 [768, 768], P('ha', ('pb', 'ka'))
- proj_second_new: float32 [768, 768], P('ha', ('pb', 'ka'))
- proj_new: float32 [768, 768], P('ha', ('pb', 'ka'))
- inner_first_new: float32 [768, 3072], P(('pb', 'ka'), 'ha')
- inner_second_new: float32 [768, 3072], P(('pb', 'ka'), 'ha')
- inner_new: float32 [768, 3072], P(('pb', 'ka'), 'ha')
- outer_first_new: float32 [3072, 768], P('ha', ('pb', 'ka'))
- outer_second_new: float32 [3072, 768], P('ha', ('pb', 'ka'))
- outer_new: float32 [3072, 768], P('ha', ('pb', 'ka'))
- norm_first_new: float32 [4, 768], P(None, ('pb', 'ka'))
- norm_second_new: float32 [4, 768], P(None, ('pb', 'ka'))
- norm_new: float32 [4, 768], P(None, ('pb', 'ka'))
- norm_two_grad: float32 [2, 768], P(None, ('pb', 'ka'))
The draws below stay inside these ranges and needn't reach their ends.
Inputs may be any that keep to these rules, and one draw needn't show every extreme that they name: `seq_lengths`: in each micro-batch the 2 lengths sum to 3072, and one of them is exactly 2048. `slot_token`: each micro-batch's row is a permutation of the token numbers.
All inputs are finite; a program needn't handle non-finite values.
Results may differ from the reference program's by a relative error of at most 0.02.
Values may be sent and summed in bfloat16 or wider, within the bound.
No kernel may reach another device: no remote copies, remote signals or barrier semaphores. Data moves between devices by JAX's collectives and lax.ppermute only.
A program may use at most 192 MiB of HBM per device.

```python
import math
import jax
import jax.numpy as jnp
from jax import lax

D = 768
H = 12
HD = 64
FF = 3072
TOK_DEV = 192
MICRO = 2
STEP = 8
TOKENS = 3072
LMIN = 1024
NSEQ = 2
N_PB = 4
N_KA = 4


def draw_seq_lengths(key, part):
    key = jax.random.fold_in(key, 7)
    spare_len = TOKENS - LMIN * NSEQ - LMIN
    rows_out = []
    for micro_step in range(MICRO):
        sub_key = jax.random.fold_in(key, micro_step)
        weight_key, shuffle_key = jax.random.split(sub_key)
        shares = jax.random.randint(weight_key, (NSEQ - 1,), 1000, 1501).astype(jnp.int32)
        extra_len = shares * spare_len // jnp.sum(shares)
        leftover = spare_len - jnp.sum(extra_len)
        extra_len = extra_len + (jnp.arange(NSEQ - 1) < leftover).astype(jnp.int32)
        lengths = jnp.concatenate([jnp.full((1,), 2 * LMIN, jnp.int32), LMIN + extra_len.astype(jnp.int32)])
        shuffle = jax.random.permutation(shuffle_key, NSEQ)
        rows_out.append(lengths[shuffle])
    return jnp.stack(rows_out).astype(jnp.int32)


def block_levels(stream_key, dims, cuts, least, top_value):
    loudness, own = 1.0, jax.random.fold_in(stream_key, 6)
    for dim, parts in cuts:
        heights = jnp.exp(jax.random.uniform(jax.random.fold_in(own, dim), (parts,), jnp.float32, least / len(cuts), top_value / len(cuts)))
        loudness = loudness * jnp.repeat(heights, dims[dim] // parts).reshape([-1 if axis == dim else 1 for axis in range(len(dims))])
    return loudness


def centred(rng, shape, scale, most, shards=(), kind=jnp.bfloat16):
    entries = jax.random.normal(rng, shape, jnp.float32) * scale
    if len(shards) > 0:
        entries = block_levels(rng, shape, shards, -0.22, 0.18) * entries
    return jnp.clip(entries, min=-most, max=most).astype(kind)


def setup_inputs(seed: int = 0) -> dict:
    streams_of = jax.random.split(jax.random.key(seed), 21)
    return {
        "tokens": centred(streams_of[0], (MICRO, TOKENS, D), 1.0, 6.0, ((1, 16),)),
        "cotangent": centred(streams_of[1], (MICRO, TOKENS, D), 1.0, 6.0, ((1, 16),)),
        "seq_lengths": draw_seq_lengths(jax.random.fold_in(streams_of[20], 71), 0),
        "slot_token": jax.vmap(lambda own: jax.random.permutation(own, TOKENS))(jax.random.split(streams_of[3], MICRO)).reshape((MICRO, TOKENS)).astype(jnp.int32),
        "w_qkv": centred(streams_of[4], (D, 3, H * HD), D ** -0.5, 0.21875, ((0, 16), (2, 2)), jnp.float32),
        "w_proj": centred(streams_of[5], (H * HD, D), (max(1, H * HD * 2 // LMIN)) ** -0.5, 6.0, ((0, 2), (1, 16)), jnp.float32),
        "w_inner": centred(streams_of[6], (D, FF), D ** -0.5, 0.21875, ((0, 16), (1, 2)), jnp.float32),
        "w_outer": centred(streams_of[7], (FF, D), FF ** -0.5, 0.109375, ((0, 2), (1, 16)), jnp.float32),
        "norm_gains": jnp.clip(1.0 + 0.1 * jax.random.normal(streams_of[8], (2, D), jnp.float32), 0.5, 1.5),
        "norm_biases": centred(streams_of[9], (2, D), 0.3, 1.75, ((1, 16),), jnp.float32),
        "qkv_first": centred(streams_of[10], (D, 3, H * HD), (0.11 * (TOKENS // MICRO) ** 0.5), 28.0, ((0, 16), (2, 2)), jnp.float32),
        "qkv_second": jnp.clip(jnp.exp(math.log(645.12) - 2.7821581 * jax.random.uniform(streams_of[11], (D, 3, H * HD), jnp.float32) ** block_levels(streams_of[11], (D, 3, H * HD), ((0, 16), (2, 2)), -0.2, 0.2)), 39.936, 645.12),
        "proj_first": centred(streams_of[12], (H * HD, D), (0.19 * (TOKENS // MICRO // LMIN) ** 0.5), 1.0, ((0, 2), (1, 16)), jnp.float32),
        "proj_second": jnp.clip(jnp.exp(math.log(1.2) - 2.7725887 * jax.random.uniform(streams_of[13], (H * HD, D), jnp.float32) ** block_levels(streams_of[13], (H * HD, D), ((0, 2), (1, 16)), -0.2, 0.2)), 0.075, 1.2),
        "inner_first": centred(streams_of[14], (D, FF), (0.033 * (TOKENS // MICRO) ** 0.5), 8.0, ((0, 16), (1, 2)), jnp.float32),
        "inner_second": jnp.clip(jnp.exp(math.log(58.368) - 2.804677 * jax.random.uniform(streams_of[15], (D, FF), jnp.float32) ** block_levels(streams_of[15], (D, FF), ((0, 16), (1, 2)), -0.2, 0.2)), 3.5328, 58.368),
        "outer_first": centred(streams_of[16], (FF, D), (0.066 * (TOKENS // MICRO) ** 0.5), 16.0, ((0, 2), (1, 16)), jnp.float32),
        "outer_second": jnp.clip(jnp.exp(math.log(230.4) - 2.7699256 * jax.random.uniform(streams_of[17], (FF, D), jnp.float32) ** block_levels(streams_of[17], (FF, D), ((0, 2), (1, 16)), -0.2, 0.2)), 14.4384, 230.4),
        "norm_first": centred(streams_of[18], (4, D), (0.11 * (TOKENS // MICRO) ** 0.5), 28.0, ((1, 16),), jnp.float32),
        "norm_second": jnp.clip(jnp.exp(math.log(645.12) - 2.7821581 * jax.random.uniform(streams_of[19], (4, D), jnp.float32) ** block_levels(streams_of[19], (4, D), ((1, 16),), -0.2, 0.2)), 39.936, 645.12),
    }


NORM_EPS = 1e-05
BETA_ONE = 0.9
BETA_TWO = 0.95
ADAM_EPS = 1e-08
DECAY_RATE = 0.1
RATE_MATRIX = 0.02
RATE_PROJ = 0.6
RATE_NORM = 0.1
HIGHEST = lax.Precision.HIGHEST

@jax.custom_vjp
def low(v):
    return lax.optimization_barrier(v.astype(jnp.bfloat16)).astype(jnp.float32)

@jax.custom_vjp
def low_back(v):
    return v

def low_keep(v):
    return (low(v), None)

def low_pass(kept, grad):
    return (grad,)

def back_keep(v):
    return (v, None)

def back_low(kept, grad):
    return (low(grad),)
low.defvjp(low_keep, low_pass)
low_back.defvjp(back_keep, back_low)

def layer_norm(values, gain_row, shift_row):
    center = values - lax.optimization_barrier(jnp.mean(values, axis=-1, keepdims=True))
    spread = lax.optimization_barrier(jnp.mean(center * center, axis=-1, keepdims=True))
    return center * lax.rsqrt(spread + NORM_EPS) * gain_row + shift_row

def doc_and_place(tok_ids, lengths):
    seq_ends = jnp.cumsum(lengths).astype(jnp.int32)
    passed = tok_ids[:, None] >= seq_ends[None, :]
    doc_ids = lax.optimization_barrier(jnp.sum(passed.astype(jnp.int32), axis=1))
    places = tok_ids - lax.optimization_barrier(jnp.sum(jnp.where(passed, lengths[None, :], 0), axis=1))
    return (doc_ids.astype(jnp.int32), places.astype(jnp.int32))

def by_key_block(array):
    grid = array.reshape((N_PB, N_KA, TOK_DEV) + array.shape[1:])
    return jnp.swapaxes(grid, 0, 1).reshape((N_KA, N_PB * TOK_DEV) + array.shape[1:])

def attention(queries, key_heads, value_heads, doc_ids, places):
    key_blocks = by_key_block(key_heads)
    value_blocks = by_key_block(value_heads)
    key_doc = by_key_block(doc_ids)
    key_pos = by_key_block(places)
    score_scale = float(HD) ** (-0.5)

    def one_block(inputs):
        query_blk, query_doc, query_pos = inputs
        scores = low_back(jnp.einsum('qhe,jkhe->hqjk', query_blk, key_blocks, precision=HIGHEST) * score_scale)
        allowed = (query_doc[:, None, None] == key_doc[None]) & (key_pos[None] <= query_pos[:, None, None])
        radius = jnp.sqrt(scores * scores + 1.0)
        local_max = lax.optimization_barrier(jnp.max(jnp.where(allowed, radius, 0.0), axis=-1))
        weights = jnp.where(allowed, jnp.exp(radius - local_max[..., None]), 0.0)
        local_sum = lax.optimization_barrier(jnp.sum(weights, axis=-1))
        signed = low(scores / radius * weights)
        pieces = low_back(jnp.einsum('hqjk,jkhe->hqje', signed, value_blocks, precision=HIGHEST))
        row_top = lax.optimization_barrier(jnp.max(local_max, axis=-1))
        row_total = lax.optimization_barrier(jnp.sum(local_sum * jnp.exp(local_max - row_top[..., None]), axis=-1))
        factor = jnp.exp(local_max - row_top[..., None]) / row_total[..., None]
        merged = lax.optimization_barrier(jnp.sum(factor[..., None] * pieces, axis=2))
        return jnp.transpose(merged, (1, 0, 2)).reshape(query_blk.shape[0], H * HD)
    block_rows = min(256, TOKENS)
    block_count = TOKENS // block_rows
    merged_all = lax.map(jax.checkpoint(one_block), (queries.reshape(block_count, block_rows, H, HD), doc_ids.reshape(block_count, block_rows), places.reshape(block_count, block_rows)))
    return merged_all.reshape(TOKENS, H * HD)

def forward(inputs, w_qkv, w_proj, w_inner, w_outer, norm_gains, norm_biases, doc_ids, places):
    gains = low(norm_gains)
    shifts = low(norm_biases)
    normed = layer_norm(inputs, gains[0], shifts[0])
    mixed_qkv = jnp.einsum('td,dkn->tkn', low(normed), low(w_qkv), precision=HIGHEST)
    mixed_qkv = low(low_back(mixed_qkv))
    count_rows = inputs.shape[0]
    attended = attention(mixed_qkv[:, 0].reshape(count_rows, H, HD), mixed_qkv[:, 1].reshape(count_rows, H, HD), mixed_qkv[:, 2].reshape(count_rows, H, HD), doc_ids, places)
    branch = low_back(jnp.dot(low(attended), low(w_proj), precision=HIGHEST, preferred_element_type=jnp.float32))
    middle = inputs + branch
    normed_two = layer_norm(middle, gains[1], shifts[1])
    hidden = low_back(jnp.dot(low(normed_two), low(w_inner), precision=HIGHEST, preferred_element_type=jnp.float32))
    active = low(jax.nn.gelu(hidden, approximate=True))
    outer_term = low_back(jnp.dot(active, low(w_outer), precision=HIGHEST, preferred_element_type=jnp.float32))
    return middle + outer_term

def adam_step(master, first_state, second_state, grad_term, step_rate, weight_decay):
    first_new = BETA_ONE * first_state + (1.0 - BETA_ONE) * grad_term
    second_new = BETA_TWO * second_state + (1.0 - BETA_TWO) * grad_term * grad_term
    first_hat = first_new / (1.0 - BETA_ONE ** STEP)
    second_hat = second_new / (1.0 - BETA_TWO ** STEP)
    master_new = master - step_rate * (first_hat / (jnp.sqrt(second_hat) + ADAM_EPS) + weight_decay * master)
    return (first_new, second_new, master_new)

def reference(tokens, cotangent, seq_lengths, slot_token, w_qkv, w_proj, w_inner, w_outer, norm_gains, norm_biases, qkv_first, qkv_second, proj_first, proj_second, inner_first, inner_second, outer_first, outer_second, norm_first, norm_second):
    masters = (w_qkv, w_proj, w_inner, w_outer, norm_gains, norm_biases)
    grad_sums = jax.tree.map(jnp.zeros_like, masters)
    layer_outs = []
    input_grads = []
    for micro_step in range(MICRO):
        doc_ids, places = doc_and_place(slot_token[micro_step], seq_lengths[micro_step])

        def layer_pass(inputs, *params):
            return forward(inputs, *params, doc_ids, places)
        result, pull_back = jax.vjp(layer_pass, tokens[micro_step].astype(jnp.float32), *masters)
        gradients = pull_back(cotangent[micro_step].astype(jnp.float32))
        layer_outs.append(result.astype(jnp.bfloat16))
        input_grads.append(gradients[0])
        grad_sums = jax.tree.map(jnp.add, grad_sums, tuple(gradients[1:]))
    grads_mean = jax.tree.map(lambda summed: summed / MICRO, grad_sums)
    qkv_out = adam_step(w_qkv, qkv_first, qkv_second, grads_mean[0], RATE_MATRIX, DECAY_RATE)
    proj_out = adam_step(w_proj, proj_first, proj_second, grads_mean[1], RATE_PROJ, DECAY_RATE)
    inner_out = adam_step(w_inner, inner_first, inner_second, grads_mean[2], RATE_MATRIX, DECAY_RATE)
    outer_out = adam_step(w_outer, outer_first, outer_second, grads_mean[3], RATE_MATRIX, DECAY_RATE)
    norm_master = jnp.concatenate([norm_gains, norm_biases], axis=0)
    norm_grad = jnp.concatenate([grads_mean[4], grads_mean[5]], axis=0)
    norm_out = adam_step(norm_master, norm_first, norm_second, norm_grad, RATE_NORM, 0.0)
    norm_two_grad = jnp.stack([norm_grad[1], norm_grad[3]])
    return (jnp.stack(layer_outs), jnp.stack(input_grads), qkv_out[0], qkv_out[1], qkv_out[2], proj_out[0], proj_out[1], proj_out[2], inner_out[0], inner_out[1], inner_out[2], outer_out[0], outer_out[1], outer_out[2], norm_out[0], norm_out[1], norm_out[2], norm_two_grad)
```

```python
import functools

import jax
import jax.numpy as jnp
from jax import lax
from jax.experimental import pallas as pl
from jax.experimental.pallas import tpu as pltpu
from jax.sharding import PartitionSpec as P

HD = 64
MICRO = 2
STEP = 8
NORM_EPS = 1e-05
BETA_ONE = 0.9
BETA_TWO = 0.95
ADAM_EPS = 1e-08
DECAY_RATE = 0.1
RATE_MATRIX = 0.02
RATE_PROJ = 0.6
RATE_NORM = 0.1
BF = jnp.bfloat16
F32 = jnp.float32
PLANE = ("pb", "ka")
VMEM_LIMIT = 60 * 1024 * 1024
SCORE_BLOCK = 512
SORT_BLOCK = 256
NT = (((1,), (1,)), ((), ()))
NN = (((1,), (0,)), ((), ()))
TN = (((0,), (0,)), ((), ()))


def dot(a, b, dims=NN):
    return lax.dot_general(a, b, dims, preferred_element_type=F32)


def params(steps=1):
    return pltpu.CompilerParams(
        dimension_semantics=("arbitrary",) * steps, vmem_limit_bytes=VMEM_LIMIT
    )


def whole(shape):
    return pl.BlockSpec(shape, lambda *_: (0,) * len(shape))


def shape_of(shape, dtype):
    return jax.ShapeDtypeStruct(shape, dtype)


def head_places(group, heads):
    return tuple(h * group // heads for h in range(heads))


def one_hot(mask):
    return jnp.where(mask, 1.0, 0.0).astype(BF)


def normalize(x):
    center = x - jnp.mean(x, axis=-1, keepdims=True)
    spread = jnp.mean(center * center, axis=-1, keepdims=True)
    scale = lax.rsqrt(spread + NORM_EPS)
    return center * scale, scale


def normalize_back(grad, unit, scale):
    return scale * (
        grad
        - jnp.mean(grad, axis=-1, keepdims=True)
        - unit * jnp.mean(grad * unit, axis=-1, keepdims=True)
    )


def qkv_kernel(x_ref, w_ref, norm_ref, h_ref, qkv_ref):
    unit, _ = normalize(x_ref[...].astype(F32))
    h = (unit * norm_ref[0:1, :] + norm_ref[2:3, :]).astype(BF)
    h_ref[...] = h
    qkv_ref[...] = dot(h, w_ref[...]).astype(BF)


def qkv_of_head(x_full, head_w, norms):
    rows, width = x_full.shape
    block = min(512, rows)
    return pl.pallas_call(
        qkv_kernel,
        grid=(rows // block,),
        in_specs=[
            pl.BlockSpec((block, width), lambda i: (i, 0)),
            whole(head_w.shape),
            whole(norms.shape),
        ],
        out_specs=[
            pl.BlockSpec((block, width), lambda i: (i, 0)),
            pl.BlockSpec((block, head_w.shape[1]), lambda i: (i, 0)),
        ],
        out_shape=[shape_of((rows, width), BF), shape_of((rows, head_w.shape[1]), BF)],
        compiler_params=params(),
        name="qkv_head",
    )(x_full, head_w, norms)


def picked_rows(row_ids, first, count, source_ref, chunk):
    total = None
    wanted = first + lax.broadcasted_iota(jnp.int32, (count, 1), 0)
    for part in range(source_ref.shape[0] // chunk):
        cut = slice(part * chunk, (part + 1) * chunk)
        piece = dot(one_hot(row_ids[:, cut] == wanted), source_ref[cut, :])
        total = piece if total is None else total + piece
    return total


def sort_kernel(chunk, tok_ref, qkv_ref, q_ref, k_ref, v_ref, vt_ref):
    count = q_ref.shape[0]
    rows = picked_rows(tok_ref, pl.program_id(0) * count, count, qkv_ref, chunk)
    q_ref[...] = (rows[:, :HD] * float(HD) ** -0.5).astype(BF)
    k_ref[...] = rows[:, HD : 2 * HD].astype(BF)
    value = rows[:, 2 * HD : 3 * HD]
    v_ref[...] = value.astype(BF)
    vt_ref[...] = value.T.astype(BF)


def sort_qkv(tok_row, qkv):
    rows = qkv.shape[0]
    block = min(SORT_BLOCK, rows)
    narrow = pl.BlockSpec((block, HD), lambda i: (i, 0))
    return pl.pallas_call(
        functools.partial(sort_kernel, min(3072, rows)),
        grid=(rows // block,),
        in_specs=[whole(tok_row.shape), whole(qkv.shape)],
        out_specs=[narrow, narrow, narrow, pl.BlockSpec((HD, block), lambda i: (0, i))],
        out_shape=[shape_of((rows, HD), BF)] * 3 + [shape_of((HD, rows), BF)],
        compiler_params=params(),
        name="sort_qkv",
    )(tok_row, qkv)


def causal(block):
    return lax.broadcasted_iota(jnp.int32, (block, block), 0) <= lax.broadcasted_iota(
        jnp.int32, (block, block), 1
    )


def forward_kernel(first_ref, q_ref, k_ref, vt_ref, o_ref, low_ref, lse_ref):
    block = q_ref.shape[0]
    index = pl.program_id(0)
    query = q_ref[...]

    def step(key_block, state, diagonal):
        top, total, acc = state
        at = pl.multiple_of(key_block * block, block)
        scores = dot(k_ref[pl.ds(at, block), :], query, NT)
        square = scores * scores + 1.0
        inverse = lax.rsqrt(square)
        radius = square * inverse
        if diagonal:
            radius = jnp.where(causal(block), radius, -1e30)
        new_top = jnp.maximum(top, jnp.max(radius, axis=0, keepdims=True))
        weights = jnp.exp(radius - new_top)
        shrink = jnp.exp(top - new_top)
        signed = (scores * inverse * weights).astype(BF)
        acc = acc * shrink + dot(vt_ref[:, pl.ds(at, block)], signed)
        total = total * shrink + jnp.sum(weights, axis=0, keepdims=True)
        return (new_top, total, acc)

    state = (
        jnp.zeros((1, block), F32),
        jnp.zeros((1, block), F32),
        jnp.zeros((HD, block), F32),
    )
    state = lax.fori_loop(first_ref[index], index, lambda j, s: step(j, s, False), state)
    top, total, acc = step(index, state, True)
    out = acc * (1.0 / total)
    o_ref[...] = out
    low_ref[...] = out.astype(BF)
    lse_ref[...] = top + jnp.log(total)


def attend(first_block, q, k, vt, block):
    rows = q.shape[0]
    return pl.pallas_call(
        forward_kernel,
        grid_spec=pltpu.PrefetchScalarGridSpec(
            num_scalar_prefetch=1,
            grid=(rows // block,),
            in_specs=[
                pl.BlockSpec((block, HD), lambda i, *_: (i, 0)),
                whole(k.shape),
                whole(vt.shape),
            ],
            out_specs=[
                pl.BlockSpec((HD, block), lambda i, *_: (0, i)),
                pl.BlockSpec((HD, block), lambda i, *_: (0, i)),
                pl.BlockSpec((1, block), lambda i, *_: (0, i)),
            ],
        ),
        out_shape=[shape_of((HD, rows), F32), shape_of((HD, rows), BF), shape_of((1, rows), F32)],
        compiler_params=params(),
        name="attend_fwd",
    )(first_block, q, k, vt)


def slots_out_kernel(chunk, tok_ref, low_ref, out_ref):
    rows = tok_ref.shape[0]
    total = None
    for part in range(low_ref.shape[1] // chunk):
        cut = slice(part * chunk, (part + 1) * chunk)
        token = part * chunk + lax.broadcasted_iota(jnp.int32, (1, chunk), 1)
        piece = dot(one_hot(tok_ref[...] == token), low_ref[:, cut], NT)
        total = piece if total is None else total + piece
    total = total.astype(BF)
    out_ref[0] = jnp.concatenate([total[: rows // 2], total[rows // 2 :]], axis=1)


def slots_out(tok_col, low, group):
    rows = tok_col.shape[0] // group
    return pl.pallas_call(
        functools.partial(slots_out_kernel, min(3072, low.shape[1])),
        grid=(group,),
        in_specs=[pl.BlockSpec((rows, 1), lambda i: (i, 0)), whole(low.shape)],
        out_specs=pl.BlockSpec((1, rows // 2, 2 * HD), lambda i: (i, 0, 0)),
        out_shape=shape_of((group, rows // 2, 2 * HD), BF),
        compiler_params=params(),
        name="slots_out",
    )(tok_col, low)


def sort_grad_kernel(chunk, tok_ref, packed_ref, o_ref, g_ref, delta_ref, flat_ref):
    group, half, _ = packed_ref.shape

    @pl.when(pl.program_id(0) == 0)
    def _():
        for d in range(group):
            piece = packed_ref[d]
            flat_ref[2 * d * half : (2 * d + 1) * half, :] = piece[:, :HD]
            flat_ref[(2 * d + 1) * half : (2 * d + 2) * half, :] = piece[:, HD:]

    count = g_ref.shape[0]
    rows = picked_rows(tok_ref, pl.program_id(0) * count, count, flat_ref, chunk)
    g_ref[...] = rows.astype(BF)
    delta_ref[...] = jnp.sum(rows.T * o_ref[...], axis=0, keepdims=True)


def sort_grad(tok_row, packed, o):
    rows = o.shape[1]
    block = min(SORT_BLOCK, rows)
    return pl.pallas_call(
        functools.partial(sort_grad_kernel, min(3072, rows)),
        grid=(rows // block,),
        in_specs=[
            whole(tok_row.shape),
            whole(packed.shape),
            pl.BlockSpec((HD, block), lambda i: (0, i)),
        ],
        out_specs=[
            pl.BlockSpec((block, HD), lambda i: (i, 0)),
            pl.BlockSpec((1, block), lambda i: (0, i)),
        ],
        out_shape=[shape_of((rows, HD), BF), shape_of((1, rows), F32)],
        scratch_shapes=[pltpu.VMEM((rows, HD), BF)],
        compiler_params=params(),
        name="sort_grad",
    )(tok_row, packed, o)


def backward_kernel(
    last_ref, q_ref, k_ref, v_ref, g_ref, lse_ref, delta_ref, out_ref, dq_ref, dk_ref, dv_ref
):
    block = k_ref.shape[0]
    index = pl.program_id(0)

    @pl.when(index == 0)
    def _():
        dq_ref[...] = jnp.zeros_like(dq_ref)

    key = k_ref[...]
    key_t = key.T
    value = v_ref[...]
    dk_ref[...] = jnp.zeros_like(dk_ref)
    dv_ref[...] = jnp.zeros_like(dv_ref)

    def step(query_block, diagonal):
        at = pl.multiple_of(query_block * block, block)
        query = q_ref[pl.ds(at, block), :]
        grad = g_ref[pl.ds(at, block), :]
        scores = dot(key, query, NT)
        square = scores * scores + 1.0
        inverse = lax.rsqrt(square)
        shifted = square * inverse - lse_ref[:, pl.ds(at, block)]
        if diagonal:
            shifted = jnp.where(causal(block), shifted, -1e30)
        weights = jnp.exp(shifted)
        slope = scores * inverse
        along = dot(value, grad, NT)
        bend = 1.0 + inverse * inverse * (inverse - 1.0)
        score_grad = weights * (bend * along - slope * delta_ref[:, pl.ds(at, block)])
        signed = (slope * weights).astype(BF)
        low_grad = score_grad.astype(BF)
        dv_ref[...] += dot(signed, grad)
        dk_ref[...] += dot(low_grad, query)
        dq_ref[:, pl.ds(at, block)] += dot(key_t, low_grad)

    step(index, True)

    def body(query_block, carry):
        step(query_block, False)
        return carry

    lax.fori_loop(index + 1, last_ref[index], body, 0)
    at = pl.multiple_of(index * block, block)
    dq = dq_ref[:, pl.ds(at, block)].T * float(HD) ** -0.5
    out_ref[...] = jnp.concatenate([dq, dk_ref[...], dv_ref[...]], axis=1).astype(BF)


def attend_back(last_block, q, k, v, g, lse, delta, block):
    rows = q.shape[0]
    return pl.pallas_call(
        backward_kernel,
        grid_spec=pltpu.PrefetchScalarGridSpec(
            num_scalar_prefetch=1,
            grid=(rows // block,),
            in_specs=[
                whole(q.shape),
                pl.BlockSpec((block, HD), lambda i, *_: (i, 0)),
                pl.BlockSpec((block, HD), lambda i, *_: (i, 0)),
                whole(g.shape),
                whole(lse.shape),
                whole(delta.shape),
            ],
            out_specs=pl.BlockSpec((block, 3 * HD), lambda i, *_: (i, 0)),
            scratch_shapes=[
                pltpu.VMEM((HD, rows), F32),
                pltpu.VMEM((block, HD), F32),
                pltpu.VMEM((block, HD), F32),
            ],
        ),
        out_shape=shape_of((rows, 3 * HD), BF),
        compiler_params=params(),
        name="attend_bwd",
    )(last_block, q, k, v, g, lse, delta)


def grads_out_kernel(chunk, tok_ref, grad_ref, out_ref):
    rows = tok_ref.shape[0]
    half = rows // 2
    total = None
    for part in range(grad_ref.shape[0] // chunk):
        cut = slice(part * chunk, (part + 1) * chunk)
        token = part * chunk + lax.broadcasted_iota(jnp.int32, (1, chunk), 1)
        piece = dot(one_hot(tok_ref[...] == token), grad_ref[cut, :])
        total = piece if total is None else total + piece
    total = total.astype(BF)
    out_ref[0, :rows, :] = total[:, : 2 * HD]
    out_ref[0, rows:, :] = jnp.concatenate(
        [total[:half, 2 * HD :], total[half:, 2 * HD :]], axis=1
    )


def grads_out(tok_col, grads, group):
    rows = tok_col.shape[0] // group
    out_rows = rows + rows // 2
    return pl.pallas_call(
        functools.partial(grads_out_kernel, min(3072, grads.shape[0])),
        grid=(group,),
        in_specs=[pl.BlockSpec((rows, 1), lambda i: (i, 0)), whole(grads.shape)],
        out_specs=pl.BlockSpec((1, out_rows, 2 * HD), lambda i: (i, 0, 0)),
        out_shape=shape_of((group, out_rows, 2 * HD), BF),
        compiler_params=params(),
        name="grads_out",
    )(tok_col, grads)


def head_weight_kernel(h_ref, packed_ref, out_ref, flat_ref, acc_ref):
    count, out_rows, _ = packed_ref.shape
    rows = out_rows // 3 * 2
    half = rows // 2
    for d in range(count):
        piece = packed_ref[d]
        low = slice(d * rows, d * rows + half)
        high = slice(d * rows + half, (d + 1) * rows)
        flat_ref[d * rows : (d + 1) * rows, : 2 * HD] = piece[:rows]
        flat_ref[low, 2 * HD :] = piece[rows:, :HD]
        flat_ref[high, 2 * HD :] = piece[rows:, HD:]
    term = dot(flat_ref[...], h_ref[...], TN)

    @pl.when(pl.program_id(0) == 0)
    def _():
        acc_ref[...] = term

    @pl.when(pl.program_id(0) > 0)
    def _():
        acc_ref[...] += term

    @pl.when(pl.program_id(0) == pl.num_programs(0) - 1)
    def _():
        out_ref[...] = acc_ref[...].T.astype(BF)


def head_weight_grad(h_full, packed):
    group, out_rows, _ = packed.shape
    rows, width = h_full.shape
    count = 4 if group % 4 == 0 else 1
    return pl.pallas_call(
        head_weight_kernel,
        grid=(group // count,),
        in_specs=[
            pl.BlockSpec((rows // group * count, width), lambda i: (i, 0)),
            pl.BlockSpec((count, out_rows, 2 * HD), lambda i: (i, 0, 0)),
        ],
        out_specs=whole((width, 3 * HD)),
        out_shape=shape_of((width, 3 * HD), BF),
        scratch_shapes=[
            pltpu.VMEM((rows // group * count, 3 * HD), BF),
            pltpu.VMEM((3 * HD, width), F32),
        ],
        compiler_params=params(),
        name="head_weight",
    )(h_full, packed)


def middle_kernel(places, x_ref, packed_ref, proj_ref, norm_ref, mid_ref, h_ref, o_ref):
    half = packed_ref.shape[1]
    for h, place in enumerate(places):
        piece = packed_ref[place]
        o_ref[:half, h * HD : (h + 1) * HD] = piece[:, :HD]
        o_ref[half:, h * HD : (h + 1) * HD] = piece[:, HD:]
    mid = x_ref[...].astype(F32) + dot(o_ref[...], proj_ref[...], NT)
    mid_ref[...] = mid
    unit, _ = normalize(mid)
    h_ref[...] = (unit * norm_ref[1:2, :] + norm_ref[3:4, :]).astype(BF)


def middle(places, x, packed, weights, proj_at, norms):
    rows, width = x.shape
    return pl.pallas_call(
        functools.partial(middle_kernel, places),
        grid=(1,),
        in_specs=[
            whole(x.shape),
            whole(packed.shape),
            pl.BlockSpec((width, width), lambda i: (0, proj_at)),
            whole(norms.shape),
        ],
        out_specs=[whole((rows, width))] * 3,
        out_shape=[
            shape_of((rows, width), F32),
            shape_of((rows, width), BF),
            shape_of((rows, width), BF),
        ],
        compiler_params=params(),
        name="middle",
    )(x, packed, weights, norms)


def hidden_kernel(h_ref, dy_ref, inner_ref, outer_ref, act_ref, dpre_ref, dh_ref, out_ref):
    pre = dot(h_ref[...], inner_ref[...])
    root = 0.7978845608028654
    squared = pre * pre
    bend = jnp.tanh(root * (pre + 0.044715 * (squared * pre)))
    act = (0.5 * pre * (1.0 + bend)).astype(BF)
    act_ref[...] = act
    slope = 0.5 * (1.0 + bend) + 0.5 * pre * (1.0 - bend * bend) * (
        root * (1.0 + 3.0 * 0.044715 * squared)
    )
    dpre = (dot(dy_ref[...], outer_ref[...]) * slope).astype(BF)
    dpre_ref[...] = dpre
    dh = dot(dpre, inner_ref[...], NT)
    out = dot(act, outer_ref[...], NT)

    @pl.when(pl.program_id(0) == 0)
    def _():
        dh_ref[...] = dh
        out_ref[...] = out

    @pl.when(pl.program_id(0) > 0)
    def _():
        dh_ref[...] += dh
        out_ref[...] += out


def hidden(h, dy, weights, hidden_width):
    rows, width = h.shape
    chunk = 512
    steps = hidden_width // chunk
    return pl.pallas_call(
        hidden_kernel,
        grid=(steps,),
        in_specs=[
            whole(h.shape),
            whole(dy.shape),
            pl.BlockSpec((width, chunk), lambda i: (0, i)),
            pl.BlockSpec((width, chunk), lambda i: (0, i + steps)),
        ],
        out_specs=[
            pl.BlockSpec((rows, chunk), lambda i: (0, i)),
            pl.BlockSpec((rows, chunk), lambda i: (0, i)),
            whole((rows, width)),
            whole((rows, width)),
        ],
        out_shape=[
            shape_of((rows, hidden_width), BF),
            shape_of((rows, hidden_width), BF),
            shape_of((rows, width), F32),
            shape_of((rows, width), F32),
        ],
        compiler_params=params(),
        name="hidden",
    )(h, dy, weights, weights)


def middle_back_kernel(
    places, own_ref, other_ref, dy_ref, mid_ref, norm_ref, proj_ref, dmid_ref, low_ref, packed_ref, sums_ref
):
    half = packed_ref.shape[1]
    dh = own_ref[...] + other_ref[...].astype(F32)
    unit, scale = normalize(mid_ref[...])
    sums_ref[0:1, :] = jnp.sum(dh * unit, axis=0, keepdims=True)
    sums_ref[1:2, :] = jnp.sum(dh, axis=0, keepdims=True)
    dmid = dy_ref[...].astype(F32) + normalize_back(dh * norm_ref[1:2, :], unit, scale)
    dmid_ref[...] = dmid
    low = dmid.astype(BF)
    low_ref[...] = low
    grad = dot(low, proj_ref[...]).astype(BF)
    packed_ref[...] = jnp.zeros_like(packed_ref)
    for h, place in enumerate(places):
        cut = slice(h * HD, (h + 1) * HD)
        packed_ref[place] = jnp.concatenate([grad[:half, cut], grad[half:, cut]], axis=1)


def middle_back(places, group, own, other, dy, mid, norms, weights, proj_at):
    rows, width = mid.shape
    return pl.pallas_call(
        functools.partial(middle_back_kernel, places),
        grid=(1,),
        in_specs=[
            whole(own.shape),
            whole(other.shape),
            whole(dy.shape),
            whole(mid.shape),
            whole(norms.shape),
            pl.BlockSpec((width, width), lambda i: (0, proj_at)),
        ],
        out_specs=[
            whole((rows, width)),
            whole((rows, width)),
            whole((group, rows // 2, 2 * HD)),
            whole((2, width)),
        ],
        out_shape=[
            shape_of((rows, width), F32),
            shape_of((rows, width), BF),
            shape_of((group, rows // 2, 2 * HD), BF),
            shape_of((2, width), F32),
        ],
        compiler_params=params(),
        name="middle_back",
    )(own, other, dy, mid, norms, weights)


def weight_kernel(span, h0, h1, p0, p1, dy0, dy1, a0, a1, low_ref, o_ref, out_ref):
    index = pl.program_id(0)

    @pl.when(index < span)
    def _():
        out_ref[...] = (dot(h0[...], p0[...], TN) + dot(h1[...], p1[...], TN)).astype(BF)

    @pl.when((index >= span) & (index < 2 * span))
    def _():
        out_ref[...] = (dot(dy0[...], a0[...], TN) + dot(dy1[...], a1[...], TN)).astype(BF)

    @pl.when(index == 2 * span)
    def _():
        out_ref[...] = dot(low_ref[...], o_ref[...], TN).astype(BF)


def weight_grads(h_pair, dpre_pair, dy_pair, act_pair, low, o):
    rows, width = o.shape
    span = act_pair[0].shape[1] // width
    first = pl.BlockSpec((rows, width), lambda i: (0, jnp.minimum(i, span - 1)))
    second = pl.BlockSpec((rows, width), lambda i: (0, jnp.clip(i - span, 0, span - 1)))
    plain = whole((rows, width))
    return pl.pallas_call(
        functools.partial(weight_kernel, span),
        grid=(2 * span + 1,),
        in_specs=[plain, plain, first, first, plain, plain, second, second, plain, plain],
        out_specs=pl.BlockSpec((width, width), lambda i: (0, i)),
        out_shape=shape_of((width, (2 * span + 1) * width), BF),
        compiler_params=params(),
        name="weight_grads",
    )(*h_pair, *dpre_pair, *dy_pair, *act_pair, low, o)


def input_back_kernel(places, packed_ref, w_ref, x_ref, dmid_ref, norm_ref, out_ref, sums_ref, flat_ref):
    rows, _ = x_ref.shape
    half = rows // 2
    for h, place in enumerate(places):
        at = 3 * HD * h
        piece = packed_ref[place]
        flat_ref[:, at : at + 2 * HD] = piece[:rows]
        flat_ref[:half, at + 2 * HD : at + 3 * HD] = piece[rows:, :HD]
        flat_ref[half:, at + 2 * HD : at + 3 * HD] = piece[rows:, HD:]
    dh = dot(flat_ref[...], w_ref[...], NT)
    unit, scale = normalize(x_ref[...].astype(F32))
    sums_ref[0:1, :] = jnp.sum(dh * unit, axis=0, keepdims=True)
    sums_ref[1:2, :] = jnp.sum(dh, axis=0, keepdims=True)
    out_ref[...] = (dmid_ref[...] + normalize_back(dh * norm_ref[0:1, :], unit, scale)).astype(BF)


def input_back(places, packed, weights, x, dmid, norms):
    rows, width = x.shape
    return pl.pallas_call(
        functools.partial(input_back_kernel, places),
        grid=(1,),
        in_specs=[whole(a.shape) for a in (packed, weights, x, dmid, norms)],
        out_specs=[whole((rows, width)), whole((2, width))],
        out_shape=[shape_of((rows, width), BF), shape_of((2, width), F32)],
        scratch_shapes=[pltpu.VMEM((rows, weights.shape[1]), BF)],
        compiler_params=params(),
        name="input_back",
    )(packed, weights, x, dmid, norms)


def adam_step(master, first_state, second_state, grad_term, step_rate, weight_decay):
    first_new = BETA_ONE * first_state + (1.0 - BETA_ONE) * grad_term
    second_new = BETA_TWO * second_state + (1.0 - BETA_TWO) * grad_term * grad_term
    first_hat = first_new / (1.0 - BETA_ONE**STEP)
    second_hat = second_new / (1.0 - BETA_TWO**STEP)
    master_new = master - step_rate * (
        first_hat / (jnp.sqrt(second_hat) + ADAM_EPS) + weight_decay * master
    )
    return (first_new, second_new, master_new)


def shards(
    tokens,
    cotangent,
    seq_lengths,
    slot_token,
    w_qkv,
    w_proj,
    w_inner,
    w_outer,
    norm_gains,
    norm_biases,
    qkv_first,
    qkv_second,
    proj_first,
    proj_second,
    inner_first,
    inner_second,
    outer_first,
    outer_second,
    norm_first,
    norm_second,
):
    side = lax.axis_index("ha")
    group = lax.axis_size("pb") * lax.axis_size("ka")
    rows, width = tokens.shape[1:]
    total = rows * group
    w_rows = w_qkv.shape[0]
    half_width = w_qkv.shape[2]
    heads = 2 * half_width // HD
    hidden_half = w_inner.shape[1]
    places = head_places(group, heads)
    head_at = [0] * group
    for h, place in enumerate(places):
        head_at[place] = h
    block = min(SCORE_BLOCK, total)

    def swap(a):
        return lax.ppermute(a, "ha", [(0, 1), (1, 0)])

    def ordered(own, other):
        return jnp.where(side == 0, own, other), jnp.where(side == 0, other, own)

    def own_micro(a):
        return lax.dynamic_index_in_dim(a, side, 0, False)

    def other_micro(a):
        return lax.dynamic_index_in_dim(a, 1 - side, 0, False)

    x = own_micro(tokens)
    x_full = lax.all_gather(x, PLANE, axis=0, tiled=True)
    mine = jnp.concatenate(
        [w_qkv.astype(BF).reshape(w_rows, 3 * half_width), w_proj.astype(BF).T], axis=1
    )
    low_half, high_half = ordered(mine, swap(mine))
    qkv_rows = jnp.concatenate(
        [
            a[:, : 3 * half_width].reshape(w_rows, 3, heads // 2, HD).swapaxes(1, 2)
            for a in (low_half, high_half)
        ],
        axis=1,
    ).reshape(w_rows, heads, 3 * HD)
    proj_rows = jnp.concatenate(
        [a[:, 3 * half_width :] for a in (low_half, high_half)], axis=1
    )
    norm_master = jnp.concatenate([norm_gains, norm_biases], axis=0)
    head_rows = jnp.stack([qkv_rows[:, head_at[d]] for d in range(group)], axis=0)
    head_rows = jnp.concatenate(
        [
            head_rows,
            jnp.broadcast_to(norm_master.astype(BF).T[None], (group, w_rows, 4)),
            jnp.zeros((group, w_rows, HD - 4), BF),
        ],
        axis=2,
    )
    head_w = lax.all_to_all(head_rows, PLANE, 0, 0, tiled=True).reshape(width, 4 * HD)
    norms = head_w[:, 3 * HD : 3 * HD + 4].astype(F32).T
    main_rows = jnp.concatenate([w_inner.astype(BF), w_outer.astype(BF).T, proj_rows], axis=1)
    main_rows, x_full = lax.optimization_barrier((main_rows, x_full))
    main_w = lax.all_gather(main_rows, PLANE, axis=0, tiled=True)
    proj_at = 2 * hidden_half // width
    late_rows, main_w = lax.optimization_barrier((qkv_rows.reshape(w_rows, -1), main_w))
    qkv_w = lax.all_gather(late_rows, PLANE, axis=0, tiled=True)

    tok = own_micro(slot_token)
    tok_row = tok.reshape(1, total)
    tok_col = tok.reshape(total, 1)
    ends = jnp.cumsum(own_micro(seq_lengths))
    starts = jnp.arange(total // block, dtype=jnp.int32) * block
    first_block = jnp.max(jnp.where(ends[None] <= starts[:, None], ends[None], 0), axis=1) // block
    last_block = jnp.min(jnp.where(ends[None] > starts[:, None], ends[None], total), axis=1) // block
    first_block = first_block.astype(jnp.int32)
    last_block = last_block.astype(jnp.int32)

    h_full, qkv = qkv_of_head(x_full, head_w, norms)
    q, k, v, vt = sort_qkv(tok_row, qkv)
    o, o_low, lse = attend(first_block, q, k, vt, block)
    o_packed = lax.all_to_all(slots_out(tok_col, o_low, group), PLANE, 0, 0, tiled=True)
    mid, h_own, o_own = middle(places, x, o_packed, main_w, proj_at, norms)
    h_other = swap(h_own)
    dy_own, dy_other = own_micro(cotangent), other_micro(cotangent)
    act_other, dpre_other, dh_send, out_send = hidden(h_other, dy_other, main_w, hidden_half)
    dh_got = swap(dh_send.astype(BF))
    act_own, dpre_own, dh_own, out_own = hidden(h_own, dy_own, main_w, hidden_half)
    out_got = swap(out_send.astype(BF))
    layer_own = (mid + out_own + out_got.astype(F32)).astype(BF)
    layer_out = jnp.stack(ordered(layer_own, swap(layer_own)))

    dmid, dmid_low, g_packed, sums_two = middle_back(
        places, group, dh_own, dh_got, dy_own, mid, norms, main_w, proj_at
    )
    main_grad = weight_grads(
        (h_own, h_other), (dpre_own, dpre_other), (dy_own, dy_other), (act_own, act_other), dmid_low, o_own
    )
    main_sum = lax.psum_scatter(main_grad, PLANE, scatter_dimension=0, tiled=True)
    g_packed = lax.all_to_all(g_packed, PLANE, 0, 0, tiled=True)
    g, delta = sort_grad(tok_row, g_packed, o)
    dqkv = attend_back(last_block, q, k, v, g, lse, delta, block)
    dqkv_packed = grads_out(tok_col, dqkv, group)
    dqkv_own = lax.all_to_all(dqkv_packed, PLANE, 0, 0, tiled=True)
    head_grad = head_weight_grad(h_full, dqkv_packed)
    input_low, sums_one = input_back(places, dqkv_own, qkv_w, x, dmid, norms)
    input_grad = jnp.stack(ordered(input_low, swap(input_low))).astype(F32)

    norm_sums = jnp.stack([sums_one[0], sums_two[0], sums_one[1], sums_two[1]])
    norm_top = norm_sums.astype(BF)
    norm_rest = (norm_sums - norm_top.astype(F32)).astype(BF)
    last_grad = jnp.concatenate(
        [head_grad, norm_top.T, norm_rest.T, jnp.zeros((width, HD - 8), BF)], axis=1
    ).reshape(group, w_rows, 4 * HD)
    last_grad = lax.all_to_all(last_grad, PLANE, 0, 0, tiled=True)
    qkv_part = jnp.stack([last_grad[place, :, : 3 * HD] for place in places], axis=1)
    qkv_part = qkv_part.reshape(w_rows, heads, 3, HD).swapaxes(1, 2).reshape(w_rows, 3, 2, half_width)
    norm_part = jnp.sum(last_grad[:, :, 3 * HD : 3 * HD + 8].astype(F32), axis=0)
    norm_part = norm_part[:, :4] + norm_part[:, 4:]
    part_top = norm_part.astype(BF)
    part_rest = (norm_part - part_top.astype(F32)).astype(BF)
    keep, send = ordered(qkv_part[:, :, 0], qkv_part[:, :, 1])
    got = swap(
        jnp.concatenate([send.reshape(w_rows, 3 * half_width), part_top, part_rest], axis=1)
    ).astype(F32)
    qkv_grad = keep.astype(F32) + got[:, : 3 * half_width].reshape(w_rows, 3, half_width)
    norm_got = got[:, 3 * half_width :]
    norm_own = part_top.astype(F32) + part_rest.astype(F32)
    norm_grad = (norm_own + (norm_got[:, :4] + norm_got[:, 4:])).T

    inner_grad = main_sum[:, :hidden_half].astype(F32)
    outer_grad = main_sum[:, hidden_half : 2 * hidden_half].astype(F32).T
    proj_part = main_sum[:, 2 * hidden_half :]
    keep, send = ordered(proj_part[:, :half_width], proj_part[:, half_width:])
    proj_grad = (keep.astype(F32) + swap(send).astype(F32)).T

    qkv_out = adam_step(w_qkv, qkv_first, qkv_second, qkv_grad / MICRO, RATE_MATRIX, DECAY_RATE)
    proj_out = adam_step(w_proj, proj_first, proj_second, proj_grad / MICRO, RATE_PROJ, DECAY_RATE)
    inner_out = adam_step(
        w_inner, inner_first, inner_second, inner_grad / MICRO, RATE_MATRIX, DECAY_RATE
    )
    outer_out = adam_step(
        w_outer, outer_first, outer_second, outer_grad / MICRO, RATE_MATRIX, DECAY_RATE
    )
    norm_grad = norm_grad / MICRO
    norm_out = adam_step(norm_master, norm_first, norm_second, norm_grad, RATE_NORM, 0.0)
    norm_two_grad = jnp.stack([norm_grad[1], norm_grad[3]])
    return (
        layer_out,
        input_grad,
        *qkv_out,
        *proj_out,
        *inner_out,
        *outer_out,
        *norm_out,
        norm_two_grad,
    )


def solution(mesh):
    tok = P(None, PLANE, None)
    qkv = P(PLANE, None, "ha")
    down = P("ha", PLANE)
    inner = P(PLANE, "ha")
    norm = P(None, PLANE)
    in_specs = (
        (tok, tok, P(), P(), qkv, down, inner, down, norm, norm)
        + (qkv, qkv, down, down, inner, inner, down, down, norm, norm)
    )
    out_specs = (
        (tok, tok, qkv, qkv, qkv, down, down, down)
        + (inner, inner, inner, down, down, down, norm, norm, norm, norm)
    )
    return jax.shard_map(shards, mesh=mesh, in_specs=in_specs, out_specs=out_specs, check_vma=False)
```

```python
import functools

import jax
import jax.numpy as jnp
from jax import lax
from jax.experimental import pallas as pl
from jax.experimental.pallas import tpu as pltpu
from jax.sharding import PartitionSpec as P

HD = 64
MICRO = 2
STEP = 8
NORM_EPS = 1e-05
BETA_ONE = 0.9
BETA_TWO = 0.95
ADAM_EPS = 1e-08
DECAY_RATE = 0.1
RATE_MATRIX = 0.02
RATE_PROJ = 0.6
RATE_NORM = 0.1
BF = jnp.bfloat16
F32 = jnp.float32
PLANE = ("pb", "ka")
VMEM_LIMIT = 60 * 1024 * 1024
SCORE_BLOCK = 512
SORT_BLOCK = 1024
NT = (((1,), (1,)), ((), ()))
NN = (((1,), (0,)), ((), ()))
TN = (((0,), (0,)), ((), ()))


def dot(a, b, dims=NN):
    return lax.dot_general(a, b, dims, preferred_element_type=F32)


def params(steps=1):
    return pltpu.CompilerParams(
        dimension_semantics=("arbitrary",) * steps, vmem_limit_bytes=VMEM_LIMIT
    )


def cost(us):
    return pl.CostEstimate(flops=int(us * 2e8), bytes_accessed=int(us * 1e6), transcendentals=0)


def tie(*arrays):
    return lax.optimization_barrier(arrays)


def whole(shape):
    return pl.BlockSpec(shape, lambda *_: (0,) * len(shape))


def shape_of(shape, dtype):
    return jax.ShapeDtypeStruct(shape, dtype)


def head_places(group, heads):
    return tuple(h * group // heads for h in range(heads))


def normalize(x):
    center = x - jnp.mean(x, axis=-1, keepdims=True)
    spread = jnp.mean(center * center, axis=-1, keepdims=True)
    scale = lax.rsqrt(spread + NORM_EPS)
    return center * scale, scale


def normalize_back(grad, unit, scale):
    return scale * (
        grad
        - jnp.mean(grad, axis=-1, keepdims=True)
        - unit * jnp.mean(grad * unit, axis=-1, keepdims=True)
    )


def matching(row_ids, index):
    low = jnp.where(
        lax.shift_right_logical(row_ids, 8) == index, lax.bitwise_and(row_ids, 255), 256
    )
    line = lax.broadcasted_iota(jnp.int32, (256, 1), 0)
    return jnp.where(
        low.astype(F32).astype(BF) == line.astype(F32).astype(BF),
        jnp.ones((), BF),
        jnp.zeros((), BF),
    )


def rearranged(row_ids, source_ref):
    count = source_ref.shape[1] // 256
    span = min(count, 12)

    def some(start, total):
        for part in range(span):
            index = start * span + part
            at = index * 256 if isinstance(index, int) else pl.multiple_of(index * 256, 256)
            piece = dot(source_ref[:, pl.ds(at, 256)], matching(row_ids, index))
            total = piece if total is None else total + piece
        return total

    if count == span:
        return some(0, None)
    empty = jnp.zeros((source_ref.shape[0], row_ids.shape[1]), F32)
    return lax.fori_loop(0, count // span, some, empty)


def place_kernel(tok_ref, out_ref):
    index = pl.program_id(0)
    total = tok_ref.shape[1]
    chunk = min(3072, total)
    hits = None
    line = lax.broadcasted_iota(jnp.int32, (8, chunk), 0)
    for part in range(total // chunk):
        slot = part * chunk + lax.broadcasted_iota(jnp.int32, (8, chunk), 1)
        ids = jnp.where(line == 0, lax.shift_right_logical(slot, 8), lax.bitwise_and(slot, 255))
        found = matching(tok_ref[:, part * chunk : (part + 1) * chunk], index)
        piece = dot(ids.astype(F32).astype(BF), found, NT)
        hits = piece if hits is None else hits + piece
    out_ref[...] = (hits[0:1] * 256.0 + hits[1:2]).astype(jnp.int32)


def slots_of_tokens(tok_row):
    total = tok_row.shape[1]
    return pl.pallas_call(
        place_kernel,
        grid=(total // 256,),
        in_specs=[whole(tok_row.shape)],
        out_specs=pl.BlockSpec((1, 256), lambda i: (0, i)),
        out_shape=shape_of((1, total), jnp.int32),
        compiler_params=params(),
        cost_estimate=cost(8),
        name="slots_of_tokens",
    )(tok_row)


def qkv_kernel(x_ref, w_ref, norm_ref, unit_ref, qkv_ref):
    unit, _ = normalize(x_ref[...].astype(F32))
    h = (unit * norm_ref[0:1, :] + norm_ref[2:3, :]).astype(BF)
    unit_ref[...] = unit.astype(BF)
    qkv_ref[...] = dot(w_ref[...], h, NT).astype(BF)


def qkv_piece_kernel(counts, at_ref, *refs):
    sources = refs[: 4 * len(counts)]
    w_ref, norm_ref = refs[4 * len(counts) :][:2]
    unit_ref, qkv_ref, x_ref = refs[-3:]
    rows = x_ref.shape[0] // 2
    even = at_ref[3] == 0
    slot = 0
    for group, count in enumerate(counts):
        for place in range(count):
            for side in range(2):

                @pl.when((pl.program_id(0) == slot) & (pl.program_id(1) == side))
                def _():
                    own = sources[4 * group + side][place]
                    other = sources[4 * group + 2 + side][place]
                    x_ref[:rows, :] = jnp.where(even, own, other)
                    x_ref[rows:, :] = jnp.where(even, other, own)

            slot += 1
    unit, _ = normalize(x_ref[...].astype(F32))
    h = (unit * norm_ref[0:1, :] + norm_ref[2:3, :]).astype(BF)
    unit_ref[...] = unit.astype(BF)
    qkv_ref[...] = dot(w_ref[...], h, NT).astype(BF)


def qkv_of_piece(at, groups, head_w, norms, total, buffers):
    counts = tuple(group[0].shape[0] for group in groups)
    pieces = [a for group in groups for a in group]
    _, rows, width = pieces[0].shape
    kept = [pl.BlockSpec(memory_space=pl.ANY)] * len(buffers)
    first = 1 + len(pieces) + 2

    def place(i, j, at):
        return (at[0] ^ (at[1] + i)) * 2 + (at[2] ^ j)

    return pl.pallas_call(
        functools.partial(qkv_piece_kernel, counts),
        grid_spec=pltpu.PrefetchScalarGridSpec(
            num_scalar_prefetch=1,
            grid=(sum(counts), 2),
            in_specs=[whole(a.shape) for a in (*pieces, head_w, norms)] + kept,
            out_specs=[
                pl.BlockSpec((2 * rows, width), lambda i, j, at: (place(i, j, at), 0)),
                pl.BlockSpec((head_w.shape[0], 2 * rows), lambda i, j, at: (0, place(i, j, at))),
            ],
            scratch_shapes=[pltpu.VMEM((2 * rows, width), BF)],
        ),
        out_shape=[shape_of((total, width), BF), shape_of((head_w.shape[0], total), BF)],
        input_output_aliases={first: 0, first + 1: 1} if buffers else {},
        compiler_params=params(2),
        cost_estimate=cost(3 * sum(counts)),
        name="qkv_piece",
    )(at, *pieces, head_w, norms, *buffers)


def qkv_of_head(x_full, head_w, norms):
    rows, width = x_full.shape
    block = min(512, rows)
    return pl.pallas_call(
        qkv_kernel,
        grid=(rows // block,),
        in_specs=[
            pl.BlockSpec((block, width), lambda i: (i, 0)),
            whole(head_w.shape),
            whole(norms.shape),
        ],
        out_specs=[
            pl.BlockSpec((block, width), lambda i: (i, 0)),
            pl.BlockSpec((head_w.shape[0], block), lambda i: (0, i)),
        ],
        out_shape=[shape_of((rows, width), BF), shape_of((head_w.shape[0], rows), BF)],
        compiler_params=params(),
        cost_estimate=cost(8),
        name="qkv_head",
    )(x_full, head_w, norms)


def sort_kernel(slot_ref, qkv_ref, q_ref, qt_ref, k_ref, v_ref, vt_ref):
    found = rearranged(slot_ref[...], qkv_ref)
    query = found[:HD] * float(HD) ** -0.5
    value = found[2 * HD :]
    qt_ref[...] = query.astype(BF)
    q_ref[...] = query.T.astype(BF)
    k_ref[...] = found[HD : 2 * HD].T.astype(BF)
    v_ref[...] = value.T.astype(BF)
    vt_ref[...] = value.astype(BF)


def sort_qkv(slot_row, qkv):
    rows = qkv.shape[1]
    block = min(SORT_BLOCK, rows)
    narrow = pl.BlockSpec((block, HD), lambda i: (i, 0))
    wide = pl.BlockSpec((HD, block), lambda i: (0, i))
    return pl.pallas_call(
        sort_kernel,
        grid=(rows // block,),
        in_specs=[pl.BlockSpec((1, block), lambda i: (0, i)), whole(qkv.shape)],
        out_specs=[narrow, wide, narrow, narrow, wide],
        out_shape=[shape_of((HD, rows) if spec is wide else (rows, HD), BF) for spec in (narrow, wide, narrow, narrow, wide)],
        compiler_params=params(),
        cost_estimate=cost(7),
        name="sort_qkv",
    )(slot_row, qkv)


def causal(block):
    return lax.broadcasted_iota(jnp.int32, (block, block), 0) <= lax.broadcasted_iota(
        jnp.int32, (block, block), 1
    )


def forward_kernel(first_ref, qt_ref, k_ref, vt_ref, o_ref, low_ref, lse_ref):
    block = qt_ref.shape[1]
    index = pl.program_id(0)
    query = qt_ref[...]

    def step(key_block, state, diagonal):
        top, total, acc = state
        at = pl.multiple_of(key_block * block, block)
        scores = dot(k_ref[pl.ds(at, block), :], query)
        square = scores * scores + 1.0
        inverse = lax.rsqrt(square)
        radius = square * inverse
        if diagonal:
            radius = jnp.where(causal(block), radius, -1e30)
        new_top = jnp.maximum(top, jnp.max(radius, axis=0, keepdims=True))
        weights = jnp.exp(radius - new_top)
        shrink = jnp.exp(top - new_top)
        signed = (scores * inverse * weights).astype(BF)
        acc = acc * shrink + dot(vt_ref[:, pl.ds(at, block)], signed)
        total = total * shrink + jnp.sum(weights, axis=0, keepdims=True)
        return (new_top, total, acc)

    state = (
        jnp.zeros((1, block), F32),
        jnp.zeros((1, block), F32),
        jnp.zeros((HD, block), F32),
    )
    state = lax.fori_loop(first_ref[index], index, lambda j, s: step(j, s, False), state)
    top, total, acc = step(index, state, True)
    out = acc * (1.0 / total)
    o_ref[...] = out
    low_ref[...] = out.astype(BF)
    lse_ref[...] = top + jnp.log(total)


def attend(first_block, qt, k, vt, block):
    rows = k.shape[0]
    return pl.pallas_call(
        forward_kernel,
        grid_spec=pltpu.PrefetchScalarGridSpec(
            num_scalar_prefetch=1,
            grid=(rows // block,),
            in_specs=[
                pl.BlockSpec((HD, block), lambda i, *_: (0, i)),
                whole(k.shape),
                whole(vt.shape),
            ],
            out_specs=[
                pl.BlockSpec((HD, block), lambda i, *_: (0, i)),
                pl.BlockSpec((HD, block), lambda i, *_: (0, i)),
                pl.BlockSpec((1, block), lambda i, *_: (0, i)),
            ],
        ),
        out_shape=[shape_of((HD, rows), F32), shape_of((HD, rows), BF), shape_of((1, rows), F32)],
        compiler_params=params(),
        cost_estimate=cost(13),
        name="attend_fwd",
    )(first_block, qt, k, vt)


def slots_out_kernel(rows, tok_ref, low_ref, out_ref):
    half = rows // 2
    found = rearranged(tok_ref[...], low_ref).T.astype(BF)
    for d in range(out_ref.shape[0]):
        at = d * rows
        out_ref[d] = jnp.concatenate([found[at : at + half], found[at + half : at + rows]], axis=1)


def slots_out(tok_row, low, group):
    total = tok_row.shape[1]
    rows = total // group
    count = owners_per_step(group, rows)
    return pl.pallas_call(
        functools.partial(slots_out_kernel, rows),
        grid=(group // count,),
        in_specs=[pl.BlockSpec((1, count * rows), lambda i: (0, i)), whole(low.shape)],
        out_specs=pl.BlockSpec((count, rows // 2, 2 * HD), lambda i: (i, 0, 0)),
        out_shape=shape_of((group, rows // 2, 2 * HD), BF),
        compiler_params=params(),
        cost_estimate=cost(6),
        name="slots_out",
    )(tok_row, low)


def owners_per_step(group, rows):
    for count in (4, 2, 1):
        if group % count == 0 and count * rows % 128 == 0:
            return count
    return group


def sort_grad_kernel(slot_ref, packed_ref, o_ref, g_ref, gt_ref, delta_ref, slots_ref, flat_ref):
    group, half, _ = packed_ref.shape

    @pl.when(pl.program_id(0) == 0)
    def _():
        for d in range(group):
            piece = packed_ref[d]
            flat_ref[2 * d * half : (2 * d + 1) * half, :] = piece[:, :HD]
            flat_ref[(2 * d + 1) * half : (2 * d + 2) * half, :] = piece[:, HD:]
        for part in range(flat_ref.shape[0] // 256):
            cut = slice(part * 256, (part + 1) * 256)
            slots_ref[:, cut] = flat_ref[cut, :].astype(F32).T.astype(BF)

    found = rearranged(slot_ref[...], slots_ref)
    gt_ref[...] = found.astype(BF)
    g_ref[...] = found.T.astype(BF)
    delta_ref[...] = jnp.sum(found * o_ref[...], axis=0, keepdims=True)


def sort_grad(slot_row, packed, o):
    rows = o.shape[1]
    block = min(SORT_BLOCK, rows)
    wide = pl.BlockSpec((HD, block), lambda i: (0, i))
    line = pl.BlockSpec((1, block), lambda i: (0, i))
    return pl.pallas_call(
        sort_grad_kernel,
        grid=(rows // block,),
        in_specs=[line, whole(packed.shape), wide],
        out_specs=[pl.BlockSpec((block, HD), lambda i: (i, 0)), wide, line],
        out_shape=[shape_of((rows, HD), BF), shape_of((HD, rows), BF), shape_of((1, rows), F32)],
        scratch_shapes=[pltpu.VMEM((HD, rows), BF), pltpu.VMEM((rows, HD), BF)],
        compiler_params=params(),
        cost_estimate=cost(6),
        name="sort_grad",
    )(slot_row, packed, o)


def backward_kernel(
    last_ref, q_ref, qt_ref, k_ref, v_ref, g_ref, gt_ref, lse_ref, delta_ref, out_ref, dq_ref, dk_ref, dv_ref
):
    block = k_ref.shape[0]
    index = pl.program_id(0)

    @pl.when(index == 0)
    def _():
        dq_ref[...] = jnp.zeros_like(dq_ref)

    key = k_ref[...]
    key_t = key.astype(F32).T.astype(BF)
    value = v_ref[...]
    dk_ref[...] = jnp.zeros_like(dk_ref)
    dv_ref[...] = jnp.zeros_like(dv_ref)

    def step(query_block, diagonal):
        at = pl.multiple_of(query_block * block, block)
        scores = dot(key, qt_ref[:, pl.ds(at, block)])
        square = scores * scores + 1.0
        inverse = lax.rsqrt(square)
        shifted = square * inverse - lse_ref[:, pl.ds(at, block)]
        if diagonal:
            shifted = jnp.where(causal(block), shifted, -1e30)
        weights = jnp.exp(shifted)
        slope = scores * inverse
        along = dot(value, gt_ref[:, pl.ds(at, block)])
        bend = 1.0 + inverse * inverse * (inverse - 1.0)
        score_grad = weights * (bend * along - slope * delta_ref[:, pl.ds(at, block)])
        signed = (slope * weights).astype(BF)
        low_grad = score_grad.astype(BF)
        dv_ref[...] += dot(signed, g_ref[pl.ds(at, block), :])
        dk_ref[...] += dot(low_grad, q_ref[pl.ds(at, block), :])
        dq_ref[:, pl.ds(at, block)] += dot(key_t, low_grad)

    step(index, True)

    def body(query_block, carry):
        step(query_block, False)
        return carry

    lax.fori_loop(index + 1, last_ref[index], body, 0)
    at = pl.multiple_of(index * block, block)
    out_ref[:HD] = (dq_ref[:, pl.ds(at, block)] * float(HD) ** -0.5).astype(BF)
    out_ref[HD : 2 * HD] = dk_ref[...].T.astype(BF)
    out_ref[2 * HD :] = dv_ref[...].T.astype(BF)


def attend_back(last_block, q, qt, k, v, g, gt, lse, delta, block):
    rows = q.shape[0]
    return pl.pallas_call(
        backward_kernel,
        grid_spec=pltpu.PrefetchScalarGridSpec(
            num_scalar_prefetch=1,
            grid=(rows // block,),
            in_specs=[
                whole(q.shape),
                whole(qt.shape),
                pl.BlockSpec((block, HD), lambda i, *_: (i, 0)),
                pl.BlockSpec((block, HD), lambda i, *_: (i, 0)),
                whole(g.shape),
                whole(gt.shape),
                whole(lse.shape),
                whole(delta.shape),
            ],
            out_specs=pl.BlockSpec((3 * HD, block), lambda i, *_: (0, i)),
            scratch_shapes=[
                pltpu.VMEM((HD, rows), F32),
                pltpu.VMEM((block, HD), F32),
                pltpu.VMEM((block, HD), F32),
            ],
        ),
        out_shape=shape_of((3 * HD, rows), BF),
        compiler_params=params(),
        cost_estimate=cost(19),
        name="attend_bwd",
    )(last_block, q, qt, k, v, g, gt, lse, delta)


def head_results(acc, column, w_ref, norm_ref, sums_ref):
    weights = w_ref[...].astype(F32)
    grad = acc * norm_ref[0:1, :] + column * norm_ref[2:3, :]
    sums = jnp.concatenate(
        [
            jnp.sum(weights * acc, axis=0, keepdims=True),
            sums_ref[0:1, :],
            jnp.sum(weights * column, axis=0, keepdims=True),
            sums_ref[1:2, :],
        ],
        axis=0,
    )
    top = sums.astype(BF).astype(F32)
    rest = jnp.concatenate([top, sums - top, jnp.zeros((HD - 8, sums.shape[1]), F32)], axis=0)
    return jnp.concatenate([grad, rest], axis=0).T.astype(BF)


def all_grads_kernel(
    rows, tok_ref, grad_ref, unit_ref, w_ref, norm_ref, sums_ref, out_ref, head_ref, acc_ref, line_ref
):
    half = rows // 2
    step = pl.program_id(0)
    count = out_ref.shape[0]
    found = rearranged(tok_ref[...], grad_ref)
    low = found.astype(BF)
    term = dot(low, unit_ref[...])
    line = jnp.sum(found, axis=1, keepdims=True)

    @pl.when(step == 0)
    def _():
        acc_ref[...] = term
        line_ref[...] = line

    @pl.when(step > 0)
    def _():
        acc_ref[...] += term
        line_ref[...] += line

    turned = found.T.astype(BF)
    for d in range(count):
        at = d * rows
        out_ref[d, :rows, :] = turned[at : at + rows, : 2 * HD]
        out_ref[d, rows:, :] = jnp.concatenate(
            [turned[at : at + half, 2 * HD :], turned[at + half : at + rows, 2 * HD :]], axis=1
        )

    @pl.when(step == pl.num_programs(0) - 1)
    def _():
        head_ref[...] = head_results(acc_ref[...], line_ref[...], w_ref, norm_ref, sums_ref)


def all_grads_out(tok_row, grads, unit, head_w, norms, sums_two, group):
    total = tok_row.shape[1]
    rows = total // group
    width = unit.shape[1]
    count = owners_per_step(group, rows)
    out_rows = rows + rows // 2
    return pl.pallas_call(
        functools.partial(all_grads_kernel, rows),
        grid=(group // count,),
        in_specs=[
            pl.BlockSpec((1, count * rows), lambda i: (0, i)),
            whole(grads.shape),
            pl.BlockSpec((count * rows, width), lambda i: (i, 0)),
            whole(head_w.shape),
            whole(norms.shape),
            whole(sums_two.shape),
        ],
        out_specs=[
            pl.BlockSpec((count, out_rows, 2 * HD), lambda i: (i, 0, 0)),
            whole((width, 4 * HD)),
        ],
        out_shape=[shape_of((group, out_rows, 2 * HD), BF), shape_of((width, 4 * HD), BF)],
        scratch_shapes=[pltpu.VMEM((3 * HD, width), F32), pltpu.VMEM((3 * HD, 1), F32)],
        compiler_params=params(),
        cost_estimate=cost(9),
        name="all_grads_out",
    )(tok_row, grads, unit, head_w, norms, sums_two)


def middle_kernel(places, x_ref, packed_ref, proj_ref, norm_ref, mid_ref, h_ref, o_ref):
    half = packed_ref.shape[1]
    for h, place in enumerate(places):
        piece = packed_ref[place]
        o_ref[:half, h * HD : (h + 1) * HD] = piece[:, :HD]
        o_ref[half:, h * HD : (h + 1) * HD] = piece[:, HD:]
    mid = x_ref[...].astype(F32) + dot(o_ref[...], proj_ref[...], NT)
    mid_ref[...] = mid
    unit, _ = normalize(mid)
    h_ref[...] = (unit * norm_ref[1:2, :] + norm_ref[3:4, :]).astype(BF)


def middle(places, x, packed, weights, proj_at, norms):
    rows, width = x.shape
    return pl.pallas_call(
        functools.partial(middle_kernel, places),
        grid=(1,),
        in_specs=[
            whole(x.shape),
            whole(packed.shape),
            pl.BlockSpec((width, width), lambda i: (0, proj_at)),
            whole(norms.shape),
        ],
        out_specs=[whole((rows, width))] * 3,
        out_shape=[
            shape_of((rows, width), F32),
            shape_of((rows, width), BF),
            shape_of((rows, width), BF),
        ],
        compiler_params=params(),
        cost_estimate=cost(3),
        name="middle",
    )(x, packed, weights, norms)


def hidden_kernel(
    h_ref, dy_ref, inner_ref, outer_ref, act_ref, dpre_ref, dh_ref, out_ref, dh_acc, out_acc
):
    pre = dot(h_ref[...], inner_ref[...])
    root = 0.7978845608028654
    squared = pre * pre
    bend = jnp.tanh(root * (pre + 0.044715 * (squared * pre)))
    act = (0.5 * pre * (1.0 + bend)).astype(BF)
    act_ref[...] = act
    slope = 0.5 * (1.0 + bend) + 0.5 * pre * (1.0 - bend * bend) * (
        root * (1.0 + 3.0 * 0.044715 * squared)
    )
    dpre = (dot(dy_ref[...], outer_ref[...]) * slope).astype(BF)
    dpre_ref[...] = dpre
    dh = dot(dpre, inner_ref[...], NT)
    out = dot(act, outer_ref[...], NT)

    @pl.when(pl.program_id(0) == 0)
    def _():
        dh_acc[...] = dh
        out_acc[...] = out

    @pl.when(pl.program_id(0) > 0)
    def _():
        dh_acc[...] += dh
        out_acc[...] += out

    @pl.when(pl.program_id(0) == pl.num_programs(0) - 1)
    def _():
        dh_ref[...] = dh_acc[...].astype(dh_ref.dtype)
        out_ref[...] = out_acc[...].astype(out_ref.dtype)


def hidden(h, dy, weights, hidden_width, kind):
    rows, width = h.shape
    chunk = 512
    steps = hidden_width // chunk
    return pl.pallas_call(
        hidden_kernel,
        grid=(steps,),
        in_specs=[
            whole(h.shape),
            whole(dy.shape),
            pl.BlockSpec((width, chunk), lambda i: (0, i)),
            pl.BlockSpec((width, chunk), lambda i: (0, i + steps)),
        ],
        out_specs=[
            pl.BlockSpec((rows, chunk), lambda i: (0, i)),
            pl.BlockSpec((rows, chunk), lambda i: (0, i)),
            whole((rows, width)),
            whole((rows, width)),
        ],
        out_shape=[
            shape_of((rows, hidden_width), BF),
            shape_of((rows, hidden_width), BF),
            shape_of((rows, width), kind),
            shape_of((rows, width), kind),
        ],
        scratch_shapes=[pltpu.VMEM((rows, width), F32)] * 2,
        compiler_params=params(),
        cost_estimate=cost(6),
        name="hidden",
    )(h, dy, weights, weights)


def middle_back_kernel(
    places, own_ref, other_ref, dy_ref, mid_ref, norm_ref, proj_ref, dmid_ref, low_ref, packed_ref, sums_ref
):
    half = packed_ref.shape[1]
    dh = own_ref[...] + other_ref[...].astype(F32)
    unit, scale = normalize(mid_ref[...])
    sums_ref[0:1, :] = jnp.sum(dh * unit, axis=0, keepdims=True)
    sums_ref[1:2, :] = jnp.sum(dh, axis=0, keepdims=True)
    dmid = dy_ref[...].astype(F32) + normalize_back(dh * norm_ref[1:2, :], unit, scale)
    dmid_ref[...] = dmid
    low = dmid.astype(BF)
    low_ref[...] = low
    grad = dot(low, proj_ref[...]).astype(BF)
    packed_ref[...] = jnp.zeros_like(packed_ref)
    for h, place in enumerate(places):
        cut = slice(h * HD, (h + 1) * HD)
        packed_ref[place] = jnp.concatenate([grad[:half, cut], grad[half:, cut]], axis=1)


def middle_back(places, group, own, other, dy, mid, norms, weights, proj_at):
    rows, width = mid.shape
    return pl.pallas_call(
        functools.partial(middle_back_kernel, places),
        grid=(1,),
        in_specs=[
            whole(own.shape),
            whole(other.shape),
            whole(dy.shape),
            whole(mid.shape),
            whole(norms.shape),
            pl.BlockSpec((width, width), lambda i: (0, proj_at)),
        ],
        out_specs=[
            whole((rows, width)),
            whole((rows, width)),
            whole((group, rows // 2, 2 * HD)),
            whole((2, width)),
        ],
        out_shape=[
            shape_of((rows, width), F32),
            shape_of((rows, width), BF),
            shape_of((group, rows // 2, 2 * HD), BF),
            shape_of((2, width), F32),
        ],
        compiler_params=params(),
        cost_estimate=cost(4),
        name="middle_back",
    )(own, other, dy, mid, norms, weights)


def weight_kernel(span, h0, h1, p0, p1, dy0, dy1, a0, a1, out_ref):
    index = pl.program_id(0)

    @pl.when(index < span)
    def _():
        out_ref[...] = (dot(h0[...], p0[...], TN) + dot(h1[...], p1[...], TN)).astype(BF)

    @pl.when(index >= span)
    def _():
        out_ref[...] = (dot(dy0[...], a0[...], TN) + dot(dy1[...], a1[...], TN)).astype(BF)


def weight_grads(h_pair, dpre_pair, dy_pair, act_pair):
    rows, width = h_pair[0].shape
    span = act_pair[0].shape[1] // width
    first = pl.BlockSpec((rows, width), lambda i: (0, jnp.minimum(i, span - 1)))
    second = pl.BlockSpec((rows, width), lambda i: (0, jnp.clip(i - span, 0, span - 1)))
    plain = whole((rows, width))
    return pl.pallas_call(
        functools.partial(weight_kernel, span),
        grid=(2 * span,),
        in_specs=[plain, plain, first, first, plain, plain, second, second],
        out_specs=pl.BlockSpec((width, width), lambda i: (0, i)),
        out_shape=shape_of((width, 2 * span * width), BF),
        compiler_params=params(),
        cost_estimate=cost(7),
        name="weight_grads",
    )(*h_pair, *dpre_pair, *dy_pair, *act_pair)


def proj_kernel(low_ref, o_ref, out_ref):
    out_ref[...] = dot(low_ref[...], o_ref[...], TN).astype(BF)


def proj_grads(low, o):
    width = o.shape[1]
    return pl.pallas_call(
        proj_kernel,
        grid=(1,),
        in_specs=[whole(low.shape), whole(o.shape)],
        out_specs=whole((width, width)),
        out_shape=shape_of((width, width), BF),
        compiler_params=params(),
        cost_estimate=cost(2),
        name="proj_grads",
    )(low, o)


def input_back_kernel(places, packed_ref, w_ref, x_ref, dmid_ref, norm_ref, out_ref, flat_ref):
    rows, _ = x_ref.shape
    half = rows // 2
    for h, place in enumerate(places):
        at = 3 * HD * h
        piece = packed_ref[place]
        flat_ref[:, at : at + 2 * HD] = piece[:rows]
        flat_ref[:half, at + 2 * HD : at + 3 * HD] = piece[rows : rows + half, :HD]
        flat_ref[half:, at + 2 * HD : at + 3 * HD] = piece[rows : rows + half, HD:]
    dh = dot(flat_ref[...], w_ref[...], NT)
    unit, scale = normalize(x_ref[...].astype(F32))
    out_ref[...] = (dmid_ref[...] + normalize_back(dh * norm_ref[0:1, :], unit, scale)).astype(BF)


def input_back(places, packed, weights, late_at, x, dmid, norms):
    rows, width = x.shape
    late = 3 * HD * len(places)
    return pl.pallas_call(
        functools.partial(input_back_kernel, places),
        grid=(1,),
        in_specs=[
            whole(packed.shape),
            pl.BlockSpec((width, late), lambda i: (0, late_at)),
            whole(x.shape),
            whole(dmid.shape),
            whole(norms.shape),
        ],
        out_specs=whole((rows, width)),
        out_shape=shape_of((rows, width), BF),
        scratch_shapes=[pltpu.VMEM((rows, late), BF)],
        compiler_params=params(),
        cost_estimate=cost(5),
        name="input_back",
    )(packed, weights, x, dmid, norms)


def adam_step(master, first_state, second_state, grad_term, step_rate, weight_decay):
    first_new = BETA_ONE * first_state + (1.0 - BETA_ONE) * grad_term
    second_new = BETA_TWO * second_state + (1.0 - BETA_TWO) * grad_term * grad_term
    first_hat = first_new / (1.0 - BETA_ONE**STEP)
    second_hat = second_new / (1.0 - BETA_TWO**STEP)
    master_new = master - step_rate * (
        first_hat / (jnp.sqrt(second_hat) + ADAM_EPS) + weight_decay * master
    )
    return (first_new, second_new, master_new)


def shards(
    tokens,
    cotangent,
    seq_lengths,
    slot_token,
    w_qkv,
    w_proj,
    w_inner,
    w_outer,
    norm_gains,
    norm_biases,
    qkv_first,
    qkv_second,
    proj_first,
    proj_second,
    inner_first,
    inner_second,
    outer_first,
    outer_second,
    norm_first,
    norm_second,
):
    side = lax.axis_index("ha")
    group = lax.axis_size("pb") * lax.axis_size("ka")
    rows, width = tokens.shape[1:]
    total = rows * group
    w_rows = w_qkv.shape[0]
    half_width = w_qkv.shape[2]
    heads = 2 * half_width // HD
    hidden_half = w_inner.shape[1]
    places = head_places(group, heads)
    head_at = [0] * group
    for h, place in enumerate(places):
        head_at[place] = h
    block = min(SCORE_BLOCK, total)

    def swap(a):
        return lax.ppermute(a, "ha", [(0, 1), (1, 0)])

    def ordered(own, other):
        return jnp.where(side == 0, own, other), jnp.where(side == 0, other, own)

    def own_micro(a):
        return lax.dynamic_index_in_dim(a, side, 0, False)

    def other_micro(a):
        return lax.dynamic_index_in_dim(a, 1 - side, 0, False)

    x = own_micro(tokens)
    along_z, along_ka = lax.axis_size("pb"), lax.axis_size("ka")
    stepped = along_z == 4 and along_ka == 4

    def flip(a, axis, size, bit):
        return lax.ppermute(a, axis, [(i, i ^ bit) for i in range(size)])

    if stepped:

        def z_flip(a, bit):
            return flip(a, "pb", along_z, bit)

        def x_flip(a):
            return flip(a, "ka", along_ka, 2)

        def c_flip(a):
            return flip(a, "ka", along_ka, 1)

        own = x[None]
        near, far, own_x, own_c = z_flip(own, 1), z_flip(own, 2), x_flip(own), c_flip(own)
    else:
        x_full = lax.all_gather(x, PLANE, axis=0, tiled=True)
    mine = jnp.concatenate(
        [w_qkv.astype(BF).reshape(w_rows, 3 * half_width), w_proj.astype(BF).T], axis=1
    )
    tok_row = own_micro(slot_token).reshape(1, total)
    mine_other, slot_row = swap(mine), slots_of_tokens(tok_row)
    if stepped:
        near, far, own_x, own_c, mine_other, slot_row = tie(
            near, far, own_x, own_c, mine_other, slot_row
        )
        mid_z = jnp.concatenate([near, far])
        last_z, mid_x, mid_c, own_xc = z_flip(far, 1), x_flip(mid_z), c_flip(mid_z), c_flip(own_x)
    low_half, high_half = ordered(mine, mine_other)
    qkv_rows = jnp.concatenate(
        [
            a[:, : 3 * half_width].reshape(w_rows, 3, heads // 2, HD).swapaxes(1, 2)
            for a in (low_half, high_half)
        ],
        axis=1,
    ).reshape(w_rows, heads, 3 * HD)
    proj_rows = jnp.concatenate(
        [a[:, 3 * half_width :] for a in (low_half, high_half)], axis=1
    )
    norm_master = jnp.concatenate([norm_gains, norm_biases], axis=0)
    head_rows = jnp.stack([qkv_rows[:, head_at[d]] for d in range(group)], axis=0)
    head_rows = jnp.concatenate(
        [
            head_rows,
            jnp.broadcast_to(norm_master.astype(BF).T[None], (group, w_rows, 4)),
            jnp.zeros((group, w_rows, HD - 4), BF),
        ],
        axis=2,
    )
    head_w = lax.all_to_all(head_rows, PLANE, 0, 0, tiled=True)
    if stepped:
        last_z, mid_x, mid_c, own_xc, head_w = tie(last_z, mid_x, mid_c, own_xc, head_w)
        last_x, last_c, mid_xc = x_flip(last_z), c_flip(last_z), c_flip(mid_x)
    else:
        head_w, slot_row = tie(head_w, slot_row)
    head_w = head_w.reshape(width, 4 * HD)
    norms = head_w[:, 3 * HD : 3 * HD + 4].astype(F32).T
    head_w = head_w[:, : 3 * HD].T
    main_rows = jnp.concatenate(
        [
            w_inner.astype(BF),
            w_outer.astype(BF).T,
            proj_rows,
        ],
        axis=1,
    )
    if stepped:
        main_rows, mid_x = tie(main_rows, mid_x)
    else:
        main_rows, x_full = tie(main_rows, x_full)
    main_w = lax.all_gather(main_rows, PLANE, axis=0, tiled=True)
    proj_at = 2 * hidden_half // width

    ends = jnp.cumsum(own_micro(seq_lengths))
    starts = jnp.arange(total // block, dtype=jnp.int32) * block
    first_block = jnp.max(jnp.where(ends[None] <= starts[:, None], ends[None], 0), axis=1) // block
    last_block = jnp.min(jnp.where(ends[None] > starts[:, None], ends[None], total), axis=1) // block
    first_block = first_block.astype(jnp.int32)
    last_block = last_block.astype(jnp.int32)

    if stepped:
        z, xc = lax.axis_index("pb"), lax.axis_index("ka")
        at = jnp.stack([z, 0 * z, xc // 2, xc % 2]).astype(jnp.int32)
        groups = ((own, own_x, own_c, own_xc), (mid_z, mid_x, mid_c, mid_xc))
        buffers = qkv_of_piece(at, groups, head_w, norms, total, ())
        last_x, last_c, *buffers = tie(last_x, last_c, *buffers)
        at = jnp.stack([z, 0 * z + 3, xc // 2, xc % 2]).astype(jnp.int32)
        groups = ((last_z, last_x, last_c, c_flip(last_x)),)
        buffers = qkv_of_piece(at, groups, head_w, norms, total, buffers)
        unit, qkv = buffers
    else:
        unit, qkv = qkv_of_head(x_full, head_w, norms)
    q, qt, k, v, vt = sort_qkv(slot_row, qkv)
    o, o_low, lse = attend(first_block, qt, k, vt, block)
    late_rows, o_low = tie(qkv_rows.reshape(w_rows, -1), o_low)
    late_w = lax.all_gather(late_rows, PLANE, axis=0, tiled=True)
    o_packed = lax.all_to_all(slots_out(tok_row, o_low, group), PLANE, 0, 0, tiled=True)
    mid, h_own, o_own = middle(places, x, o_packed, main_w, proj_at, norms)
    h_other = swap(h_own)
    dy_own, dy_other = own_micro(cotangent), other_micro(cotangent)
    act_own, dpre_own, dh_own, out_own = hidden(h_own, dy_own, main_w, hidden_half, F32)
    h_other, dh_own = tie(h_other, dh_own)
    act_other, dpre_other, dh_send, out_send = hidden(h_other, dy_other, main_w, hidden_half, BF)
    dh_got = swap(dh_send)
    main_grad = weight_grads(
        (h_own, h_other), (dpre_own, dpre_other), (dy_own, dy_other), (act_own, act_other)
    )
    dh_got, main_grad = tie(dh_got, main_grad)

    dmid, dmid_low, g_packed, sums_two = middle_back(
        places, group, dh_own, dh_got, dy_own, mid, norms, main_w, proj_at
    )
    late_w, main_grad, _ = tie(late_w, main_grad, dmid_low)
    main_sum = lax.psum_scatter(main_grad, PLANE, scatter_dimension=0, tiled=True)
    g_packed = lax.all_to_all(g_packed, PLANE, 0, 0, tiled=True)
    proj_grad = proj_grads(dmid_low, o_own).reshape(group, w_rows, width)
    proj_grad, g_packed, out_send, out_own = tie(proj_grad, g_packed, out_send, out_own)
    proj_grad = lax.all_to_all(proj_grad, PLANE, 0, 0, tiled=True)
    out_got = swap(out_send)
    layer_own = (mid + out_own + out_got.astype(F32)).astype(BF)
    layer_out = jnp.stack(ordered(layer_own, swap(layer_own)))
    g, gt, delta = sort_grad(slot_row, g_packed, o)
    dqkv = attend_back(last_block, q, qt, k, v, g, gt, lse, delta, block)
    packed, head_grad = all_grads_out(tok_row, dqkv, unit, head_w, norms, sums_two, group)
    packed, proj_grad, layer_out = tie(packed, proj_grad, layer_out)
    dqkv_own = lax.all_to_all(packed, PLANE, 0, 0, tiled=True)

    head_grad = head_grad.reshape(group, 2, w_rows // 2, 4 * HD)
    keep, send = ordered(head_grad[:, 0], head_grad[:, 1])
    keep = (keep.astype(F32) + swap(send).astype(F32)).astype(BF)
    keep, dqkv_own, main_sum = tie(keep, dqkv_own, main_sum)
    input_low = input_back(places, dqkv_own, late_w, 0, x, dmid, norms)
    head_grad = lax.all_to_all(keep, PLANE, 0, 0, tiled=True)
    input_grad = jnp.stack(ordered(input_low, swap(input_low))).astype(F32)

    norm_parts = head_grad[:, :, 3 * HD : 3 * HD + 8].astype(F32)
    norm_parts = norm_parts[:, :, :4] + norm_parts[:, :, 4:]
    first_sums = sum(norm_parts[place] for place in places)
    second_sums = jnp.sum(norm_parts, axis=0)
    norm_grad = jnp.stack(
        [first_sums[:, 0], second_sums[:, 1], first_sums[:, 2], second_sums[:, 3]]
    )
    norm_grad = jnp.concatenate(ordered(norm_grad, swap(norm_grad)), axis=1)
    qkv_part = jnp.stack([head_grad[place, :, : 3 * HD] for place in places], axis=1)
    qkv_part = qkv_part.reshape(w_rows // 2, 2, heads // 2, 3, HD)
    keep, send = ordered(qkv_part[:, 0], qkv_part[:, 1])
    qkv_grad = jnp.concatenate(ordered(keep, swap(send)), axis=0).astype(F32)
    qkv_grad = qkv_grad.swapaxes(1, 2).reshape(w_rows, 3, half_width)
    inner_grad = main_sum[:, :hidden_half].astype(F32)
    outer_grad = main_sum[:, hidden_half:].astype(F32).T
    proj_part = jnp.sum(proj_grad.astype(F32), axis=0)
    keep, send = ordered(proj_part[:, :half_width], proj_part[:, half_width:])
    proj_grad = (keep + swap(send.astype(BF)).astype(F32)).T

    qkv_out = adam_step(w_qkv, qkv_first, qkv_second, qkv_grad / MICRO, RATE_MATRIX, DECAY_RATE)
    proj_out = adam_step(w_proj, proj_first, proj_second, proj_grad / MICRO, RATE_PROJ, DECAY_RATE)
    inner_out = adam_step(
        w_inner, inner_first, inner_second, inner_grad / MICRO, RATE_MATRIX, DECAY_RATE
    )
    outer_out = adam_step(
        w_outer, outer_first, outer_second, outer_grad / MICRO, RATE_MATRIX, DECAY_RATE
    )
    norm_grad = norm_grad / MICRO
    norm_out = adam_step(norm_master, norm_first, norm_second, norm_grad, RATE_NORM, 0.0)
    norm_two_grad = jnp.stack([norm_grad[1], norm_grad[3]])
    return (
        layer_out,
        input_grad,
        *qkv_out,
        *proj_out,
        *inner_out,
        *outer_out,
        *norm_out,
        norm_two_grad,
    )


def solution(mesh):
    tok = P(None, PLANE, None)
    qkv = P(PLANE, None, "ha")
    down = P("ha", PLANE)
    inner = P(PLANE, "ha")
    norm = P(None, PLANE)
    in_specs = (
        (tok, tok, P(), P(), qkv, down, inner, down, norm, norm)
        + (qkv, qkv, down, down, inner, inner, down, down, norm, norm)
    )
    out_specs = (
        (tok, tok, qkv, qkv, qkv, down, down, down)
        + (inner, inner, inner, down, down, down, norm, norm, norm, norm)
    )
    return jax.shard_map(shards, mesh=mesh, in_specs=in_specs, out_specs=out_specs, check_vma=False)
```

```python
import functools

import jax
import jax.numpy as jnp
from jax import lax
from jax.experimental import pallas as pl
from jax.experimental.pallas import tpu as pltpu
from jax.sharding import PartitionSpec as P

HD = 64
MICRO = 2
STEP = 8
NORM_EPS = 1e-05
BETA_ONE = 0.9
BETA_TWO = 0.95
ADAM_EPS = 1e-08
DECAY_RATE = 0.1
RATE_MATRIX = 0.02
RATE_PROJ = 0.6
RATE_NORM = 0.1
BF = jnp.bfloat16
F32 = jnp.float32
PLANE = ("pb", "ka")
VMEM_LIMIT = 60 * 1024 * 1024
SCORE_BLOCK = 512
SHORT = 4096
STRAIGHT = 4
NT = (((1,), (1,)), ((), ()))
NN = (((1,), (0,)), ((), ()))
TN = (((0,), (0,)), ((), ()))


def dot(a, b, dims=NN):
    return lax.dot_general(a, b, dims, preferred_element_type=F32)


def params(steps=1):
    return pltpu.CompilerParams(
        dimension_semantics=("arbitrary",) * steps, vmem_limit_bytes=VMEM_LIMIT
    )


def cost(us):
    return pl.CostEstimate(flops=int(us * 2e8), bytes_accessed=int(us * 1e6), transcendentals=0)


def tie(*arrays):
    return lax.optimization_barrier(arrays)


def whole(shape):
    return pl.BlockSpec(shape, lambda *_: (0,) * len(shape))


def shape_of(shape, dtype):
    return jax.ShapeDtypeStruct(shape, dtype)


def head_places(group, heads):
    return tuple(h * group // heads for h in range(heads))


def normalize(x):
    center = x - jnp.mean(x, axis=-1, keepdims=True)
    spread = jnp.mean(center * center, axis=-1, keepdims=True)
    scale = lax.rsqrt(spread + NORM_EPS)
    return center * scale, scale


def normalize_back(grad, unit, scale):
    return scale * (
        grad
        - jnp.mean(grad, axis=-1, keepdims=True)
        - unit * jnp.mean(grad * unit, axis=-1, keepdims=True)
    )


def low_match(ids):
    low = lax.bitwise_and(ids, 255).astype(F32).astype(BF)
    line = lax.broadcasted_iota(jnp.int32, (256, 1), 0).astype(F32).astype(BF)
    return jnp.where(low == line, jnp.ones((), BF), jnp.zeros((), BF))


def moved(ids_ref, match_ref, source_ref, stack_ref, first):
    features = source_ref.shape[0]
    chunk = stack_ref.shape[1]
    total = None
    for part in range(source_ref.shape[1] // chunk):
        cut = slice(part * chunk, (part + 1) * chunk)
        high = lax.shift_right_logical(ids_ref[:, cut], 8)
        source = source_ref[:, cut]
        for block in range(stack_ref.shape[0] // features):
            stack_ref[block * features : (block + 1) * features, :] = jnp.where(
                high == first + block, source, jnp.zeros((), BF)
            )
        piece = dot(stack_ref[...], match_ref[:, cut], NT)
        total = piece if total is None else total + piece
    return total


def sort_block(total):
    return total if total <= SHORT else 1024


def stack_shape(features, columns, total):
    return pltpu.VMEM((features * columns // 256, min(3072, total)), BF)


def place_kernel(tok_ref, out_ref):
    total = tok_ref.shape[1]
    count = total // 256
    ids = tok_ref[...]
    high = lax.shift_right_logical(ids, 8)
    slot = lax.broadcasted_iota(jnp.int32, (1, total), 1)
    rows = lax.broadcasted_iota(jnp.int32, (count, 1), 0)
    match = low_match(ids)

    def part(values):
        picked = jnp.where(high == rows, values.astype(F32), 0.0).astype(BF)
        return dot(picked, match, NT)

    found = part(lax.shift_right_logical(slot, 8)) * 256.0 + part(lax.bitwise_and(slot, 255))
    found = found.astype(jnp.int32)
    for a in range(count):
        out_ref[:, a * 256 : (a + 1) * 256] = found[a : a + 1]


def slots_of_tokens(tok_row):
    return pl.pallas_call(
        place_kernel,
        grid=(1,),
        in_specs=[whole(tok_row.shape)],
        out_specs=whole(tok_row.shape),
        out_shape=shape_of(tok_row.shape, jnp.int32),
        compiler_params=params(),
        cost_estimate=cost(2),
        name="slots_of_tokens",
    )(tok_row)


def qkv_kernel(x_ref, w_ref, norm_ref, unit_ref, qkv_ref):
    unit, _ = normalize(x_ref[...].astype(F32))
    h = (unit * norm_ref[0:1, :] + norm_ref[2:3, :]).astype(BF)
    unit_ref[...] = unit.astype(BF)
    qkv_ref[...] = dot(w_ref[...], h, NT).astype(BF)


def qkv_piece_kernel(counts, at_ref, *refs):
    sources = refs[: 4 * len(counts)]
    w_ref, norm_ref = refs[4 * len(counts) :][:2]
    unit_ref, qkv_ref, x_ref = refs[-3:]
    rows = x_ref.shape[0] // 2
    even = at_ref[3] == 0
    slot = 0
    for group, count in enumerate(counts):
        for place in range(count):
            for side in range(2):

                @pl.when((pl.program_id(0) == slot) & (pl.program_id(1) == side))
                def _():
                    own = sources[4 * group + side][place]
                    other = sources[4 * group + 2 + side][place]
                    x_ref[:rows, :] = jnp.where(even, own, other)
                    x_ref[rows:, :] = jnp.where(even, other, own)

            slot += 1
    unit, _ = normalize(x_ref[...].astype(F32))
    h = (unit * norm_ref[0:1, :] + norm_ref[2:3, :]).astype(BF)
    unit_ref[...] = unit.astype(BF)
    qkv_ref[...] = dot(w_ref[...], h, NT).astype(BF)


def qkv_of_piece(at, groups, head_w, norms, total, buffers):
    counts = tuple(group[0].shape[0] for group in groups)
    pieces = [a for group in groups for a in group]
    _, rows, width = pieces[0].shape
    kept = [pl.BlockSpec(memory_space=pl.ANY)] * len(buffers)
    first = 1 + len(pieces) + 2

    def place(i, j, at):
        return (at[0] ^ (at[1] + i)) * 2 + (at[2] ^ j)

    return pl.pallas_call(
        functools.partial(qkv_piece_kernel, counts),
        grid_spec=pltpu.PrefetchScalarGridSpec(
            num_scalar_prefetch=1,
            grid=(sum(counts), 2),
            in_specs=[whole(a.shape) for a in (*pieces, head_w, norms)] + kept,
            out_specs=[
                pl.BlockSpec((2 * rows, width), lambda i, j, at: (place(i, j, at), 0)),
                pl.BlockSpec((head_w.shape[0], 2 * rows), lambda i, j, at: (0, place(i, j, at))),
            ],
            scratch_shapes=[pltpu.VMEM((2 * rows, width), BF)],
        ),
        out_shape=[shape_of((total, width), BF), shape_of((head_w.shape[0], total), BF)],
        input_output_aliases={first: 0, first + 1: 1} if buffers else {},
        compiler_params=params(2),
        cost_estimate=cost(3 * sum(counts)),
        name="qkv_piece",
    )(at, *pieces, head_w, norms, *buffers)


def qkv_of_head(x_full, head_w, norms):
    rows, width = x_full.shape
    block = min(512, rows)
    return pl.pallas_call(
        qkv_kernel,
        grid=(rows // block,),
        in_specs=[
            pl.BlockSpec((block, width), lambda i: (i, 0)),
            whole(head_w.shape),
            whole(norms.shape),
        ],
        out_specs=[
            pl.BlockSpec((block, width), lambda i: (i, 0)),
            pl.BlockSpec((head_w.shape[0], block), lambda i: (0, i)),
        ],
        out_shape=[shape_of((rows, width), BF), shape_of((head_w.shape[0], rows), BF)],
        compiler_params=params(),
        cost_estimate=cost(8),
        name="qkv_head",
    )(x_full, head_w, norms)


def sort_kernel(tok_ref, qkv_ref, q_ref, qt_ref, k_ref, v_ref, vt_ref, match_ref, stack_ref):
    @pl.when(pl.program_id(0) == 0)
    def _():
        match_ref[...] = low_match(tok_ref[...])

    count = k_ref.shape[0] // 256
    found = moved(tok_ref, match_ref, qkv_ref, stack_ref, pl.program_id(0) * count)
    for part in range(count):
        cut = slice(part * 256, (part + 1) * 256)
        at = 3 * HD * part
        query = found[at : at + HD] * float(HD) ** -0.5
        value = found[at + 2 * HD : at + 3 * HD]
        qt_ref[:, cut] = query.astype(BF)
        q_ref[cut, :] = query.T.astype(BF)
        k_ref[cut, :] = found[at + HD : at + 2 * HD].T.astype(BF)
        v_ref[cut, :] = value.T.astype(BF)
        vt_ref[:, cut] = value.astype(BF)


def sort_qkv(tok_row, qkv):
    rows = qkv.shape[1]
    block = sort_block(rows)
    narrow = (pl.BlockSpec((block, HD), lambda i: (i, 0)), shape_of((rows, HD), BF))
    wide = (pl.BlockSpec((HD, block), lambda i: (0, i)), shape_of((HD, rows), BF))
    outs = (narrow, wide, narrow, narrow, wide)
    return pl.pallas_call(
        sort_kernel,
        grid=(rows // block,),
        in_specs=[whole(tok_row.shape), whole(qkv.shape)],
        out_specs=[spec for spec, _ in outs],
        out_shape=[shape for _, shape in outs],
        scratch_shapes=[pltpu.VMEM((256, rows), BF), stack_shape(3 * HD, block, rows)],
        compiler_params=params(),
        cost_estimate=cost(5),
        name="sort_qkv",
    )(tok_row, qkv)


def causal(block):
    return lax.broadcasted_iota(jnp.int32, (block, block), 0) <= lax.broadcasted_iota(
        jnp.int32, (block, block), 1
    )


def forward_kernel(first_ref, qt_ref, k_ref, vt_ref, o_ref, low_ref, lse_ref):
    block = qt_ref.shape[1]
    index = pl.program_id(0)
    query = qt_ref[...]

    def step(key_block, state, diagonal):
        top, total, acc = state
        at = pl.multiple_of(key_block * block, block)
        scores = dot(k_ref[pl.ds(at, block), :], query)
        square = scores * scores + 1.0
        inverse = lax.rsqrt(square)
        radius = square * inverse
        if diagonal:
            radius = jnp.where(causal(block), radius, -1e30)
        new_top = jnp.maximum(top, jnp.max(radius, axis=0, keepdims=True))
        weights = jnp.exp(radius - new_top)
        shrink = jnp.exp(top - new_top)
        signed = (scores * inverse * weights).astype(BF)
        acc = acc * shrink + dot(vt_ref[:, pl.ds(at, block)], signed)
        total = total * shrink + jnp.sum(weights, axis=0, keepdims=True)
        return (new_top, total, acc)

    def finish(state):
        top, total, acc = state
        out = acc * (1.0 / total)
        o_ref[...] = out
        low_ref[...] = out.astype(BF)
        lse_ref[...] = top + jnp.log(total)

    start = (
        jnp.zeros((1, block), F32),
        jnp.zeros((1, block), F32),
        jnp.zeros((HD, block), F32),
    )
    earlier = index - first_ref[index]
    for count in range(STRAIGHT):

        @pl.when(earlier == count)
        def _():
            state = step(index, start, True)
            for back in range(1, count + 1):
                state = step(index - back, state, False)
            finish(state)

    @pl.when(earlier >= STRAIGHT)
    def _():
        state = lax.fori_loop(first_ref[index], index, lambda j, s: step(j, s, False), start)
        finish(step(index, state, True))


def attend(first_block, qt, k, vt, block):
    rows = k.shape[0]
    return pl.pallas_call(
        forward_kernel,
        grid_spec=pltpu.PrefetchScalarGridSpec(
            num_scalar_prefetch=1,
            grid=(rows // block,),
            in_specs=[
                pl.BlockSpec((HD, block), lambda i, *_: (0, i)),
                whole(k.shape),
                whole(vt.shape),
            ],
            out_specs=[
                pl.BlockSpec((HD, block), lambda i, *_: (0, i)),
                pl.BlockSpec((HD, block), lambda i, *_: (0, i)),
                pl.BlockSpec((1, block), lambda i, *_: (0, i)),
            ],
        ),
        out_shape=[shape_of((HD, rows), F32), shape_of((HD, rows), BF), shape_of((1, rows), F32)],
        compiler_params=params(),
        cost_estimate=cost(13),
        name="attend_fwd",
    )(first_block, qt, k, vt)


def slots_out_kernel(rows, slot_ref, low_ref, out_ref, match_ref, stack_ref):
    half = rows // 2

    @pl.when(pl.program_id(0) == 0)
    def _():
        match_ref[...] = low_match(slot_ref[...])

    owners = out_ref.shape[0]
    count = owners * rows // 256
    found = moved(slot_ref, match_ref, low_ref, stack_ref, pl.program_id(0) * count)
    found = jnp.concatenate([found[p * HD : (p + 1) * HD].T for p in range(count)], axis=0)
    found = found.astype(BF)
    for d in range(owners):
        at = d * rows
        out_ref[d] = jnp.concatenate([found[at : at + half], found[at + half : at + rows]], axis=1)


def slots_out(slot_row, low, group):
    total = slot_row.shape[1]
    rows = total // group
    count = owners_per_step(group, rows)
    return pl.pallas_call(
        functools.partial(slots_out_kernel, rows),
        grid=(group // count,),
        in_specs=[whole(slot_row.shape), whole(low.shape)],
        out_specs=pl.BlockSpec((count, rows // 2, 2 * HD), lambda i: (i, 0, 0)),
        out_shape=shape_of((group, rows // 2, 2 * HD), BF),
        scratch_shapes=[pltpu.VMEM((256, total), BF), stack_shape(HD, count * rows, total)],
        compiler_params=params(),
        cost_estimate=cost(3),
        name="slots_out",
    )(slot_row, low)


def owners_per_step(group, rows, most=16):
    for count in (16, 8, 4, 2, 1):
        if count > (most if group * rows <= SHORT else 4):
            continue
        if group % count == 0 and count * rows % 256 == 0:
            return count
    return group


def sort_grad_kernel(
    tok_ref, packed_ref, o_ref, g_ref, gt_ref, delta_ref, slots_ref, match_ref, stack_ref
):
    group, half, _ = packed_ref.shape

    @pl.when(pl.program_id(0) == 0)
    def _():
        match_ref[...] = low_match(tok_ref[...])
        for d in range(group):
            piece = packed_ref[d].astype(F32).T.astype(BF)
            slots_ref[:, 2 * d * half : (2 * d + 1) * half] = piece[:HD]
            slots_ref[:, (2 * d + 1) * half : (2 * d + 2) * half] = piece[HD:]

    count = g_ref.shape[0] // 256
    found = moved(tok_ref, match_ref, slots_ref, stack_ref, pl.program_id(0) * count)
    for part in range(count):
        cut = slice(part * 256, (part + 1) * 256)
        grad = found[part * HD : (part + 1) * HD]
        gt_ref[:, cut] = grad.astype(BF)
        g_ref[cut, :] = grad.T.astype(BF)
        delta_ref[:, cut] = jnp.sum(grad * o_ref[:, cut], axis=0, keepdims=True)


def sort_grad(tok_row, packed, o):
    rows = o.shape[1]
    block = sort_block(rows)
    wide = pl.BlockSpec((HD, block), lambda i: (0, i))
    return pl.pallas_call(
        sort_grad_kernel,
        grid=(rows // block,),
        in_specs=[whole(tok_row.shape), whole(packed.shape), wide],
        out_specs=[
            pl.BlockSpec((block, HD), lambda i: (i, 0)),
            wide,
            pl.BlockSpec((1, block), lambda i: (0, i)),
        ],
        out_shape=[shape_of((rows, HD), BF), shape_of((HD, rows), BF), shape_of((1, rows), F32)],
        scratch_shapes=[
            pltpu.VMEM((HD, rows), BF),
            pltpu.VMEM((256, rows), BF),
            stack_shape(HD, block, rows),
        ],
        compiler_params=params(),
        cost_estimate=cost(4),
        name="sort_grad",
    )(tok_row, packed, o)


def backward_kernel(
    last_ref, q_ref, qt_ref, k_ref, v_ref, g_ref, gt_ref, lse_ref, delta_ref, out_ref, dq_ref, dk_ref, dv_ref
):
    block = k_ref.shape[0]
    index = pl.program_id(0)

    @pl.when(index == 0)
    def _():
        dq_ref[...] = jnp.zeros_like(dq_ref)

    key = k_ref[...]
    key_t = key.astype(F32).T.astype(BF)
    value = v_ref[...]

    def step(query_block, diagonal):
        at = pl.multiple_of(query_block * block, block)
        scores = dot(key, qt_ref[:, pl.ds(at, block)])
        square = scores * scores + 1.0
        inverse = lax.rsqrt(square)
        shifted = square * inverse - lse_ref[:, pl.ds(at, block)]
        if diagonal:
            shifted = jnp.where(causal(block), shifted, -1e30)
        weights = jnp.exp(shifted)
        slope = scores * inverse
        along = dot(value, gt_ref[:, pl.ds(at, block)])
        bend = 1.0 + inverse * inverse * (inverse - 1.0)
        score_grad = weights * (bend * along - slope * delta_ref[:, pl.ds(at, block)])
        signed = (slope * weights).astype(BF)
        low_grad = score_grad.astype(BF)
        dv = dot(signed, g_ref[pl.ds(at, block), :])
        dk = dot(low_grad, q_ref[pl.ds(at, block), :])
        dq_ref[:, pl.ds(at, block)] += dot(key_t, low_grad)
        return dk, dv

    def finish(dk, dv):
        at = pl.multiple_of(index * block, block)
        out_ref[:HD] = (dq_ref[:, pl.ds(at, block)] * float(HD) ** -0.5).astype(BF)
        out_ref[HD : 2 * HD] = dk.T.astype(BF)
        out_ref[2 * HD :] = dv.T.astype(BF)

    later = last_ref[index] - index
    for count in range(1, STRAIGHT + 1):

        @pl.when(later == count)
        def _():
            dk, dv = step(index, True)
            for ahead in range(1, count):
                dk_more, dv_more = step(index + ahead, False)
                dk, dv = dk + dk_more, dv + dv_more
            finish(dk, dv)

    @pl.when(later > STRAIGHT)
    def _():
        dk_ref[...], dv_ref[...] = step(index, True)

        def body(query_block, carry):
            dk_more, dv_more = step(query_block, False)
            dk_ref[...] += dk_more
            dv_ref[...] += dv_more
            return carry

        lax.fori_loop(index + 1, last_ref[index], body, 0)
        finish(dk_ref[...], dv_ref[...])


def attend_back(last_block, q, qt, k, v, g, gt, lse, delta, block):
    rows = q.shape[0]
    return pl.pallas_call(
        backward_kernel,
        grid_spec=pltpu.PrefetchScalarGridSpec(
            num_scalar_prefetch=1,
            grid=(rows // block,),
            in_specs=[
                whole(q.shape),
                whole(qt.shape),
                pl.BlockSpec((block, HD), lambda i, *_: (i, 0)),
                pl.BlockSpec((block, HD), lambda i, *_: (i, 0)),
                whole(g.shape),
                whole(gt.shape),
                whole(lse.shape),
                whole(delta.shape),
            ],
            out_specs=pl.BlockSpec((3 * HD, block), lambda i, *_: (0, i)),
            scratch_shapes=[
                pltpu.VMEM((HD, rows), F32),
                pltpu.VMEM((block, HD), F32),
                pltpu.VMEM((block, HD), F32),
            ],
        ),
        out_shape=shape_of((3 * HD, rows), BF),
        compiler_params=params(),
        cost_estimate=cost(19),
        name="attend_bwd",
    )(last_block, q, qt, k, v, g, gt, lse, delta)


def head_results(acc, column, w_ref, norm_ref, sums_ref):
    weights = w_ref[...].astype(F32)
    grad = acc * norm_ref[0:1, :] + column * norm_ref[2:3, :]
    sums = jnp.concatenate(
        [
            jnp.sum(weights * acc, axis=0, keepdims=True),
            sums_ref[0:1, :],
            jnp.sum(weights * column, axis=0, keepdims=True),
            sums_ref[1:2, :],
        ],
        axis=0,
    )
    top = sums.astype(BF).astype(F32)
    rest = jnp.concatenate([top, sums - top, jnp.zeros((HD - 8, sums.shape[1]), F32)], axis=0)
    return jnp.concatenate([grad, rest], axis=0).T.astype(BF)


def grads_out_kernel(rows, slot_ref, grad_ref, out_ref, low_ref, match_ref, stack_ref):
    half = rows // 2
    step = pl.program_id(0)

    @pl.when(step == 0)
    def _():
        match_ref[...] = low_match(slot_ref[...])

    count = out_ref.shape[0]
    parts = count * rows // 256
    found = moved(slot_ref, match_ref, grad_ref, stack_ref, step * parts)
    turned = []
    for p in range(parts):
        piece = found[3 * HD * p : 3 * HD * (p + 1)]
        low_ref[:, p * 256 : (p + 1) * 256] = piece.astype(BF)
        turned.append(piece.T)
    turned = jnp.concatenate(turned, axis=0).astype(BF)
    for d in range(count):
        at = d * rows
        out_ref[d, :rows, :] = turned[at : at + rows, : 2 * HD]
        out_ref[d, rows:, :] = jnp.concatenate(
            [turned[at : at + half, 2 * HD :], turned[at + half : at + rows, 2 * HD :]], axis=1
        )


def grads_out(slot_row, grads, group):
    total = slot_row.shape[1]
    rows = total // group
    out_rows = rows + rows // 2
    count = owners_per_step(group, rows, 8)
    return pl.pallas_call(
        functools.partial(grads_out_kernel, rows),
        grid=(group // count,),
        in_specs=[whole(slot_row.shape), whole(grads.shape)],
        out_specs=[
            pl.BlockSpec((count, out_rows, 2 * HD), lambda i: (i, 0, 0)),
            pl.BlockSpec((3 * HD, count * rows), lambda i: (0, i)),
        ],
        out_shape=[shape_of((group, out_rows, 2 * HD), BF), shape_of((3 * HD, total), BF)],
        scratch_shapes=[
            pltpu.VMEM((256, total), BF),
            stack_shape(3 * HD, count * rows, total),
        ],
        compiler_params=params(),
        cost_estimate=cost(7),
        name="grads_out",
    )(slot_row, grads)


def head_weight_kernel(grad_ref, unit_ref, w_ref, norm_ref, sums_ref, head_ref, acc_ref, line_ref):
    step = pl.program_id(0)
    term = dot(grad_ref[...], unit_ref[...])
    line = jnp.sum(grad_ref[...].astype(F32), axis=1, keepdims=True)

    @pl.when(step == 0)
    def _():
        acc_ref[...] = term
        line_ref[...] = line

    @pl.when(step > 0)
    def _():
        acc_ref[...] += term
        line_ref[...] += line

    @pl.when(step == pl.num_programs(0) - 1)
    def _():
        head_ref[...] = head_results(acc_ref[...], line_ref[...], w_ref, norm_ref, sums_ref)


def head_weight_grad(grads, unit, head_w, norms, sums_two):
    total, width = unit.shape
    block = 768 if total % 768 == 0 else total
    return pl.pallas_call(
        head_weight_kernel,
        grid=(total // block,),
        in_specs=[
            pl.BlockSpec((3 * HD, block), lambda i: (0, i)),
            pl.BlockSpec((block, width), lambda i: (i, 0)),
            whole(head_w.shape),
            whole(norms.shape),
            whole(sums_two.shape),
        ],
        out_specs=whole((width, 4 * HD)),
        out_shape=shape_of((width, 4 * HD), BF),
        scratch_shapes=[pltpu.VMEM((3 * HD, width), F32), pltpu.VMEM((3 * HD, 1), F32)],
        compiler_params=params(),
        cost_estimate=cost(5),
        name="head_weight",
    )(grads, unit, head_w, norms, sums_two)


def middle_kernel(places, x_ref, packed_ref, proj_ref, norm_ref, mid_ref, h_ref, o_ref):
    half = packed_ref.shape[1]
    for h, place in enumerate(places):
        piece = packed_ref[place]
        o_ref[:half, h * HD : (h + 1) * HD] = piece[:, :HD]
        o_ref[half:, h * HD : (h + 1) * HD] = piece[:, HD:]
    mid = x_ref[...].astype(F32) + dot(o_ref[...], proj_ref[...], NT)
    mid_ref[...] = mid
    unit, _ = normalize(mid)
    h_ref[...] = (unit * norm_ref[1:2, :] + norm_ref[3:4, :]).astype(BF)


def middle(places, x, packed, weights, proj_at, norms):
    rows, width = x.shape
    return pl.pallas_call(
        functools.partial(middle_kernel, places),
        grid=(1,),
        in_specs=[
            whole(x.shape),
            whole(packed.shape),
            pl.BlockSpec((width, width), lambda i: (0, proj_at)),
            whole(norms.shape),
        ],
        out_specs=[whole((rows, width))] * 3,
        out_shape=[
            shape_of((rows, width), F32),
            shape_of((rows, width), BF),
            shape_of((rows, width), BF),
        ],
        compiler_params=params(),
        cost_estimate=cost(3),
        name="middle",
    )(x, packed, weights, norms)


def hidden_kernel(h_ref, dy_ref, inner_ref, outer_ref, act_ref, dpre_ref, dh_ref, dh_acc):
    pre = dot(h_ref[...], inner_ref[...])
    root = 0.7978845608028654
    squared = pre * pre
    bend = jnp.tanh(root * (pre + 0.044715 * (squared * pre)))
    act_ref[...] = (0.5 * pre * (1.0 + bend)).astype(BF)
    slope = 0.5 * (1.0 + bend) + 0.5 * pre * (1.0 - bend * bend) * (
        root * (1.0 + 3.0 * 0.044715 * squared)
    )
    dpre = (dot(dy_ref[...], outer_ref[...]) * slope).astype(BF)
    dpre_ref[...] = dpre
    dh = dot(dpre, inner_ref[...], NT)

    @pl.when(pl.program_id(0) == 0)
    def _():
        dh_acc[...] = dh

    @pl.when(pl.program_id(0) > 0)
    def _():
        dh_acc[...] += dh

    @pl.when(pl.program_id(0) == pl.num_programs(0) - 1)
    def _():
        dh_ref[...] = dh_acc[...].astype(dh_ref.dtype)


def hidden(h, dy, weights, hidden_width, kind):
    rows, width = h.shape
    chunk = 512
    steps = hidden_width // chunk
    return pl.pallas_call(
        hidden_kernel,
        grid=(steps,),
        in_specs=[
            whole(h.shape),
            whole(dy.shape),
            pl.BlockSpec((width, chunk), lambda i: (0, i)),
            pl.BlockSpec((width, chunk), lambda i: (0, i + steps)),
        ],
        out_specs=[
            pl.BlockSpec((rows, chunk), lambda i: (0, i)),
            pl.BlockSpec((rows, chunk), lambda i: (0, i)),
            whole((rows, width)),
        ],
        out_shape=[
            shape_of((rows, hidden_width), BF),
            shape_of((rows, hidden_width), BF),
            shape_of((rows, width), kind),
        ],
        scratch_shapes=[pltpu.VMEM((rows, width), F32)],
        compiler_params=params(),
        cost_estimate=cost(6),
        name="hidden",
    )(h, dy, weights, weights)


def layer_kernel(own_ref, other_ref, outer_ref, out_ref, send_ref):
    out_ref[...] = dot(own_ref[...], outer_ref[...], NT)
    send_ref[...] = dot(other_ref[...], outer_ref[...], NT).astype(BF)


def layer_terms(act_own, act_other, weights):
    rows, span = act_own.shape
    width = weights.shape[0]
    return pl.pallas_call(
        layer_kernel,
        grid=(1,),
        in_specs=[
            whole(act_own.shape),
            whole(act_other.shape),
            pl.BlockSpec((width, span), lambda i: (0, 1)),
        ],
        out_specs=[whole((rows, width))] * 2,
        out_shape=[shape_of((rows, width), F32), shape_of((rows, width), BF)],
        compiler_params=params(),
        cost_estimate=cost(4),
        name="layer_terms",
    )(act_own, act_other, weights)


def middle_back_kernel(
    places, own_ref, other_ref, dy_ref, mid_ref, norm_ref, proj_ref, dmid_ref, low_ref, packed_ref, sums_ref
):
    half = packed_ref.shape[1]
    dh = own_ref[...] + other_ref[...].astype(F32)
    unit, scale = normalize(mid_ref[...])
    sums_ref[0:1, :] = jnp.sum(dh * unit, axis=0, keepdims=True)
    sums_ref[1:2, :] = jnp.sum(dh, axis=0, keepdims=True)
    dmid = dy_ref[...].astype(F32) + normalize_back(dh * norm_ref[1:2, :], unit, scale)
    dmid_ref[...] = dmid
    low = dmid.astype(BF)
    low_ref[...] = low
    grad = dot(low, proj_ref[...]).astype(BF)
    packed_ref[...] = jnp.zeros_like(packed_ref)
    for h, place in enumerate(places):
        cut = slice(h * HD, (h + 1) * HD)
        packed_ref[place] = jnp.concatenate([grad[:half, cut], grad[half:, cut]], axis=1)


def middle_back(places, group, own, other, dy, mid, norms, weights, proj_at):
    rows, width = mid.shape
    return pl.pallas_call(
        functools.partial(middle_back_kernel, places),
        grid=(1,),
        in_specs=[
            whole(own.shape),
            whole(other.shape),
            whole(dy.shape),
            whole(mid.shape),
            whole(norms.shape),
            pl.BlockSpec((width, width), lambda i: (0, proj_at)),
        ],
        out_specs=[
            whole((rows, width)),
            whole((rows, width)),
            whole((group, rows // 2, 2 * HD)),
            whole((2, width)),
        ],
        out_shape=[
            shape_of((rows, width), F32),
            shape_of((rows, width), BF),
            shape_of((group, rows // 2, 2 * HD), BF),
            shape_of((2, width), F32),
        ],
        compiler_params=params(),
        cost_estimate=cost(4),
        name="middle_back",
    )(own, other, dy, mid, norms, weights)


def split_rows(share, at_ref, block, scratch_ref, keep_ref, send_ref):
    if share == 0:
        half = keep_ref.shape[0]
        keep_ref[...] = block[:half].astype(BF)
        send_ref[...] = block[half:].astype(BF)
        return
    scratch_ref[...] = block
    for pair in range(keep_ref.shape[0] // share):
        cut = slice(pair * share, (pair + 1) * share)
        for target, parity in ((keep_ref, at_ref[0]), (send_ref, 1 - at_ref[0])):
            at = pl.multiple_of((2 * pair + parity) * share, share)
            target[cut, :] = scratch_ref[pl.ds(at, share), :].astype(BF)


def weight_kernel(share, at_ref, a0, a1, b0, b1, keep_ref, send_ref, scratch_ref):
    block = dot(a0[...], b0[...], TN) + dot(a1[...], b1[...], TN)
    split_rows(share, at_ref, block, scratch_ref, keep_ref, send_ref)


def weight_grads(share, parity, left, right, spare):
    rows, width = left[0].shape
    span = right[0].shape[1] // width
    column = pl.BlockSpec((rows, width), lambda i, at: (0, i))
    plain = whole((rows, width))
    out = shape_of((width // 2, span * width + spare), BF)
    return pl.pallas_call(
        functools.partial(weight_kernel, share),
        grid_spec=pltpu.PrefetchScalarGridSpec(
            num_scalar_prefetch=1,
            grid=(span,),
            in_specs=[plain, plain, column, column],
            out_specs=[pl.BlockSpec((width // 2, width), lambda i, at: (0, i))] * 2,
            scratch_shapes=[pltpu.VMEM((width, width), F32)],
        ),
        out_shape=[out, out],
        compiler_params=params(),
        cost_estimate=cost(4),
        name="weight_grads",
    )(parity, *left, *right)


def proj_kernel(share, at_ref, low_ref, o_ref, kept_ref, sent_ref, keep_ref, send_ref, scratch_ref):
    block = dot(low_ref[...], o_ref[...], TN)
    split_rows(share, at_ref, block, scratch_ref, keep_ref, send_ref)


def proj_grads(share, parity, low, o, keep, send):
    width = o.shape[1]
    last = keep.shape[1] // width - 1
    return pl.pallas_call(
        functools.partial(proj_kernel, share),
        grid_spec=pltpu.PrefetchScalarGridSpec(
            num_scalar_prefetch=1,
            grid=(1,),
            in_specs=[whole(low.shape), whole(o.shape)] + [pl.BlockSpec(memory_space=pl.ANY)] * 2,
            out_specs=[pl.BlockSpec((width // 2, width), lambda i, at: (0, last))] * 2,
            scratch_shapes=[pltpu.VMEM((width, width), F32)],
        ),
        out_shape=[shape_of(keep.shape, BF)] * 2,
        input_output_aliases={3: 0, 4: 1},
        compiler_params=params(),
        cost_estimate=cost(2),
        name="proj_grads",
    )(parity, low, o, keep, send)


def input_back_kernel(places, packed_ref, w_ref, x_ref, dmid_ref, norm_ref, out_ref, flat_ref):
    rows, _ = x_ref.shape
    half = rows // 2
    for h, place in enumerate(places):
        at = 3 * HD * h
        piece = packed_ref[place]
        flat_ref[:, at : at + 2 * HD] = piece[:rows]
        flat_ref[:half, at + 2 * HD : at + 3 * HD] = piece[rows:, :HD]
        flat_ref[half:, at + 2 * HD : at + 3 * HD] = piece[rows:, HD:]
    dh = dot(flat_ref[...], w_ref[...], NT)
    unit, scale = normalize(x_ref[...].astype(F32))
    out_ref[...] = (dmid_ref[...] + normalize_back(dh * norm_ref[0:1, :], unit, scale)).astype(BF)


def input_back(places, packed, weights, x, dmid, norms):
    rows, width = x.shape
    return pl.pallas_call(
        functools.partial(input_back_kernel, places),
        grid=(1,),
        in_specs=[whole(a.shape) for a in (packed, weights, x, dmid, norms)],
        out_specs=whole((rows, width)),
        out_shape=shape_of((rows, width), BF),
        scratch_shapes=[pltpu.VMEM((rows, 3 * HD * len(places)), BF)],
        compiler_params=params(),
        cost_estimate=cost(5),
        name="input_back",
    )(packed, weights, x, dmid, norms)


def adam_step(master, first_state, second_state, grad_term, step_rate, weight_decay):
    first_new = BETA_ONE * first_state + (1.0 - BETA_ONE) * grad_term
    second_new = BETA_TWO * second_state + (1.0 - BETA_TWO) * grad_term * grad_term
    first_hat = first_new / (1.0 - BETA_ONE**STEP)
    second_hat = second_new / (1.0 - BETA_TWO**STEP)
    master_new = master - step_rate * (
        first_hat / (jnp.sqrt(second_hat) + ADAM_EPS) + weight_decay * master
    )
    return (first_new, second_new, master_new)


def shards(
    tokens,
    cotangent,
    seq_lengths,
    slot_token,
    w_qkv,
    w_proj,
    w_inner,
    w_outer,
    norm_gains,
    norm_biases,
    qkv_first,
    qkv_second,
    proj_first,
    proj_second,
    inner_first,
    inner_second,
    outer_first,
    outer_second,
    norm_first,
    norm_second,
):
    side = lax.axis_index("ha")
    group = lax.axis_size("pb") * lax.axis_size("ka")
    rows, width = tokens.shape[1:]
    total = rows * group
    w_rows = w_qkv.shape[0]
    half_width = w_qkv.shape[2]
    heads = 2 * half_width // HD
    hidden_half = w_inner.shape[1]
    places = head_places(group, heads)
    head_at = [0] * group
    for h, place in enumerate(places):
        head_at[place] = h
    block = min(SCORE_BLOCK, total)

    def swap(a):
        return lax.ppermute(a, "ha", [(0, 1), (1, 0)])

    def ordered(own, other):
        return jnp.where(side == 0, own, other), jnp.where(side == 0, other, own)

    def own_micro(a):
        return lax.dynamic_index_in_dim(a, side, 0, False)

    def other_micro(a):
        return lax.dynamic_index_in_dim(a, 1 - side, 0, False)

    x = own_micro(tokens)
    along_z, along_ka = lax.axis_size("pb"), lax.axis_size("ka")
    stepped = along_z == 4 and along_ka == 4

    def flip(a, axis, size, bit):
        return lax.ppermute(a, axis, [(i, i ^ bit) for i in range(size)])

    if stepped:

        def z_flip(a, bit):
            return flip(a, "pb", along_z, bit)

        def x_flip(a):
            return flip(a, "ka", along_ka, 2)

        def c_flip(a):
            return flip(a, "ka", along_ka, 1)

        own = x[None]
        near, far, own_x, own_c = z_flip(own, 1), z_flip(own, 2), x_flip(own), c_flip(own)
    else:
        x_full = lax.all_gather(x, PLANE, axis=0, tiled=True)
    mine = jnp.concatenate(
        [w_qkv.astype(BF).reshape(w_rows, 3 * half_width), w_proj.astype(BF).T], axis=1
    )
    tok_row = own_micro(slot_token).reshape(1, total)
    mine_other, slot_row = swap(mine), slots_of_tokens(tok_row)
    if stepped:
        near, far, own_x, own_c, mine_other, slot_row = tie(
            near, far, own_x, own_c, mine_other, slot_row
        )
        mid_z = jnp.concatenate([near, far])
        last_z, mid_x, mid_c, own_xc = z_flip(far, 1), x_flip(mid_z), c_flip(mid_z), c_flip(own_x)
    low_half, high_half = ordered(mine, mine_other)
    qkv_rows = jnp.concatenate(
        [
            a[:, : 3 * half_width].reshape(w_rows, 3, heads // 2, HD).swapaxes(1, 2)
            for a in (low_half, high_half)
        ],
        axis=1,
    ).reshape(w_rows, heads, 3 * HD)
    proj_rows = jnp.concatenate(
        [a[:, 3 * half_width :] for a in (low_half, high_half)], axis=1
    )
    norm_master = jnp.concatenate([norm_gains, norm_biases], axis=0)
    head_rows = jnp.stack([qkv_rows[:, head_at[d]] for d in range(group)], axis=0)
    head_rows = jnp.concatenate(
        [
            head_rows,
            jnp.broadcast_to(norm_master.astype(BF).T[None], (group, w_rows, 4)),
            jnp.zeros((group, w_rows, HD - 4), BF),
        ],
        axis=2,
    )
    head_w = lax.all_to_all(head_rows, PLANE, 0, 0, tiled=True)
    if stepped:
        last_z, mid_x, mid_c, own_xc, head_w = tie(last_z, mid_x, mid_c, own_xc, head_w)
        last_x, last_c, mid_xc = x_flip(last_z), c_flip(last_z), c_flip(mid_x)
    else:
        head_w, slot_row = tie(head_w, slot_row)
    head_w = head_w.reshape(width, 4 * HD)
    norms = head_w[:, 3 * HD : 3 * HD + 4].astype(F32).T
    head_w = head_w[:, : 3 * HD].T
    main_rows = jnp.concatenate(
        [
            w_inner.astype(BF),
            w_outer.astype(BF).T,
            proj_rows,
        ],
        axis=1,
    )
    if stepped:
        main_rows, mid_x = tie(main_rows, mid_x)
    else:
        main_rows, x_full = tie(main_rows, x_full)
    main_w = lax.all_gather(main_rows, PLANE, axis=0, tiled=True)
    proj_at = 2 * hidden_half // width

    ends = jnp.cumsum(own_micro(seq_lengths))
    starts = jnp.arange(total // block, dtype=jnp.int32) * block
    first_block = jnp.max(jnp.where(ends[None] <= starts[:, None], ends[None], 0), axis=1) // block
    last_block = jnp.min(jnp.where(ends[None] > starts[:, None], ends[None], total), axis=1) // block
    first_block = first_block.astype(jnp.int32)
    last_block = last_block.astype(jnp.int32)

    if stepped:
        z, xc = lax.axis_index("pb"), lax.axis_index("ka")
        at = jnp.stack([z, 0 * z, xc // 2, xc % 2]).astype(jnp.int32)
        groups = ((own, own_x, own_c, own_xc), (mid_z, mid_x, mid_c, mid_xc))
        buffers = qkv_of_piece(at, groups, head_w, norms, total, ())
        last_x, last_c, *buffers = tie(last_x, last_c, *buffers)
        at = jnp.stack([z, 0 * z + 3, xc // 2, xc % 2]).astype(jnp.int32)
        groups = ((last_z, last_x, last_c, c_flip(last_x)),)
        buffers = qkv_of_piece(at, groups, head_w, norms, total, buffers)
        unit, qkv = buffers
    else:
        unit, qkv = qkv_of_head(x_full, head_w, norms)
    q, qt, k, v, vt = sort_qkv(tok_row, qkv)
    o, o_low, lse = attend(first_block, qt, k, vt, block)
    late_rows, o_low = tie(qkv_rows.reshape(w_rows, -1), o_low)
    late_w = lax.all_gather(late_rows, PLANE, axis=0, tiled=True)
    o_packed = lax.all_to_all(slots_out(slot_row, o_low, group), PLANE, 0, 0, tiled=True)
    mid, h_own, o_own = middle(places, x, o_packed, main_w, proj_at, norms)
    h_other = swap(h_own)
    dy_own, dy_other = own_micro(cotangent), other_micro(cotangent)
    act_own, dpre_own, dh_own = hidden(h_own, dy_own, main_w, hidden_half, F32)
    h_other, dh_own = tie(h_other, dh_own)
    act_other, dpre_other, dh_send = hidden(h_other, dy_other, main_w, hidden_half, BF)
    dh_got = swap(dh_send)
    xc = lax.axis_index("ka")
    parity = (xc % 2).reshape(1).astype(jnp.int32)
    share = w_rows if stepped else 0
    inner_halves = weight_grads(share, parity, (h_own, h_other), (dpre_own, dpre_other), 0)
    outer_halves = weight_grads(share, parity, (dy_own, dy_other), (act_own, act_other), width)

    def pair_sum(halves, at):
        shape = (along_z, along_ka // 2, w_rows, halves[0].shape[1])
        parts = [lax.dynamic_index_in_dim(a.reshape(shape), at, 1, False) for a in halves]
        return parts[0].astype(F32) + parts[1].astype(F32)

    def scattered(halves, got):
        rest = (pair_sum(halves, xc // 2) + got.astype(F32)).astype(BF)
        return rest.reshape(-1, rest.shape[-1])

    if stepped:
        inner_halves = (inner_halves[0], c_flip(inner_halves[1]))
        inner_send = pair_sum(inner_halves, 1 - xc // 2).astype(BF)
        dh_got, inner_send, *outer_halves = tie(dh_got, inner_send, *outer_halves)
        inner_got = x_flip(inner_send)
    else:
        dh_got, *outer_halves = tie(dh_got, *outer_halves)

    dmid, dmid_low, g_packed, sums_two = middle_back(
        places, group, dh_own, dh_got, dy_own, mid, norms, main_w, proj_at
    )
    outer_halves = proj_grads(share, parity, dmid_low, o_own, *outer_halves)
    g_packed = lax.all_to_all(g_packed, PLANE, 0, 0, tiled=True)
    out_own, out_send = layer_terms(act_own, act_other, main_w)
    g_packed, out_own, out_send = tie(g_packed, out_own, out_send)
    if stepped:
        outer_halves = (outer_halves[0], c_flip(outer_halves[1]))
        outer_send = pair_sum(outer_halves, 1 - xc // 2).astype(BF)
        inner_got, outer_send = tie(inner_got, outer_send)
        inner_rest = scattered(inner_halves, inner_got)
        outer_got = x_flip(outer_send)
    else:
        inner_sum = lax.psum_scatter(
            jnp.concatenate(inner_halves), PLANE, scatter_dimension=0, tiled=True
        )
    g, gt, delta = sort_grad(tok_row, g_packed, o)
    if stepped:
        g, inner_rest = tie(g, inner_rest)
        inner_sum = lax.psum_scatter(inner_rest, "pb", scatter_dimension=0, tiled=True)
    dqkv = attend_back(last_block, q, qt, k, v, g, gt, lse, delta, block)
    packed, dqkv_low = grads_out(slot_row, dqkv, group)
    if stepped:
        outer_rest = scattered(outer_halves, outer_got)
        dqkv_low, outer_rest, late_w, out_send, out_own, inner_sum = tie(
            dqkv_low, outer_rest, late_w, out_send, out_own, inner_sum
        )
    else:
        outer_sum = lax.psum_scatter(
            jnp.concatenate(outer_halves), PLANE, scatter_dimension=0, tiled=True
        )
    dqkv_own = lax.all_to_all(packed, PLANE, 0, 0, tiled=True)
    out_got = swap(out_send)
    layer_own = (mid + out_own + out_got.astype(F32)).astype(BF)
    layer_out = jnp.stack(ordered(layer_own, swap(layer_own)))

    head_grad = head_weight_grad(dqkv_low, unit, head_w, norms, sums_two)
    head_grad = head_grad.reshape(group, 2, w_rows // 2, 4 * HD)
    keep, send = ordered(head_grad[:, 0], head_grad[:, 1])
    keep = (keep.astype(F32) + swap(send).astype(F32)).astype(BF)
    keep, dqkv_own, layer_out = tie(keep, dqkv_own, layer_out)
    if stepped:
        dqkv_own, outer_rest = tie(dqkv_own, outer_rest)
        outer_sum = lax.psum_scatter(outer_rest, "pb", scatter_dimension=0, tiled=True)
    head_grad = lax.all_to_all(keep, PLANE, 0, 0, tiled=True)
    input_low = input_back(places, dqkv_own, late_w, x, dmid, norms)
    head_grad, outer_sum = tie(head_grad, outer_sum)
    input_grad = jnp.stack(ordered(input_low, swap(input_low))).astype(F32)

    norm_parts = head_grad[:, :, 3 * HD : 3 * HD + 8].astype(F32)
    norm_parts = norm_parts[:, :, :4] + norm_parts[:, :, 4:]
    first_sums = sum(norm_parts[place] for place in places)
    second_sums = jnp.sum(norm_parts, axis=0)
    norm_grad = jnp.stack(
        [first_sums[:, 0], second_sums[:, 1], first_sums[:, 2], second_sums[:, 3]]
    )
    norm_grad = jnp.concatenate(ordered(norm_grad, swap(norm_grad)), axis=1)
    qkv_part = jnp.stack([head_grad[place, :, : 3 * HD] for place in places], axis=1)
    qkv_part = qkv_part.reshape(w_rows // 2, 2, heads // 2, 3, HD)
    keep, send = ordered(qkv_part[:, 0], qkv_part[:, 1])
    qkv_grad = jnp.concatenate(ordered(keep, swap(send)), axis=0).astype(F32)
    qkv_grad = qkv_grad.swapaxes(1, 2).reshape(w_rows, 3, half_width)
    inner_grad = inner_sum.astype(F32)
    outer_grad = outer_sum[:, :hidden_half].astype(F32).T
    proj_part = outer_sum[:, hidden_half:]
    keep, send = ordered(proj_part[:, :half_width], proj_part[:, half_width:])
    proj_grad = (keep.astype(F32) + swap(send).astype(F32)).T

    qkv_out = adam_step(w_qkv, qkv_first, qkv_second, qkv_grad / MICRO, RATE_MATRIX, DECAY_RATE)
    proj_out = adam_step(w_proj, proj_first, proj_second, proj_grad / MICRO, RATE_PROJ, DECAY_RATE)
    inner_out = adam_step(
        w_inner, inner_first, inner_second, inner_grad / MICRO, RATE_MATRIX, DECAY_RATE
    )
    outer_out = adam_step(
        w_outer, outer_first, outer_second, outer_grad / MICRO, RATE_MATRIX, DECAY_RATE
    )
    norm_grad = norm_grad / MICRO
    norm_out = adam_step(norm_master, norm_first, norm_second, norm_grad, RATE_NORM, 0.0)
    norm_two_grad = jnp.stack([norm_grad[1], norm_grad[3]])
    return (
        layer_out,
        input_grad,
        *qkv_out,
        *proj_out,
        *inner_out,
        *outer_out,
        *norm_out,
        norm_two_grad,
    )


def solution(mesh):
    tok = P(None, PLANE, None)
    qkv = P(PLANE, None, "ha")
    down = P("ha", PLANE)
    inner = P(PLANE, "ha")
    norm = P(None, PLANE)
    in_specs = (
        (tok, tok, P(), P(), qkv, down, inner, down, norm, norm)
        + (qkv, qkv, down, down, inner, inner, down, down, norm, norm)
    )
    out_specs = (
        (tok, tok, qkv, qkv, qkv, down, down, down)
        + (inner, inner, inner, down, down, down, norm, norm, norm, norm)
    )
    return jax.shard_map(shards, mesh=mesh, in_specs=in_specs, out_specs=out_specs, check_vma=False)
```

```python
import functools

import jax
import jax.numpy as jnp
from jax import lax
from jax.experimental import pallas as pl
from jax.experimental.pallas import tpu as pltpu
from jax.sharding import PartitionSpec as P

HD = 64
MICRO = 2
STEP = 8
NORM_EPS = 1e-05
BETA_ONE = 0.9
BETA_TWO = 0.95
ADAM_EPS = 1e-08
DECAY_RATE = 0.1
RATE_MATRIX = 0.02
RATE_PROJ = 0.6
RATE_NORM = 0.1
BF = jnp.bfloat16
F32 = jnp.float32
PLANE = ("pb", "ka")
VMEM_LIMIT = 60 * 1024 * 1024
SCORE_BLOCK = 512
SHORT = 4096
STRAIGHT = 4
NT = (((1,), (1,)), ((), ()))
NN = (((1,), (0,)), ((), ()))
TN = (((0,), (0,)), ((), ()))


def dot(a, b, dims=NN):
    return lax.dot_general(a, b, dims, preferred_element_type=F32)


def params(steps=1):
    return pltpu.CompilerParams(
        dimension_semantics=("arbitrary",) * steps, vmem_limit_bytes=VMEM_LIMIT
    )


def cost(us):
    return pl.CostEstimate(flops=int(us * 2e8), bytes_accessed=int(us * 1e6), transcendentals=0)


def tie(*arrays):
    return lax.optimization_barrier(arrays)


def whole(shape):
    return pl.BlockSpec(shape, lambda *_: (0,) * len(shape))


def shape_of(shape, dtype):
    return jax.ShapeDtypeStruct(shape, dtype)


def head_places(group, heads):
    return tuple(h * group // heads for h in range(heads))


def normalize(x):
    center = x - jnp.mean(x, axis=-1, keepdims=True)
    spread = jnp.mean(center * center, axis=-1, keepdims=True)
    scale = lax.rsqrt(spread + NORM_EPS)
    return center * scale, scale


def normalize_back(grad, unit, scale):
    return scale * (
        grad
        - jnp.mean(grad, axis=-1, keepdims=True)
        - unit * jnp.mean(grad * unit, axis=-1, keepdims=True)
    )


def low_match(ids):
    low = lax.bitwise_and(ids, 255).astype(F32).astype(BF)
    line = lax.broadcasted_iota(jnp.int32, (256, 1), 0).astype(F32).astype(BF)
    return jnp.where(low == line, jnp.ones((), BF), jnp.zeros((), BF))


def moved(ids_ref, match_ref, source_ref, stack_ref, first):
    features = source_ref.shape[0]
    chunk = stack_ref.shape[1]
    total = None
    for part in range(source_ref.shape[1] // chunk):
        cut = slice(part * chunk, (part + 1) * chunk)
        high = lax.shift_right_logical(ids_ref[:, cut], 8)
        source = source_ref[:, cut]
        for block in range(stack_ref.shape[0] // features):
            stack_ref[block * features : (block + 1) * features, :] = jnp.where(
                high == first + block, source, jnp.zeros((), BF)
            )
        piece = dot(stack_ref[...], match_ref[:, cut], NT)
        total = piece if total is None else total + piece
    return total


def sort_block(total):
    return total if total <= SHORT else 1024


def stack_shape(features, columns, total):
    return pltpu.VMEM((features * columns // 256, min(3072, total)), BF)


def place_kernel(tok_ref, out_ref):
    total = tok_ref.shape[1]
    count = total // 256
    ids = tok_ref[...]
    high = lax.shift_right_logical(ids, 8)
    slot = lax.broadcasted_iota(jnp.int32, (1, total), 1)
    rows = lax.broadcasted_iota(jnp.int32, (count, 1), 0)
    match = low_match(ids)

    def part(values):
        picked = jnp.where(high == rows, values.astype(F32), 0.0).astype(BF)
        return dot(picked, match, NT)

    found = part(lax.shift_right_logical(slot, 8)) * 256.0 + part(lax.bitwise_and(slot, 255))
    found = found.astype(jnp.int32)
    for a in range(count):
        out_ref[:, a * 256 : (a + 1) * 256] = found[a : a + 1]


def slots_of_tokens(tok_row):
    return pl.pallas_call(
        place_kernel,
        grid=(1,),
        in_specs=[whole(tok_row.shape)],
        out_specs=whole(tok_row.shape),
        out_shape=shape_of(tok_row.shape, jnp.int32),
        compiler_params=params(),
        cost_estimate=cost(2),
        name="slots_of_tokens",
    )(tok_row)


def qkv_kernel(x_ref, w_ref, norm_ref, unit_ref, qkv_ref):
    unit, _ = normalize(x_ref[...].astype(F32))
    h = (unit * norm_ref[0:1, :] + norm_ref[2:3, :]).astype(BF)
    unit_ref[...] = unit.astype(BF)
    qkv_ref[...] = dot(w_ref[...], h, NT).astype(BF)


def qkv_piece_kernel(counts, at_ref, *refs):
    sources = refs[: 4 * len(counts)]
    w_ref, norm_ref = refs[4 * len(counts) :][:2]
    unit_ref, qkv_ref, x_ref = refs[-3:]
    rows = x_ref.shape[0] // 2
    even = at_ref[3] == 0
    slot = 0
    for group, count in enumerate(counts):
        for place in range(count):
            for side in range(2):

                @pl.when((pl.program_id(0) == slot) & (pl.program_id(1) == side))
                def _():
                    own = sources[4 * group + side][place]
                    other = sources[4 * group + 2 + side][place]
                    x_ref[:rows, :] = jnp.where(even, own, other)
                    x_ref[rows:, :] = jnp.where(even, other, own)

            slot += 1
    unit, _ = normalize(x_ref[...].astype(F32))
    h = (unit * norm_ref[0:1, :] + norm_ref[2:3, :]).astype(BF)
    unit_ref[...] = unit.astype(BF)
    qkv_ref[...] = dot(w_ref[...], h, NT).astype(BF)


def qkv_of_piece(at, groups, head_w, norms, total, buffers):
    counts = tuple(group[0].shape[0] for group in groups)
    pieces = [a for group in groups for a in group]
    _, rows, width = pieces[0].shape
    kept = [pl.BlockSpec(memory_space=pl.ANY)] * len(buffers)
    first = 1 + len(pieces) + 2

    def place(i, j, at):
        return (at[0] ^ (at[1] + i)) * 2 + (at[2] ^ j)

    return pl.pallas_call(
        functools.partial(qkv_piece_kernel, counts),
        grid_spec=pltpu.PrefetchScalarGridSpec(
            num_scalar_prefetch=1,
            grid=(sum(counts), 2),
            in_specs=[whole(a.shape) for a in (*pieces, head_w, norms)] + kept,
            out_specs=[
                pl.BlockSpec((2 * rows, width), lambda i, j, at: (place(i, j, at), 0)),
                pl.BlockSpec((head_w.shape[0], 2 * rows), lambda i, j, at: (0, place(i, j, at))),
            ],
            scratch_shapes=[pltpu.VMEM((2 * rows, width), BF)],
        ),
        out_shape=[shape_of((total, width), BF), shape_of((head_w.shape[0], total), BF)],
        input_output_aliases={first: 0, first + 1: 1} if buffers else {},
        compiler_params=params(2),
        cost_estimate=cost(3 * sum(counts)),
        name="qkv_piece",
    )(at, *pieces, head_w, norms, *buffers)


def qkv_of_head(x_full, head_w, norms):
    rows, width = x_full.shape
    block = min(512, rows)
    return pl.pallas_call(
        qkv_kernel,
        grid=(rows // block,),
        in_specs=[
            pl.BlockSpec((block, width), lambda i: (i, 0)),
            whole(head_w.shape),
            whole(norms.shape),
        ],
        out_specs=[
            pl.BlockSpec((block, width), lambda i: (i, 0)),
            pl.BlockSpec((head_w.shape[0], block), lambda i: (0, i)),
        ],
        out_shape=[shape_of((rows, width), BF), shape_of((head_w.shape[0], rows), BF)],
        compiler_params=params(),
        cost_estimate=cost(8),
        name="qkv_head",
    )(x_full, head_w, norms)


def sort_kernel(tok_ref, qkv_ref, q_ref, qt_ref, k_ref, v_ref, vt_ref, match_ref, stack_ref):
    @pl.when(pl.program_id(0) == 0)
    def _():
        match_ref[...] = low_match(tok_ref[...])

    count = k_ref.shape[0] // 256
    found = moved(tok_ref, match_ref, qkv_ref, stack_ref, pl.program_id(0) * count)
    for part in range(count):
        cut = slice(part * 256, (part + 1) * 256)
        at = 3 * HD * part
        query = found[at : at + HD] * float(HD) ** -0.5
        value = found[at + 2 * HD : at + 3 * HD]
        qt_ref[:, cut] = query.astype(BF)
        q_ref[cut, :] = query.T.astype(BF)
        k_ref[cut, :] = found[at + HD : at + 2 * HD].T.astype(BF)
        v_ref[cut, :] = value.T.astype(BF)
        vt_ref[:, cut] = value.astype(BF)


def sort_qkv(tok_row, qkv):
    rows = qkv.shape[1]
    block = sort_block(rows)
    narrow = (pl.BlockSpec((block, HD), lambda i: (i, 0)), shape_of((rows, HD), BF))
    wide = (pl.BlockSpec((HD, block), lambda i: (0, i)), shape_of((HD, rows), BF))
    outs = (narrow, wide, narrow, narrow, wide)
    return pl.pallas_call(
        sort_kernel,
        grid=(rows // block,),
        in_specs=[whole(tok_row.shape), whole(qkv.shape)],
        out_specs=[spec for spec, _ in outs],
        out_shape=[shape for _, shape in outs],
        scratch_shapes=[pltpu.VMEM((256, rows), BF), stack_shape(3 * HD, block, rows)],
        compiler_params=params(),
        cost_estimate=cost(5),
        name="sort_qkv",
    )(tok_row, qkv)


def causal(block):
    return lax.broadcasted_iota(jnp.int32, (block, block), 0) <= lax.broadcasted_iota(
        jnp.int32, (block, block), 1
    )


def forward_kernel(first_ref, qt_ref, k_ref, vt_ref, o_ref, low_ref, lse_ref):
    block = qt_ref.shape[1]
    index = pl.program_id(0)
    query = qt_ref[...]

    def step(key_block, state, diagonal):
        top, total, acc = state
        at = pl.multiple_of(key_block * block, block)
        scores = dot(k_ref[pl.ds(at, block), :], query)
        square = scores * scores + 1.0
        inverse = lax.rsqrt(square)
        radius = square * inverse
        if diagonal:
            radius = jnp.where(causal(block), radius, -1e30)
        new_top = jnp.maximum(top, jnp.max(radius, axis=0, keepdims=True))
        weights = jnp.exp(radius - new_top)
        shrink = jnp.exp(top - new_top)
        signed = (scores * inverse * weights).astype(BF)
        acc = acc * shrink + dot(vt_ref[:, pl.ds(at, block)], signed)
        total = total * shrink + jnp.sum(weights, axis=0, keepdims=True)
        return (new_top, total, acc)

    def finish(state):
        top, total, acc = state
        out = acc * (1.0 / total)
        o_ref[...] = out
        low_ref[...] = out.astype(BF)
        lse_ref[...] = top + jnp.log(total)

    start = (
        jnp.zeros((1, block), F32),
        jnp.zeros((1, block), F32),
        jnp.zeros((HD, block), F32),
    )
    earlier = index - first_ref[index]
    for count in range(STRAIGHT):

        @pl.when(earlier == count)
        def _():
            state = step(index, start, True)
            for back in range(1, count + 1):
                state = step(index - back, state, False)
            finish(state)

    @pl.when(earlier >= STRAIGHT)
    def _():
        state = lax.fori_loop(first_ref[index], index, lambda j, s: step(j, s, False), start)
        finish(step(index, state, True))


def attend(first_block, qt, k, vt, block):
    rows = k.shape[0]
    return pl.pallas_call(
        forward_kernel,
        grid_spec=pltpu.PrefetchScalarGridSpec(
            num_scalar_prefetch=1,
            grid=(rows // block,),
            in_specs=[
                pl.BlockSpec((HD, block), lambda i, *_: (0, i)),
                whole(k.shape),
                whole(vt.shape),
            ],
            out_specs=[
                pl.BlockSpec((HD, block), lambda i, *_: (0, i)),
                pl.BlockSpec((HD, block), lambda i, *_: (0, i)),
                pl.BlockSpec((1, block), lambda i, *_: (0, i)),
            ],
        ),
        out_shape=[shape_of((HD, rows), F32), shape_of((HD, rows), BF), shape_of((1, rows), F32)],
        compiler_params=params(),
        cost_estimate=cost(13),
        name="attend_fwd",
    )(first_block, qt, k, vt)


def slots_out_kernel(rows, slot_ref, low_ref, out_ref, match_ref, stack_ref):
    half = rows // 2

    @pl.when(pl.program_id(0) == 0)
    def _():
        match_ref[...] = low_match(slot_ref[...])

    owners = out_ref.shape[0]
    count = owners * rows // 256
    found = moved(slot_ref, match_ref, low_ref, stack_ref, pl.program_id(0) * count)
    found = jnp.concatenate([found[p * HD : (p + 1) * HD].T for p in range(count)], axis=0)
    found = found.astype(BF)
    for d in range(owners):
        at = d * rows
        out_ref[d] = jnp.concatenate([found[at : at + half], found[at + half : at + rows]], axis=1)


def slots_out(slot_row, low, group):
    total = slot_row.shape[1]
    rows = total // group
    count = owners_per_step(group, rows)
    return pl.pallas_call(
        functools.partial(slots_out_kernel, rows),
        grid=(group // count,),
        in_specs=[whole(slot_row.shape), whole(low.shape)],
        out_specs=pl.BlockSpec((count, rows // 2, 2 * HD), lambda i: (i, 0, 0)),
        out_shape=shape_of((group, rows // 2, 2 * HD), BF),
        scratch_shapes=[pltpu.VMEM((256, total), BF), stack_shape(HD, count * rows, total)],
        compiler_params=params(),
        cost_estimate=cost(3),
        name="slots_out",
    )(slot_row, low)


def owners_per_step(group, rows, most=16):
    for count in (16, 8, 4, 2, 1):
        if count > (most if group * rows <= SHORT else 4):
            continue
        if group % count == 0 and count * rows % 256 == 0:
            return count
    return group


def sort_grad_kernel(
    tok_ref, packed_ref, o_ref, g_ref, gt_ref, delta_ref, slots_ref, match_ref, stack_ref
):
    group, half, _ = packed_ref.shape

    @pl.when(pl.program_id(0) == 0)
    def _():
        match_ref[...] = low_match(tok_ref[...])
        for d in range(group):
            piece = packed_ref[d].astype(F32).T.astype(BF)
            slots_ref[:, 2 * d * half : (2 * d + 1) * half] = piece[:HD]
            slots_ref[:, (2 * d + 1) * half : (2 * d + 2) * half] = piece[HD:]

    count = g_ref.shape[0] // 256
    found = moved(tok_ref, match_ref, slots_ref, stack_ref, pl.program_id(0) * count)
    for part in range(count):
        cut = slice(part * 256, (part + 1) * 256)
        grad = found[part * HD : (part + 1) * HD]
        gt_ref[:, cut] = grad.astype(BF)
        g_ref[cut, :] = grad.T.astype(BF)
        delta_ref[:, cut] = jnp.sum(grad * o_ref[:, cut], axis=0, keepdims=True)


def sort_grad(tok_row, packed, o):
    rows = o.shape[1]
    block = sort_block(rows)
    wide = pl.BlockSpec((HD, block), lambda i: (0, i))
    return pl.pallas_call(
        sort_grad_kernel,
        grid=(rows // block,),
        in_specs=[whole(tok_row.shape), whole(packed.shape), wide],
        out_specs=[
            pl.BlockSpec((block, HD), lambda i: (i, 0)),
            wide,
            pl.BlockSpec((1, block), lambda i: (0, i)),
        ],
        out_shape=[shape_of((rows, HD), BF), shape_of((HD, rows), BF), shape_of((1, rows), F32)],
        scratch_shapes=[
            pltpu.VMEM((HD, rows), BF),
            pltpu.VMEM((256, rows), BF),
            stack_shape(HD, block, rows),
        ],
        compiler_params=params(),
        cost_estimate=cost(4),
        name="sort_grad",
    )(tok_row, packed, o)


def backward_kernel(
    last_ref, q_ref, qt_ref, k_ref, v_ref, g_ref, gt_ref, lse_ref, delta_ref, out_ref, dq_ref, dk_ref, dv_ref
):
    block = k_ref.shape[0]
    index = pl.program_id(0)

    @pl.when(index == 0)
    def _():
        dq_ref[...] = jnp.zeros_like(dq_ref)

    key = k_ref[...]
    key_t = key.astype(F32).T.astype(BF)
    value = v_ref[...]

    def step(query_block, diagonal):
        at = pl.multiple_of(query_block * block, block)
        scores = dot(key, qt_ref[:, pl.ds(at, block)])
        square = scores * scores + 1.0
        inverse = lax.rsqrt(square)
        shifted = square * inverse - lse_ref[:, pl.ds(at, block)]
        if diagonal:
            shifted = jnp.where(causal(block), shifted, -1e30)
        weights = jnp.exp(shifted)
        slope = scores * inverse
        along = dot(value, gt_ref[:, pl.ds(at, block)])
        bend = 1.0 + inverse * inverse * (inverse - 1.0)
        score_grad = weights * (bend * along - slope * delta_ref[:, pl.ds(at, block)])
        signed = (slope * weights).astype(BF)
        low_grad = score_grad.astype(BF)
        dv = dot(signed, g_ref[pl.ds(at, block), :])
        dk = dot(low_grad, q_ref[pl.ds(at, block), :])
        dq_ref[:, pl.ds(at, block)] += dot(key_t, low_grad)
        return dk, dv

    def finish(dk, dv):
        at = pl.multiple_of(index * block, block)
        out_ref[:HD] = (dq_ref[:, pl.ds(at, block)] * float(HD) ** -0.5).astype(BF)
        out_ref[HD : 2 * HD] = dk.T.astype(BF)
        out_ref[2 * HD :] = dv.T.astype(BF)

    later = last_ref[index] - index
    for count in range(1, STRAIGHT + 1):

        @pl.when(later == count)
        def _():
            dk, dv = step(index, True)
            for ahead in range(1, count):
                dk_more, dv_more = step(index + ahead, False)
                dk, dv = dk + dk_more, dv + dv_more
            finish(dk, dv)

    @pl.when(later > STRAIGHT)
    def _():
        dk_ref[...], dv_ref[...] = step(index, True)

        def body(query_block, carry):
            dk_more, dv_more = step(query_block, False)
            dk_ref[...] += dk_more
            dv_ref[...] += dv_more
            return carry

        lax.fori_loop(index + 1, last_ref[index], body, 0)
        finish(dk_ref[...], dv_ref[...])


def attend_back(last_block, q, qt, k, v, g, gt, lse, delta, block):
    rows = q.shape[0]
    return pl.pallas_call(
        backward_kernel,
        grid_spec=pltpu.PrefetchScalarGridSpec(
            num_scalar_prefetch=1,
            grid=(rows // block,),
            in_specs=[
                whole(q.shape),
                whole(qt.shape),
                pl.BlockSpec((block, HD), lambda i, *_: (i, 0)),
                pl.BlockSpec((block, HD), lambda i, *_: (i, 0)),
                whole(g.shape),
                whole(gt.shape),
                whole(lse.shape),
                whole(delta.shape),
            ],
            out_specs=pl.BlockSpec((3 * HD, block), lambda i, *_: (0, i)),
            scratch_shapes=[
                pltpu.VMEM((HD, rows), F32),
                pltpu.VMEM((block, HD), F32),
                pltpu.VMEM((block, HD), F32),
            ],
        ),
        out_shape=shape_of((3 * HD, rows), BF),
        compiler_params=params(),
        cost_estimate=cost(19),
        name="attend_bwd",
    )(last_block, q, qt, k, v, g, gt, lse, delta)


def head_results(acc, column, w_ref, norm_ref, sums_ref):
    weights = w_ref[...].astype(F32)
    grad = acc * norm_ref[0:1, :] + column * norm_ref[2:3, :]
    sums = jnp.concatenate(
        [
            jnp.sum(weights * acc, axis=0, keepdims=True),
            sums_ref[0:1, :],
            jnp.sum(weights * column, axis=0, keepdims=True),
            sums_ref[1:2, :],
        ],
        axis=0,
    )
    top = sums.astype(BF).astype(F32)
    rest = jnp.concatenate([top, sums - top, jnp.zeros((HD - 8, sums.shape[1]), F32)], axis=0)
    return jnp.concatenate([grad, rest], axis=0).T.astype(BF)


def grads_out_kernel(rows, slot_ref, grad_ref, out_ref, low_ref, match_ref, stack_ref):
    half = rows // 2
    step = pl.program_id(0)

    @pl.when(step == 0)
    def _():
        match_ref[...] = low_match(slot_ref[...])

    count = out_ref.shape[0]
    parts = count * rows // 256
    found = moved(slot_ref, match_ref, grad_ref, stack_ref, step * parts)
    turned = []
    for p in range(parts):
        piece = found[3 * HD * p : 3 * HD * (p + 1)]
        low_ref[:, p * 256 : (p + 1) * 256] = piece.astype(BF)
        turned.append(piece.T)
    turned = jnp.concatenate(turned, axis=0).astype(BF)
    for d in range(count):
        at = d * rows
        out_ref[d, :rows, :] = turned[at : at + rows, : 2 * HD]
        out_ref[d, rows:, :] = jnp.concatenate(
            [turned[at : at + half, 2 * HD :], turned[at + half : at + rows, 2 * HD :]], axis=1
        )


def grads_out(slot_row, grads, group):
    total = slot_row.shape[1]
    rows = total // group
    out_rows = rows + rows // 2
    count = owners_per_step(group, rows, 8)
    return pl.pallas_call(
        functools.partial(grads_out_kernel, rows),
        grid=(group // count,),
        in_specs=[whole(slot_row.shape), whole(grads.shape)],
        out_specs=[
            pl.BlockSpec((count, out_rows, 2 * HD), lambda i: (i, 0, 0)),
            pl.BlockSpec((3 * HD, count * rows), lambda i: (0, i)),
        ],
        out_shape=[shape_of((group, out_rows, 2 * HD), BF), shape_of((3 * HD, total), BF)],
        scratch_shapes=[
            pltpu.VMEM((256, total), BF),
            stack_shape(3 * HD, count * rows, total),
        ],
        compiler_params=params(),
        cost_estimate=cost(7),
        name="grads_out",
    )(slot_row, grads)


def head_weight_kernel(grad_ref, unit_ref, w_ref, norm_ref, sums_ref, head_ref, acc_ref, line_ref):
    step = pl.program_id(0)
    term = dot(grad_ref[...], unit_ref[...])
    line = jnp.sum(grad_ref[...].astype(F32), axis=1, keepdims=True)

    @pl.when(step == 0)
    def _():
        acc_ref[...] = term
        line_ref[...] = line

    @pl.when(step > 0)
    def _():
        acc_ref[...] += term
        line_ref[...] += line

    @pl.when(step == pl.num_programs(0) - 1)
    def _():
        head_ref[...] = head_results(acc_ref[...], line_ref[...], w_ref, norm_ref, sums_ref)


def head_weight_grad(grads, unit, head_w, norms, sums_two):
    total, width = unit.shape
    block = 768 if total % 768 == 0 else total
    return pl.pallas_call(
        head_weight_kernel,
        grid=(total // block,),
        in_specs=[
            pl.BlockSpec((3 * HD, block), lambda i: (0, i)),
            pl.BlockSpec((block, width), lambda i: (i, 0)),
            whole(head_w.shape),
            whole(norms.shape),
            whole(sums_two.shape),
        ],
        out_specs=whole((width, 4 * HD)),
        out_shape=shape_of((width, 4 * HD), BF),
        scratch_shapes=[pltpu.VMEM((3 * HD, width), F32), pltpu.VMEM((3 * HD, 1), F32)],
        compiler_params=params(),
        cost_estimate=cost(5),
        name="head_weight",
    )(grads, unit, head_w, norms, sums_two)


def middle_kernel(places, x_ref, packed_ref, proj_ref, norm_ref, mid_ref, h_ref, o_ref):
    half = packed_ref.shape[1]
    for h, place in enumerate(places):
        piece = packed_ref[place]
        o_ref[:half, h * HD : (h + 1) * HD] = piece[:, :HD]
        o_ref[half:, h * HD : (h + 1) * HD] = piece[:, HD:]
    mid = x_ref[...].astype(F32) + dot(o_ref[...], proj_ref[...], NT)
    mid_ref[...] = mid
    unit, _ = normalize(mid)
    h_ref[...] = (unit * norm_ref[1:2, :] + norm_ref[3:4, :]).astype(BF)


def middle(places, x, packed, weights, proj_at, norms):
    rows, width = x.shape
    return pl.pallas_call(
        functools.partial(middle_kernel, places),
        grid=(1,),
        in_specs=[
            whole(x.shape),
            whole(packed.shape),
            pl.BlockSpec((width, width), lambda i: (0, proj_at)),
            whole(norms.shape),
        ],
        out_specs=[whole((rows, width))] * 3,
        out_shape=[
            shape_of((rows, width), F32),
            shape_of((rows, width), BF),
            shape_of((rows, width), BF),
        ],
        compiler_params=params(),
        cost_estimate=cost(3),
        name="middle",
    )(x, packed, weights, norms)


def hidden_kernel(h_ref, dy_ref, inner_ref, outer_ref, act_ref, dpre_ref, dh_ref, dh_acc):
    pre = dot(h_ref[...], inner_ref[...])
    root = 0.7978845608028654
    squared = pre * pre
    bend = jnp.tanh(root * (pre + 0.044715 * (squared * pre)))
    act_ref[...] = (0.5 * pre * (1.0 + bend)).astype(BF)
    slope = 0.5 * (1.0 + bend) + 0.5 * pre * (1.0 - bend * bend) * (
        root * (1.0 + 3.0 * 0.044715 * squared)
    )
    dpre = (dot(dy_ref[...], outer_ref[...]) * slope).astype(BF)
    dpre_ref[...] = dpre
    dh = dot(dpre, inner_ref[...], NT)

    @pl.when(pl.program_id(0) == 0)
    def _():
        dh_acc[...] = dh

    @pl.when(pl.program_id(0) > 0)
    def _():
        dh_acc[...] += dh

    @pl.when(pl.program_id(0) == pl.num_programs(0) - 1)
    def _():
        dh_ref[...] = dh_acc[...].astype(dh_ref.dtype)


def hidden(h, dy, weights, hidden_width, kind):
    rows, width = h.shape
    chunk = 512
    steps = hidden_width // chunk
    return pl.pallas_call(
        hidden_kernel,
        grid=(steps,),
        in_specs=[
            whole(h.shape),
            whole(dy.shape),
            pl.BlockSpec((width, chunk), lambda i: (0, i)),
            pl.BlockSpec((width, chunk), lambda i: (0, i + steps)),
        ],
        out_specs=[
            pl.BlockSpec((rows, chunk), lambda i: (0, i)),
            pl.BlockSpec((rows, chunk), lambda i: (0, i)),
            whole((rows, width)),
        ],
        out_shape=[
            shape_of((rows, hidden_width), BF),
            shape_of((rows, hidden_width), BF),
            shape_of((rows, width), kind),
        ],
        scratch_shapes=[pltpu.VMEM((rows, width), F32)],
        compiler_params=params(),
        cost_estimate=cost(6),
        name="hidden",
    )(h, dy, weights, weights)


def layer_kernel(own_ref, other_ref, outer_ref, out_ref, send_ref):
    out_ref[...] = dot(own_ref[...], outer_ref[...], NT)
    send_ref[...] = dot(other_ref[...], outer_ref[...], NT).astype(BF)


def layer_terms(act_own, act_other, weights):
    rows, span = act_own.shape
    width = weights.shape[0]
    return pl.pallas_call(
        layer_kernel,
        grid=(1,),
        in_specs=[
            whole(act_own.shape),
            whole(act_other.shape),
            pl.BlockSpec((width, span), lambda i: (0, 1)),
        ],
        out_specs=[whole((rows, width))] * 2,
        out_shape=[shape_of((rows, width), F32), shape_of((rows, width), BF)],
        compiler_params=params(),
        cost_estimate=cost(4),
        name="layer_terms",
    )(act_own, act_other, weights)


def middle_back_kernel(
    places, own_ref, other_ref, dy_ref, mid_ref, norm_ref, proj_ref, dmid_ref, low_ref, packed_ref, sums_ref
):
    half = packed_ref.shape[1]
    dh = own_ref[...] + other_ref[...].astype(F32)
    unit, scale = normalize(mid_ref[...])
    sums_ref[0:1, :] = jnp.sum(dh * unit, axis=0, keepdims=True)
    sums_ref[1:2, :] = jnp.sum(dh, axis=0, keepdims=True)
    dmid = dy_ref[...].astype(F32) + normalize_back(dh * norm_ref[1:2, :], unit, scale)
    dmid_ref[...] = dmid
    low = dmid.astype(BF)
    low_ref[...] = low
    grad = dot(low, proj_ref[...]).astype(BF)
    packed_ref[...] = jnp.zeros_like(packed_ref)
    for h, place in enumerate(places):
        cut = slice(h * HD, (h + 1) * HD)
        packed_ref[place] = jnp.concatenate([grad[:half, cut], grad[half:, cut]], axis=1)


def middle_back(places, group, own, other, dy, mid, norms, weights, proj_at):
    rows, width = mid.shape
    return pl.pallas_call(
        functools.partial(middle_back_kernel, places),
        grid=(1,),
        in_specs=[
            whole(own.shape),
            whole(other.shape),
            whole(dy.shape),
            whole(mid.shape),
            whole(norms.shape),
            pl.BlockSpec((width, width), lambda i: (0, proj_at)),
        ],
        out_specs=[
            whole((rows, width)),
            whole((rows, width)),
            whole((group, rows // 2, 2 * HD)),
            whole((2, width)),
        ],
        out_shape=[
            shape_of((rows, width), F32),
            shape_of((rows, width), BF),
            shape_of((group, rows // 2, 2 * HD), BF),
            shape_of((2, width), F32),
        ],
        compiler_params=params(),
        cost_estimate=cost(4),
        name="middle_back",
    )(own, other, dy, mid, norms, weights)


def split_rows(share, at_ref, block, scratch_ref, keep_ref, send_ref):
    if share == 0:
        half = keep_ref.shape[0]
        keep_ref[...] = block[:half].astype(BF)
        send_ref[...] = block[half:].astype(BF)
        return
    scratch_ref[...] = block
    for pair in range(keep_ref.shape[0] // share):
        cut = slice(pair * share, (pair + 1) * share)
        for target, parity in ((keep_ref, at_ref[0]), (send_ref, 1 - at_ref[0])):
            at = pl.multiple_of((2 * pair + parity) * share, share)
            target[cut, :] = scratch_ref[pl.ds(at, share), :].astype(BF)


def weight_kernel(share, at_ref, a0, a1, b0, b1, keep_ref, send_ref, scratch_ref):
    block = dot(a0[...], b0[...], TN) + dot(a1[...], b1[...], TN)
    split_rows(share, at_ref, block, scratch_ref, keep_ref, send_ref)


def weight_grads(share, parity, left, right, spare):
    rows, width = left[0].shape
    span = right[0].shape[1] // width
    column = pl.BlockSpec((rows, width), lambda i, at: (0, i))
    plain = whole((rows, width))
    out = shape_of((width // 2, span * width + spare), BF)
    return pl.pallas_call(
        functools.partial(weight_kernel, share),
        grid_spec=pltpu.PrefetchScalarGridSpec(
            num_scalar_prefetch=1,
            grid=(span,),
            in_specs=[plain, plain, column, column],
            out_specs=[pl.BlockSpec((width // 2, width), lambda i, at: (0, i))] * 2,
            scratch_shapes=[pltpu.VMEM((width, width), F32)],
        ),
        out_shape=[out, out],
        compiler_params=params(),
        cost_estimate=cost(4),
        name="weight_grads",
    )(parity, *left, *right)


def proj_kernel(share, at_ref, low_ref, o_ref, kept_ref, sent_ref, keep_ref, send_ref, scratch_ref):
    block = dot(low_ref[...], o_ref[...], TN)
    split_rows(share, at_ref, block, scratch_ref, keep_ref, send_ref)


def proj_grads(share, parity, low, o, keep, send):
    width = o.shape[1]
    last = keep.shape[1] // width - 1
    return pl.pallas_call(
        functools.partial(proj_kernel, share),
        grid_spec=pltpu.PrefetchScalarGridSpec(
            num_scalar_prefetch=1,
            grid=(1,),
            in_specs=[whole(low.shape), whole(o.shape)] + [pl.BlockSpec(memory_space=pl.ANY)] * 2,
            out_specs=[pl.BlockSpec((width // 2, width), lambda i, at: (0, last))] * 2,
            scratch_shapes=[pltpu.VMEM((width, width), F32)],
        ),
        out_shape=[shape_of(keep.shape, BF)] * 2,
        input_output_aliases={3: 0, 4: 1},
        compiler_params=params(),
        cost_estimate=cost(2),
        name="proj_grads",
    )(parity, low, o, keep, send)


def input_back_kernel(places, packed_ref, w_ref, x_ref, dmid_ref, norm_ref, out_ref, flat_ref):
    rows, _ = x_ref.shape
    half = rows // 2
    for h, place in enumerate(places):
        at = 3 * HD * h
        piece = packed_ref[place]
        flat_ref[:, at : at + 2 * HD] = piece[:rows]
        flat_ref[:half, at + 2 * HD : at + 3 * HD] = piece[rows:, :HD]
        flat_ref[half:, at + 2 * HD : at + 3 * HD] = piece[rows:, HD:]
    dh = dot(flat_ref[...], w_ref[...], NT)
    unit, scale = normalize(x_ref[...].astype(F32))
    out_ref[...] = (dmid_ref[...] + normalize_back(dh * norm_ref[0:1, :], unit, scale)).astype(BF)


def input_back(places, packed, weights, x, dmid, norms):
    rows, width = x.shape
    return pl.pallas_call(
        functools.partial(input_back_kernel, places),
        grid=(1,),
        in_specs=[whole(a.shape) for a in (packed, weights, x, dmid, norms)],
        out_specs=whole((rows, width)),
        out_shape=shape_of((rows, width), BF),
        scratch_shapes=[pltpu.VMEM((rows, 3 * HD * len(places)), BF)],
        compiler_params=params(),
        cost_estimate=cost(5),
        name="input_back",
    )(packed, weights, x, dmid, norms)


def adam_step(master, first_state, second_state, grad_term, step_rate, weight_decay):
    first_new = BETA_ONE * first_state + (1.0 - BETA_ONE) * grad_term
    second_new = BETA_TWO * second_state + (1.0 - BETA_TWO) * grad_term * grad_term
    first_hat = first_new / (1.0 - BETA_ONE**STEP)
    second_hat = second_new / (1.0 - BETA_TWO**STEP)
    master_new = master - step_rate * (
        first_hat / (jnp.sqrt(second_hat) + ADAM_EPS) + weight_decay * master
    )
    return (first_new, second_new, master_new)


def shards(
    tokens,
    cotangent,
    seq_lengths,
    slot_token,
    w_qkv,
    w_proj,
    w_inner,
    w_outer,
    norm_gains,
    norm_biases,
    qkv_first,
    qkv_second,
    proj_first,
    proj_second,
    inner_first,
    inner_second,
    outer_first,
    outer_second,
    norm_first,
    norm_second,
):
    side = lax.axis_index("ha")
    group = lax.axis_size("pb") * lax.axis_size("ka")
    rows, width = tokens.shape[1:]
    total = rows * group
    w_rows = w_qkv.shape[0]
    half_width = w_qkv.shape[2]
    heads = 2 * half_width // HD
    hidden_half = w_inner.shape[1]
    places = head_places(group, heads)
    head_at = [0] * group
    for h, place in enumerate(places):
        head_at[place] = h
    block = min(SCORE_BLOCK, total)

    def swap(a):
        return lax.ppermute(a, "ha", [(0, 1), (1, 0)])

    def ordered(own, other):
        return jnp.where(side == 0, own, other), jnp.where(side == 0, other, own)

    def own_micro(a):
        return lax.dynamic_index_in_dim(a, side, 0, False)

    def other_micro(a):
        return lax.dynamic_index_in_dim(a, 1 - side, 0, False)

    x = own_micro(tokens)
    along_z, along_ka = lax.axis_size("pb"), lax.axis_size("ka")
    stepped = along_z == 4 and along_ka == 4

    def flip(a, axis, size, bit):
        return lax.ppermute(a, axis, [(i, i ^ bit) for i in range(size)])

    if stepped:

        def z_flip(a, bit):
            return flip(a, "pb", along_z, bit)

        def x_flip(a):
            return flip(a, "ka", along_ka, 2)

        def c_flip(a):
            return flip(a, "ka", along_ka, 1)

        own = x[None]
        near, far, own_x, own_c = z_flip(own, 1), z_flip(own, 2), x_flip(own), c_flip(own)
    else:
        x_full = lax.all_gather(x, PLANE, axis=0, tiled=True)
    mine = jnp.concatenate(
        [w_qkv.astype(BF).reshape(w_rows, 3 * half_width), w_proj.astype(BF).T], axis=1
    )
    tok_row = own_micro(slot_token).reshape(1, total)
    mine_other, slot_row = swap(mine), slots_of_tokens(tok_row)
    if stepped:
        near, far = tie(near, far)
        mid_z = jnp.concatenate([near, far])
        last_z, mid_x, mid_c, own_xc = z_flip(far, 1), x_flip(mid_z), c_flip(mid_z), c_flip(own_x)
    low_half, high_half = ordered(mine, mine_other)
    qkv_rows = jnp.concatenate(
        [
            a[:, : 3 * half_width].reshape(w_rows, 3, heads // 2, HD).swapaxes(1, 2)
            for a in (low_half, high_half)
        ],
        axis=1,
    ).reshape(w_rows, heads, 3 * HD)
    proj_rows = jnp.concatenate(
        [a[:, 3 * half_width :] for a in (low_half, high_half)], axis=1
    )
    norm_master = jnp.concatenate([norm_gains, norm_biases], axis=0)
    head_rows = jnp.stack([qkv_rows[:, head_at[d]] for d in range(group)], axis=0)
    head_rows = jnp.concatenate(
        [
            head_rows,
            jnp.broadcast_to(norm_master.astype(BF).T[None], (group, w_rows, 4)),
            jnp.zeros((group, w_rows, HD - 4), BF),
        ],
        axis=2,
    )
    head_w = lax.all_to_all(head_rows, PLANE, 0, 0, tiled=True)
    if stepped:
        last_z, mid_x, mid_c, own_xc, head_w, slot_row = tie(
            last_z, mid_x, mid_c, own_xc, head_w, slot_row
        )
        last_x, last_c, mid_xc = x_flip(last_z), c_flip(last_z), c_flip(mid_x)
    else:
        head_w, slot_row = tie(head_w, slot_row)
    head_w = head_w.reshape(width, 4 * HD)
    norms = head_w[:, 3 * HD : 3 * HD + 4].astype(F32).T
    head_w = head_w[:, : 3 * HD].T
    main_rows = jnp.concatenate(
        [
            w_inner.astype(BF),
            w_outer.astype(BF).T,
            proj_rows,
        ],
        axis=1,
    )
    if stepped:
        main_rows, mid_x = tie(main_rows, mid_x)
    else:
        main_rows, x_full = tie(main_rows, x_full)
    main_w = lax.all_gather(main_rows, PLANE, axis=0, tiled=True)
    proj_at = 2 * hidden_half // width

    ends = jnp.cumsum(own_micro(seq_lengths))
    starts = jnp.arange(total // block, dtype=jnp.int32) * block
    first_block = jnp.max(jnp.where(ends[None] <= starts[:, None], ends[None], 0), axis=1) // block
    last_block = jnp.min(jnp.where(ends[None] > starts[:, None], ends[None], total), axis=1) // block
    first_block = first_block.astype(jnp.int32)
    last_block = last_block.astype(jnp.int32)

    if stepped:
        z, xc = lax.axis_index("pb"), lax.axis_index("ka")
        at = jnp.stack([z, 0 * z, xc // 2, xc % 2]).astype(jnp.int32)
        groups = ((own, own_x, own_c, own_xc), (mid_z, mid_x, mid_c, mid_xc))
        buffers = qkv_of_piece(at, groups, head_w, norms, total, ())
        last_x, last_c, *buffers = tie(last_x, last_c, *buffers)
        at = jnp.stack([z, 0 * z + 3, xc // 2, xc % 2]).astype(jnp.int32)
        groups = ((last_z, last_x, last_c, c_flip(last_x)),)
        buffers = qkv_of_piece(at, groups, head_w, norms, total, buffers)
        unit, qkv = buffers
    else:
        unit, qkv = qkv_of_head(x_full, head_w, norms)
    q, qt, k, v, vt = sort_qkv(tok_row, qkv)
    o, o_low, lse = attend(first_block, qt, k, vt, block)
    late_rows, o_low = tie(qkv_rows.reshape(w_rows, -1), o_low)
    late_w = lax.all_gather(late_rows, PLANE, axis=0, tiled=True)
    o_packed = lax.all_to_all(slots_out(slot_row, o_low, group), PLANE, 0, 0, tiled=True)
    mid, h_own, o_own = middle(places, x, o_packed, main_w, proj_at, norms)
    h_other = swap(h_own)
    dy_own, dy_other = own_micro(cotangent), other_micro(cotangent)
    act_own, dpre_own, dh_own = hidden(h_own, dy_own, main_w, hidden_half, F32)
    h_other, dh_own = tie(h_other, dh_own)
    act_other, dpre_other, dh_send = hidden(h_other, dy_other, main_w, hidden_half, BF)
    dh_got = swap(dh_send)
    xc = lax.axis_index("ka")
    parity = (xc % 2).reshape(1).astype(jnp.int32)
    share = w_rows if stepped else 0
    inner_halves = weight_grads(share, parity, (h_own, h_other), (dpre_own, dpre_other), 0)
    outer_halves = weight_grads(share, parity, (dy_own, dy_other), (act_own, act_other), width)

    def pair_sum(halves, at):
        shape = (along_z, along_ka // 2, w_rows, halves[0].shape[1])
        parts = [lax.dynamic_index_in_dim(a.reshape(shape), at, 1, False) for a in halves]
        return parts[0].astype(F32) + parts[1].astype(F32)

    def scattered(halves, got):
        rest = (pair_sum(halves, xc // 2) + got.astype(F32)).astype(BF)
        return rest.reshape(-1, rest.shape[-1])

    if stepped:
        inner_halves = (inner_halves[0], c_flip(inner_halves[1]))
        inner_send = pair_sum(inner_halves, 1 - xc // 2).astype(BF)
        dh_got, inner_send, *outer_halves = tie(dh_got, inner_send, *outer_halves)
        inner_got = x_flip(inner_send)
    else:
        dh_got, *outer_halves = tie(dh_got, *outer_halves)

    dmid, dmid_low, g_packed, sums_two = middle_back(
        places, group, dh_own, dh_got, dy_own, mid, norms, main_w, proj_at
    )
    outer_halves = proj_grads(share, parity, dmid_low, o_own, *outer_halves)
    g_packed = lax.all_to_all(g_packed, PLANE, 0, 0, tiled=True)
    out_own, out_send = layer_terms(act_own, act_other, main_w)
    g_packed, out_own, out_send = tie(g_packed, out_own, out_send)
    if stepped:
        outer_halves = (outer_halves[0], c_flip(outer_halves[1]))
        outer_send = pair_sum(outer_halves, 1 - xc // 2).astype(BF)
        inner_got, outer_send = tie(inner_got, outer_send)
        inner_rest = scattered(inner_halves, inner_got)
        outer_got = x_flip(outer_send)
    else:
        inner_sum = lax.psum_scatter(
            jnp.concatenate(inner_halves), PLANE, scatter_dimension=0, tiled=True
        )
    g, gt, delta = sort_grad(tok_row, g_packed, o)
    if stepped:
        g, inner_rest = tie(g, inner_rest)
        inner_sum = lax.psum_scatter(inner_rest, "pb", scatter_dimension=0, tiled=True)
    dqkv = attend_back(last_block, q, qt, k, v, g, gt, lse, delta, block)
    packed, dqkv_low = grads_out(slot_row, dqkv, group)
    if stepped:
        outer_rest = scattered(outer_halves, outer_got)
        dqkv_low, outer_rest, late_w, out_send, out_own, inner_sum = tie(
            dqkv_low, outer_rest, late_w, out_send, out_own, inner_sum
        )
    else:
        outer_sum = lax.psum_scatter(
            jnp.concatenate(outer_halves), PLANE, scatter_dimension=0, tiled=True
        )
    dqkv_own = lax.all_to_all(packed, PLANE, 0, 0, tiled=True)
    out_got = swap(out_send)
    layer_own = (mid + out_own + out_got.astype(F32)).astype(BF)
    layer_out = jnp.stack(ordered(layer_own, swap(layer_own)))

    head_grad = head_weight_grad(dqkv_low, unit, head_w, norms, sums_two)
    head_grad = head_grad.reshape(group, 2, w_rows // 2, 4 * HD)
    keep, send = ordered(head_grad[:, 0], head_grad[:, 1])
    keep = (keep.astype(F32) + swap(send).astype(F32)).astype(BF)
    keep, dqkv_own, layer_out = tie(keep, dqkv_own, layer_out)
    if stepped:
        dqkv_own, outer_rest = tie(dqkv_own, outer_rest)
        outer_sum = lax.psum_scatter(outer_rest, "pb", scatter_dimension=0, tiled=True)
    head_grad = lax.all_to_all(keep, PLANE, 0, 0, tiled=True)
    input_low = input_back(places, dqkv_own, late_w, x, dmid, norms)
    head_grad, outer_sum = tie(head_grad, outer_sum)
    input_grad = jnp.stack(ordered(input_low, swap(input_low))).astype(F32)

    norm_parts = head_grad[:, :, 3 * HD : 3 * HD + 8].astype(F32)
    norm_parts = norm_parts[:, :, :4] + norm_parts[:, :, 4:]
    first_sums = sum(norm_parts[place] for place in places)
    second_sums = jnp.sum(norm_parts, axis=0)
    norm_grad = jnp.stack(
        [first_sums[:, 0], second_sums[:, 1], first_sums[:, 2], second_sums[:, 3]]
    )
    norm_grad = jnp.concatenate(ordered(norm_grad, swap(norm_grad)), axis=1)
    qkv_part = jnp.stack([head_grad[place, :, : 3 * HD] for place in places], axis=1)
    qkv_part = qkv_part.reshape(w_rows // 2, 2, heads // 2, 3, HD)
    keep, send = ordered(qkv_part[:, 0], qkv_part[:, 1])
    qkv_grad = jnp.concatenate(ordered(keep, swap(send)), axis=0).astype(F32)
    qkv_grad = qkv_grad.swapaxes(1, 2).reshape(w_rows, 3, half_width)
    inner_grad = inner_sum.astype(F32)
    outer_grad = outer_sum[:, :hidden_half].astype(F32).T
    proj_part = outer_sum[:, hidden_half:]
    keep, send = ordered(proj_part[:, :half_width], proj_part[:, half_width:])
    proj_grad = (keep.astype(F32) + swap(send).astype(F32)).T

    qkv_out = adam_step(w_qkv, qkv_first, qkv_second, qkv_grad / MICRO, RATE_MATRIX, DECAY_RATE)
    proj_out = adam_step(w_proj, proj_first, proj_second, proj_grad / MICRO, RATE_PROJ, DECAY_RATE)
    inner_out = adam_step(
        w_inner, inner_first, inner_second, inner_grad / MICRO, RATE_MATRIX, DECAY_RATE
    )
    outer_out = adam_step(
        w_outer, outer_first, outer_second, outer_grad / MICRO, RATE_MATRIX, DECAY_RATE
    )
    norm_grad = norm_grad / MICRO
    norm_out = adam_step(norm_master, norm_first, norm_second, norm_grad, RATE_NORM, 0.0)
    norm_two_grad = jnp.stack([norm_grad[1], norm_grad[3]])
    return (
        layer_out,
        input_grad,
        *qkv_out,
        *proj_out,
        *inner_out,
        *outer_out,
        *norm_out,
        norm_two_grad,
    )


def solution(mesh):
    tok = P(None, PLANE, None)
    qkv = P(PLANE, None, "ha")
    down = P("ha", PLANE)
    inner = P(PLANE, "ha")
    norm = P(None, PLANE)
    in_specs = (
        (tok, tok, P(), P(), qkv, down, inner, down, norm, norm)
        + (qkv, qkv, down, down, inner, inner, down, down, norm, norm)
    )
    out_specs = (
        (tok, tok, qkv, qkv, qkv, down, down, down)
        + (inner, inner, inner, down, down, down, norm, norm, norm, norm)
    )
    return jax.shard_map(shards, mesh=mesh, in_specs=in_specs, out_specs=out_specs, check_vma=False)
```

```python
import functools

import jax
import jax.numpy as jnp
from jax import lax
from jax.experimental import pallas as pl
from jax.experimental.pallas import tpu as pltpu
from jax.sharding import PartitionSpec as P

HD = 64
MICRO = 2
STEP = 8
NORM_EPS = 1e-05
BETA_ONE = 0.9
BETA_TWO = 0.95
ADAM_EPS = 1e-08
DECAY_RATE = 0.1
RATE_MATRIX = 0.02
RATE_PROJ = 0.6
RATE_NORM = 0.1
BF = jnp.bfloat16
F32 = jnp.float32
PLANE = ("pb", "ka")
VMEM_LIMIT = 60 * 1024 * 1024
SCORE_BLOCK = 512
SHORT = 4096
STRAIGHT = 4
NT = (((1,), (1,)), ((), ()))
NN = (((1,), (0,)), ((), ()))
TN = (((0,), (0,)), ((), ()))


def dot(a, b, dims=NN):
    return lax.dot_general(a, b, dims, preferred_element_type=F32)


def params(steps=1):
    return pltpu.CompilerParams(
        dimension_semantics=("arbitrary",) * steps, vmem_limit_bytes=VMEM_LIMIT
    )


def cost(us):
    return pl.CostEstimate(flops=int(us * 2e8), bytes_accessed=int(us * 1e6), transcendentals=0)


def tie(*arrays):
    return lax.optimization_barrier(arrays)


def whole(shape):
    return pl.BlockSpec(shape, lambda *_: (0,) * len(shape))


def shape_of(shape, dtype):
    return jax.ShapeDtypeStruct(shape, dtype)


def head_places(group, heads):
    return tuple(h * group // heads for h in range(heads))


def normalize(x):
    center = x - jnp.mean(x, axis=-1, keepdims=True)
    spread = jnp.mean(center * center, axis=-1, keepdims=True)
    scale = lax.rsqrt(spread + NORM_EPS)
    return center * scale, scale


def normalize_back(grad, unit, scale):
    return scale * (
        grad
        - jnp.mean(grad, axis=-1, keepdims=True)
        - unit * jnp.mean(grad * unit, axis=-1, keepdims=True)
    )


def low_match(ids):
    low = lax.bitwise_and(ids, 255).astype(F32).astype(BF)
    line = lax.broadcasted_iota(jnp.int32, (256, 1), 0).astype(F32).astype(BF)
    return jnp.where(low == line, jnp.ones((), BF), jnp.zeros((), BF))


def moved(ids_ref, match_ref, source_ref, stack_ref, first):
    features = source_ref.shape[0]
    chunk = stack_ref.shape[1]
    total = None
    for part in range(source_ref.shape[1] // chunk):
        cut = slice(part * chunk, (part + 1) * chunk)
        high = lax.shift_right_logical(ids_ref[:, cut], 8)
        source = source_ref[:, cut]
        for block in range(stack_ref.shape[0] // features):
            stack_ref[block * features : (block + 1) * features, :] = jnp.where(
                high == first + block, source, jnp.zeros((), BF)
            )
        piece = dot(stack_ref[...], match_ref[:, cut], NT)
        total = piece if total is None else total + piece
    return total


def sort_block(total):
    return total if total <= SHORT else 1024


def stack_shape(features, columns, total):
    return pltpu.VMEM((features * columns // 256, min(3072, total)), BF)


def place_kernel(tok_ref, out_ref):
    total = tok_ref.shape[1]
    count = total // 256
    ids = tok_ref[...]
    high = lax.shift_right_logical(ids, 8)
    slot = lax.broadcasted_iota(jnp.int32, (1, total), 1)
    rows = lax.broadcasted_iota(jnp.int32, (count, 1), 0)
    match = low_match(ids)

    def part(values):
        picked = jnp.where(high == rows, values.astype(F32), 0.0).astype(BF)
        return dot(picked, match, NT)

    found = part(lax.shift_right_logical(slot, 8)) * 256.0 + part(lax.bitwise_and(slot, 255))
    found = found.astype(jnp.int32)
    for a in range(count):
        out_ref[:, a * 256 : (a + 1) * 256] = found[a : a + 1]


def slots_of_tokens(tok_row):
    return pl.pallas_call(
        place_kernel,
        grid=(1,),
        in_specs=[whole(tok_row.shape)],
        out_specs=whole(tok_row.shape),
        out_shape=shape_of(tok_row.shape, jnp.int32),
        compiler_params=params(),
        cost_estimate=cost(2),
        name="slots_of_tokens",
    )(tok_row)


def qkv_kernel(x_ref, w_ref, norm_ref, unit_ref, qkv_ref):
    unit, _ = normalize(x_ref[...].astype(F32))
    h = (unit * norm_ref[0:1, :] + norm_ref[2:3, :]).astype(BF)
    unit_ref[...] = unit.astype(BF)
    qkv_ref[...] = dot(w_ref[...], h, NT).astype(BF)


def qkv_piece_kernel(counts, at_ref, *refs):
    sources = refs[: 4 * len(counts)]
    raw_ref = refs[4 * len(counts)]
    unit_ref, qkv_ref, x_ref, w_ref, norm_ref = refs[-5:]

    @pl.when((pl.program_id(0) == 0) & (pl.program_id(1) == 0))
    def _():
        flat = raw_ref[...].astype(F32).T
        w_ref[...] = flat[: 3 * HD].astype(BF)
        norm_ref[...] = flat[3 * HD : 3 * HD + 8]

    rows = x_ref.shape[0] // 2
    even = at_ref[3] == 0
    slot = 0
    for group, count in enumerate(counts):
        for place in range(count):
            for side in range(2):

                @pl.when((pl.program_id(0) == slot) & (pl.program_id(1) == side))
                def _():
                    own = sources[4 * group + side][place]
                    other = sources[4 * group + 2 + side][place]
                    x_ref[:rows, :] = jnp.where(even, own, other)
                    x_ref[rows:, :] = jnp.where(even, other, own)

            slot += 1
    unit, _ = normalize(x_ref[...].astype(F32))
    h = (unit * norm_ref[0:1, :] + norm_ref[2:3, :]).astype(BF)
    unit_ref[...] = unit.astype(BF)
    qkv_ref[...] = dot(w_ref[...], h, NT).astype(BF)


def qkv_of_piece(at, groups, raw, total, buffers):
    counts = tuple(group[0].shape[0] for group in groups)
    pieces = [a for group in groups for a in group]
    _, rows, width = pieces[0].shape
    kept = [pl.BlockSpec(memory_space=pl.ANY)] * len(buffers)
    first = 1 + len(pieces) + 1

    def place(i, j, at):
        return (at[0] ^ (at[1] + i)) * 2 + (at[2] ^ j)

    return pl.pallas_call(
        functools.partial(qkv_piece_kernel, counts),
        grid_spec=pltpu.PrefetchScalarGridSpec(
            num_scalar_prefetch=1,
            grid=(sum(counts), 2),
            in_specs=[whole(a.shape) for a in (*pieces, raw)] + kept,
            out_specs=[
                pl.BlockSpec((2 * rows, width), lambda i, j, at: (place(i, j, at), 0)),
                pl.BlockSpec((3 * HD, 2 * rows), lambda i, j, at: (0, place(i, j, at))),
            ],
            scratch_shapes=[
                pltpu.VMEM((2 * rows, width), BF),
                pltpu.VMEM((3 * HD, width), BF),
                pltpu.VMEM((8, width), F32),
            ],
        ),
        out_shape=[shape_of((total, width), BF), shape_of((3 * HD, total), BF)],
        input_output_aliases={first: 0, first + 1: 1} if buffers else {},
        compiler_params=params(2),
        cost_estimate=cost(3 * sum(counts)),
        name="qkv_piece",
    )(at, *pieces, raw, *buffers)


def qkv_of_head(x_full, head_w, norms):
    rows, width = x_full.shape
    block = min(512, rows)
    return pl.pallas_call(
        qkv_kernel,
        grid=(rows // block,),
        in_specs=[
            pl.BlockSpec((block, width), lambda i: (i, 0)),
            whole(head_w.shape),
            whole(norms.shape),
        ],
        out_specs=[
            pl.BlockSpec((block, width), lambda i: (i, 0)),
            pl.BlockSpec((head_w.shape[0], block), lambda i: (0, i)),
        ],
        out_shape=[shape_of((rows, width), BF), shape_of((head_w.shape[0], rows), BF)],
        compiler_params=params(),
        cost_estimate=cost(8),
        name="qkv_head",
    )(x_full, head_w, norms)


def sort_kernel(tok_ref, qkv_ref, q_ref, qt_ref, k_ref, v_ref, vt_ref, match_ref, stack_ref):
    @pl.when(pl.program_id(0) == 0)
    def _():
        match_ref[...] = low_match(tok_ref[...])

    count = k_ref.shape[0] // 256
    found = moved(tok_ref, match_ref, qkv_ref, stack_ref, pl.program_id(0) * count)
    for part in range(count):
        cut = slice(part * 256, (part + 1) * 256)
        at = 3 * HD * part
        query = found[at : at + HD] * float(HD) ** -0.5
        value = found[at + 2 * HD : at + 3 * HD]
        qt_ref[:, cut] = query.astype(BF)
        q_ref[cut, :] = query.T.astype(BF)
        k_ref[cut, :] = found[at + HD : at + 2 * HD].T.astype(BF)
        v_ref[cut, :] = value.T.astype(BF)
        vt_ref[:, cut] = value.astype(BF)


def sort_qkv(tok_row, qkv):
    rows = qkv.shape[1]
    block = sort_block(rows)
    narrow = (pl.BlockSpec((block, HD), lambda i: (i, 0)), shape_of((rows, HD), BF))
    wide = (pl.BlockSpec((HD, block), lambda i: (0, i)), shape_of((HD, rows), BF))
    outs = (narrow, wide, narrow, narrow, wide)
    return pl.pallas_call(
        sort_kernel,
        grid=(rows // block,),
        in_specs=[whole(tok_row.shape), whole(qkv.shape)],
        out_specs=[spec for spec, _ in outs],
        out_shape=[shape for _, shape in outs],
        scratch_shapes=[pltpu.VMEM((256, rows), BF), stack_shape(3 * HD, block, rows)],
        compiler_params=params(),
        cost_estimate=cost(5),
        name="sort_qkv",
    )(tok_row, qkv)


def causal(keys, queries, ahead):
    return (
        lax.broadcasted_iota(jnp.int32, (keys, queries), 0)
        <= lax.broadcasted_iota(jnp.int32, (keys, queries), 1) + ahead
    )


def forward_kernel(first_ref, qt_ref, k_ref, vt_ref, o_ref, low_ref, lse_ref):
    block = qt_ref.shape[1]
    index = pl.program_id(0)
    half = block // 2

    def part(keys_at, count, query, state, ahead):
        top, total, acc = state
        scores = dot(k_ref[pl.ds(keys_at, count), :], query)
        square = scores * scores + 1.0
        inverse = lax.rsqrt(square)
        radius = square * inverse
        if ahead is not None:
            radius = jnp.where(causal(count, query.shape[1], ahead), radius, -1e30)
        new_top = jnp.maximum(top, jnp.max(radius, axis=0, keepdims=True))
        weights = jnp.exp(radius - new_top)
        shrink = jnp.exp(top - new_top)
        signed = (scores * inverse * weights).astype(BF)
        acc = acc * shrink + dot(vt_ref[:, pl.ds(keys_at, count)], signed)
        total = total * shrink + jnp.sum(weights, axis=0, keepdims=True)
        return (new_top, total, acc)

    def step(key_block, state):
        at = pl.multiple_of(key_block * block, block)
        return part(at, block, qt_ref[...], state, None)

    def diagonal():
        at = pl.multiple_of(index * block, block)
        empty = tuple(jnp.zeros((n, half), F32) for n in (1, 1, HD))
        low = part(at, half, qt_ref[:, :half], empty, 0)
        high = part(at, block, qt_ref[:, half:], empty, half)
        return tuple(jnp.concatenate([x, y], axis=1) for x, y in zip(low, high))

    def finish(state):
        top, total, acc = state
        out = acc * (1.0 / total)
        o_ref[...] = out
        low_ref[...] = out.astype(BF)
        lse_ref[...] = top + jnp.log(total)

    earlier = index - first_ref[index]
    for count in range(STRAIGHT):

        @pl.when(earlier == count)
        def _():
            state = diagonal()
            for back in range(1, count + 1):
                state = step(index - back, state)
            finish(state)

    @pl.when(earlier >= STRAIGHT)
    def _():
        finish(lax.fori_loop(first_ref[index], index, step, diagonal()))


def attend(first_block, qt, k, vt, block):
    rows = k.shape[0]
    return pl.pallas_call(
        forward_kernel,
        grid_spec=pltpu.PrefetchScalarGridSpec(
            num_scalar_prefetch=1,
            grid=(rows // block,),
            in_specs=[
                pl.BlockSpec((HD, block), lambda i, *_: (0, i)),
                whole(k.shape),
                whole(vt.shape),
            ],
            out_specs=[
                pl.BlockSpec((HD, block), lambda i, *_: (0, i)),
                pl.BlockSpec((HD, block), lambda i, *_: (0, i)),
                pl.BlockSpec((1, block), lambda i, *_: (0, i)),
            ],
        ),
        out_shape=[shape_of((HD, rows), F32), shape_of((HD, rows), BF), shape_of((1, rows), F32)],
        compiler_params=params(),
        cost_estimate=cost(13),
        name="attend_fwd",
    )(first_block, qt, k, vt)


def slots_out_kernel(rows, slot_ref, low_ref, out_ref, match_ref, stack_ref):
    half = rows // 2

    @pl.when(pl.program_id(0) == 0)
    def _():
        match_ref[...] = low_match(slot_ref[...])

    owners = out_ref.shape[0]
    count = owners * rows // 256
    found = moved(slot_ref, match_ref, low_ref, stack_ref, pl.program_id(0) * count)
    found = jnp.concatenate([found[p * HD : (p + 1) * HD].T for p in range(count)], axis=0)
    found = found.astype(BF)
    for d in range(owners):
        at = d * rows
        out_ref[d] = jnp.concatenate([found[at : at + half], found[at + half : at + rows]], axis=1)


def slots_out(slot_row, low, group):
    total = slot_row.shape[1]
    rows = total // group
    count = owners_per_step(group, rows)
    return pl.pallas_call(
        functools.partial(slots_out_kernel, rows),
        grid=(group // count,),
        in_specs=[whole(slot_row.shape), whole(low.shape)],
        out_specs=pl.BlockSpec((count, rows // 2, 2 * HD), lambda i: (i, 0, 0)),
        out_shape=shape_of((group, rows // 2, 2 * HD), BF),
        scratch_shapes=[pltpu.VMEM((256, total), BF), stack_shape(HD, count * rows, total)],
        compiler_params=params(),
        cost_estimate=cost(3),
        name="slots_out",
    )(slot_row, low)


def owners_per_step(group, rows, most=16):
    for count in (16, 8, 4, 2, 1):
        if count > (most if group * rows <= SHORT else 4):
            continue
        if group % count == 0 and count * rows % 256 == 0:
            return count
    return group


def sort_grad_kernel(
    tok_ref, packed_ref, o_ref, g_ref, gt_ref, delta_ref, slots_ref, match_ref, stack_ref
):
    group, half, _ = packed_ref.shape

    @pl.when(pl.program_id(0) == 0)
    def _():
        match_ref[...] = low_match(tok_ref[...])
        for d in range(group):
            piece = packed_ref[d].astype(F32).T.astype(BF)
            slots_ref[:, 2 * d * half : (2 * d + 1) * half] = piece[:HD]
            slots_ref[:, (2 * d + 1) * half : (2 * d + 2) * half] = piece[HD:]

    count = g_ref.shape[0] // 256
    found = moved(tok_ref, match_ref, slots_ref, stack_ref, pl.program_id(0) * count)
    for part in range(count):
        cut = slice(part * 256, (part + 1) * 256)
        grad = found[part * HD : (part + 1) * HD]
        gt_ref[:, cut] = grad.astype(BF)
        g_ref[cut, :] = grad.T.astype(BF)
        delta_ref[:, cut] = jnp.sum(grad * o_ref[:, cut], axis=0, keepdims=True)


def sort_grad(tok_row, packed, o):
    rows = o.shape[1]
    block = sort_block(rows)
    wide = pl.BlockSpec((HD, block), lambda i: (0, i))
    return pl.pallas_call(
        sort_grad_kernel,
        grid=(rows // block,),
        in_specs=[whole(tok_row.shape), whole(packed.shape), wide],
        out_specs=[
            pl.BlockSpec((block, HD), lambda i: (i, 0)),
            wide,
            pl.BlockSpec((1, block), lambda i: (0, i)),
        ],
        out_shape=[shape_of((rows, HD), BF), shape_of((HD, rows), BF), shape_of((1, rows), F32)],
        scratch_shapes=[
            pltpu.VMEM((HD, rows), BF),
            pltpu.VMEM((256, rows), BF),
            stack_shape(HD, block, rows),
        ],
        compiler_params=params(),
        cost_estimate=cost(4),
        name="sort_grad",
    )(tok_row, packed, o)


def backward_kernel(
    last_ref, q_ref, qt_ref, k_ref, v_ref, g_ref, gt_ref, lse_ref, delta_ref, out_ref, dq_ref, dk_ref, dv_ref
):
    block = k_ref.shape[0]
    index = pl.program_id(0)

    @pl.when(index == 0)
    def _():
        dq_ref[...] = jnp.zeros_like(dq_ref)

    key = k_ref[...]
    key_t = key.astype(F32).T.astype(BF)
    value = v_ref[...]

    half = block // 2

    def part(at, width, count, ahead):
        cut = pl.ds(at, width)
        scores = dot(key[:count], qt_ref[:, cut])
        square = scores * scores + 1.0
        inverse = lax.rsqrt(square)
        shifted = square * inverse - lse_ref[:, cut]
        if ahead is not None:
            shifted = jnp.where(causal(count, width, ahead), shifted, -1e30)
        weights = jnp.exp(shifted)
        slope = scores * inverse
        along = dot(value[:count], gt_ref[:, cut])
        bend = 1.0 + inverse * inverse * (inverse - 1.0)
        score_grad = weights * (bend * along - slope * delta_ref[:, cut])
        signed = (slope * weights).astype(BF)
        low_grad = score_grad.astype(BF)
        dv = dot(signed, g_ref[cut, :])
        dk = dot(low_grad, q_ref[cut, :])
        dq_ref[:, cut] += dot(key_t[:, :count], low_grad)
        return dk, dv

    def step(query_block):
        return part(pl.multiple_of(query_block * block, block), block, block, None)

    def diagonal():
        at = pl.multiple_of(index * block, block)
        low = part(at, half, half, 0)
        high = part(pl.multiple_of(at + half, half), half, block, half)
        return tuple(jnp.concatenate([x + y[:half], y[half:]], axis=0) for x, y in zip(low, high))

    def finish(dk, dv):
        at = pl.multiple_of(index * block, block)
        out_ref[:HD] = (dq_ref[:, pl.ds(at, block)] * float(HD) ** -0.5).astype(BF)
        out_ref[HD : 2 * HD] = dk.T.astype(BF)
        out_ref[2 * HD :] = dv.T.astype(BF)

    later = last_ref[index] - index
    for count in range(1, STRAIGHT + 1):

        @pl.when(later == count)
        def _():
            dk, dv = diagonal()
            for ahead in range(1, count):
                dk_more, dv_more = step(index + ahead)
                dk, dv = dk + dk_more, dv + dv_more
            finish(dk, dv)

    @pl.when(later > STRAIGHT)
    def _():
        dk_ref[...], dv_ref[...] = diagonal()

        def body(query_block, carry):
            dk_more, dv_more = step(query_block)
            dk_ref[...] += dk_more
            dv_ref[...] += dv_more
            return carry

        lax.fori_loop(index + 1, last_ref[index], body, 0)
        finish(dk_ref[...], dv_ref[...])


def attend_back(last_block, q, qt, k, v, g, gt, lse, delta, block):
    rows = q.shape[0]
    return pl.pallas_call(
        backward_kernel,
        grid_spec=pltpu.PrefetchScalarGridSpec(
            num_scalar_prefetch=1,
            grid=(rows // block,),
            in_specs=[
                whole(q.shape),
                whole(qt.shape),
                pl.BlockSpec((block, HD), lambda i, *_: (i, 0)),
                pl.BlockSpec((block, HD), lambda i, *_: (i, 0)),
                whole(g.shape),
                whole(gt.shape),
                whole(lse.shape),
                whole(delta.shape),
            ],
            out_specs=pl.BlockSpec((3 * HD, block), lambda i, *_: (0, i)),
            scratch_shapes=[
                pltpu.VMEM((HD, rows), F32),
                pltpu.VMEM((block, HD), F32),
                pltpu.VMEM((block, HD), F32),
            ],
        ),
        out_shape=shape_of((3 * HD, rows), BF),
        compiler_params=params(),
        cost_estimate=cost(19),
        name="attend_bwd",
    )(last_block, q, qt, k, v, g, gt, lse, delta)


def head_results(acc, column, w_ref, norm_ref, sums_ref):
    weights = w_ref[...].astype(F32)
    grad = acc * norm_ref[0:1, :] + column * norm_ref[2:3, :]
    sums = jnp.concatenate(
        [
            jnp.sum(weights * acc, axis=0, keepdims=True),
            sums_ref[0:1, :],
            jnp.sum(weights * column, axis=0, keepdims=True),
            sums_ref[1:2, :],
        ],
        axis=0,
    )
    top = sums.astype(BF).astype(F32)
    rest = jnp.concatenate([top, sums - top, jnp.zeros((HD - 8, sums.shape[1]), F32)], axis=0)
    return jnp.concatenate([grad, rest], axis=0).T.astype(BF)


def grads_out_kernel(rows, slot_ref, grad_ref, out_ref, low_ref, match_ref, stack_ref):
    half = rows // 2
    step = pl.program_id(0)

    @pl.when(step == 0)
    def _():
        match_ref[...] = low_match(slot_ref[...])

    count = out_ref.shape[0]
    parts = count * rows // 256
    found = moved(slot_ref, match_ref, grad_ref, stack_ref, step * parts)
    turned = []
    for p in range(parts):
        piece = found[3 * HD * p : 3 * HD * (p + 1)]
        low_ref[:, p * 256 : (p + 1) * 256] = piece.astype(BF)
        turned.append(piece.T)
    turned = jnp.concatenate(turned, axis=0).astype(BF)
    for d in range(count):
        at = d * rows
        out_ref[d, :rows, :] = turned[at : at + rows, : 2 * HD]
        out_ref[d, rows:, :] = jnp.concatenate(
            [turned[at : at + half, 2 * HD :], turned[at + half : at + rows, 2 * HD :]], axis=1
        )


def grads_out(slot_row, grads, group):
    total = slot_row.shape[1]
    rows = total // group
    out_rows = rows + rows // 2
    count = owners_per_step(group, rows, 8)
    return pl.pallas_call(
        functools.partial(grads_out_kernel, rows),
        grid=(group // count,),
        in_specs=[whole(slot_row.shape), whole(grads.shape)],
        out_specs=[
            pl.BlockSpec((count, out_rows, 2 * HD), lambda i: (i, 0, 0)),
            pl.BlockSpec((3 * HD, count * rows), lambda i: (0, i)),
        ],
        out_shape=[shape_of((group, out_rows, 2 * HD), BF), shape_of((3 * HD, total), BF)],
        scratch_shapes=[
            pltpu.VMEM((256, total), BF),
            stack_shape(3 * HD, count * rows, total),
        ],
        compiler_params=params(),
        cost_estimate=cost(7),
        name="grads_out",
    )(slot_row, grads)


def head_weight_kernel(grad_ref, unit_ref, w_ref, norm_ref, sums_ref, head_ref, acc_ref, line_ref):
    step = pl.program_id(0)
    term = dot(grad_ref[...], unit_ref[...])
    line = jnp.sum(grad_ref[...].astype(F32), axis=1, keepdims=True)

    @pl.when(step == 0)
    def _():
        acc_ref[...] = term
        line_ref[...] = line

    @pl.when(step > 0)
    def _():
        acc_ref[...] += term
        line_ref[...] += line

    @pl.when(step == pl.num_programs(0) - 1)
    def _():
        head_ref[...] = head_results(acc_ref[...], line_ref[...], w_ref, norm_ref, sums_ref)


def head_weight_grad(grads, unit, head_w, norms, sums_two):
    total, width = unit.shape
    block = 768 if total % 768 == 0 else total
    return pl.pallas_call(
        head_weight_kernel,
        grid=(total // block,),
        in_specs=[
            pl.BlockSpec((3 * HD, block), lambda i: (0, i)),
            pl.BlockSpec((block, width), lambda i: (i, 0)),
            whole(head_w.shape),
            whole(norms.shape),
            whole(sums_two.shape),
        ],
        out_specs=whole((width, 4 * HD)),
        out_shape=shape_of((width, 4 * HD), BF),
        scratch_shapes=[pltpu.VMEM((3 * HD, width), F32), pltpu.VMEM((3 * HD, 1), F32)],
        compiler_params=params(),
        cost_estimate=cost(5),
        name="head_weight",
    )(grads, unit, head_w, norms, sums_two)


def middle_kernel(places, x_ref, packed_ref, proj_ref, norm_ref, mid_ref, h_ref, o_ref):
    half = packed_ref.shape[1]
    for h, place in enumerate(places):
        piece = packed_ref[place]
        o_ref[:half, h * HD : (h + 1) * HD] = piece[:, :HD]
        o_ref[half:, h * HD : (h + 1) * HD] = piece[:, HD:]
    mid = x_ref[...].astype(F32) + dot(o_ref[...], proj_ref[...], NT)
    mid_ref[...] = mid
    unit, _ = normalize(mid)
    h_ref[...] = (unit * norm_ref[1:2, :] + norm_ref[3:4, :]).astype(BF)


def middle(places, x, packed, weights, proj_at, norms):
    rows, width = x.shape
    return pl.pallas_call(
        functools.partial(middle_kernel, places),
        grid=(1,),
        in_specs=[
            whole(x.shape),
            whole(packed.shape),
            pl.BlockSpec((width, width), lambda i: (0, proj_at)),
            whole(norms.shape),
        ],
        out_specs=[whole((rows, width))] * 3,
        out_shape=[
            shape_of((rows, width), F32),
            shape_of((rows, width), BF),
            shape_of((rows, width), BF),
        ],
        compiler_params=params(),
        cost_estimate=cost(3),
        name="middle",
    )(x, packed, weights, norms)


def hidden_kernel(h_ref, dy_ref, inner_ref, outer_ref, act_ref, dpre_ref, dh_ref, dh_acc):
    pre = dot(h_ref[...], inner_ref[...])
    root = 0.7978845608028654
    squared = pre * pre
    bend = jnp.tanh(root * (pre + 0.044715 * (squared * pre)))
    act_ref[...] = (0.5 * pre * (1.0 + bend)).astype(BF)
    slope = 0.5 * (1.0 + bend) + 0.5 * pre * (1.0 - bend * bend) * (
        root * (1.0 + 3.0 * 0.044715 * squared)
    )
    dpre = (dot(dy_ref[...], outer_ref[...]) * slope).astype(BF)
    dpre_ref[...] = dpre
    dh = dot(dpre, inner_ref[...], NT)

    @pl.when(pl.program_id(0) == 0)
    def _():
        dh_acc[...] = dh

    @pl.when(pl.program_id(0) > 0)
    def _():
        dh_acc[...] += dh

    @pl.when(pl.program_id(0) == pl.num_programs(0) - 1)
    def _():
        dh_ref[...] = dh_acc[...].astype(dh_ref.dtype)


def hidden(h, dy, weights, hidden_width, kind):
    rows, width = h.shape
    chunk = 512
    steps = hidden_width // chunk
    return pl.pallas_call(
        hidden_kernel,
        grid=(steps,),
        in_specs=[
            whole(h.shape),
            whole(dy.shape),
            pl.BlockSpec((width, chunk), lambda i: (0, i)),
            pl.BlockSpec((width, chunk), lambda i: (0, i + steps)),
        ],
        out_specs=[
            pl.BlockSpec((rows, chunk), lambda i: (0, i)),
            pl.BlockSpec((rows, chunk), lambda i: (0, i)),
            whole((rows, width)),
        ],
        out_shape=[
            shape_of((rows, hidden_width), BF),
            shape_of((rows, hidden_width), BF),
            shape_of((rows, width), kind),
        ],
        scratch_shapes=[pltpu.VMEM((rows, width), F32)],
        compiler_params=params(),
        cost_estimate=cost(6),
        name="hidden",
    )(h, dy, weights, weights)


def layer_kernel(own_ref, other_ref, outer_ref, out_ref, send_ref):
    out_ref[...] = dot(own_ref[...], outer_ref[...], NT)
    send_ref[...] = dot(other_ref[...], outer_ref[...], NT).astype(BF)


def layer_terms(act_own, act_other, weights):
    rows, span = act_own.shape
    width = weights.shape[0]
    return pl.pallas_call(
        layer_kernel,
        grid=(1,),
        in_specs=[
            whole(act_own.shape),
            whole(act_other.shape),
            pl.BlockSpec((width, span), lambda i: (0, 1)),
        ],
        out_specs=[whole((rows, width))] * 2,
        out_shape=[shape_of((rows, width), F32), shape_of((rows, width), BF)],
        compiler_params=params(),
        cost_estimate=cost(4),
        name="layer_terms",
    )(act_own, act_other, weights)


def middle_back_kernel(
    places, own_ref, other_ref, dy_ref, mid_ref, norm_ref, proj_ref, dmid_ref, low_ref, packed_ref, sums_ref
):
    half = packed_ref.shape[1]
    dh = own_ref[...] + other_ref[...].astype(F32)
    unit, scale = normalize(mid_ref[...])
    sums_ref[0:1, :] = jnp.sum(dh * unit, axis=0, keepdims=True)
    sums_ref[1:2, :] = jnp.sum(dh, axis=0, keepdims=True)
    dmid = dy_ref[...].astype(F32) + normalize_back(dh * norm_ref[1:2, :], unit, scale)
    dmid_ref[...] = dmid
    low = dmid.astype(BF)
    low_ref[...] = low
    grad = dot(low, proj_ref[...]).astype(BF)
    packed_ref[...] = jnp.zeros_like(packed_ref)
    for h, place in enumerate(places):
        cut = slice(h * HD, (h + 1) * HD)
        packed_ref[place] = jnp.concatenate([grad[:half, cut], grad[half:, cut]], axis=1)


def middle_back(places, group, own, other, dy, mid, norms, weights, proj_at):
    rows, width = mid.shape
    return pl.pallas_call(
        functools.partial(middle_back_kernel, places),
        grid=(1,),
        in_specs=[
            whole(own.shape),
            whole(other.shape),
            whole(dy.shape),
            whole(mid.shape),
            whole(norms.shape),
            pl.BlockSpec((width, width), lambda i: (0, proj_at)),
        ],
        out_specs=[
            whole((rows, width)),
            whole((rows, width)),
            whole((group, rows // 2, 2 * HD)),
            whole((2, width)),
        ],
        out_shape=[
            shape_of((rows, width), F32),
            shape_of((rows, width), BF),
            shape_of((group, rows // 2, 2 * HD), BF),
            shape_of((2, width), F32),
        ],
        compiler_params=params(),
        cost_estimate=cost(4),
        name="middle_back",
    )(own, other, dy, mid, norms, weights)


def split_rows(share, at_ref, block, scratch_ref, keep_ref, send_ref):
    if share == 0:
        half = keep_ref.shape[0]
        keep_ref[...] = block[:half].astype(BF)
        send_ref[...] = block[half:].astype(BF)
        return
    scratch_ref[...] = block
    for pair in range(keep_ref.shape[0] // share):
        cut = slice(pair * share, (pair + 1) * share)
        for target, parity in ((keep_ref, at_ref[0]), (send_ref, 1 - at_ref[0])):
            at = pl.multiple_of((2 * pair + parity) * share, share)
            target[cut, :] = scratch_ref[pl.ds(at, share), :].astype(BF)


def weight_kernel(
    span, share, at_ref, h0, h1, p0, p1, dy0, dy1, a0, a1, keep_in, send_in, keep_out, send_out, scratch_ref
):
    index = pl.program_id(0)

    @pl.when(index < span)
    def _():
        block = dot(h0[...], p0[...], TN) + dot(h1[...], p1[...], TN)
        split_rows(share, at_ref, block, scratch_ref, keep_in, send_in)

    @pl.when(index >= span)
    def _():
        block = dot(dy0[...], a0[...], TN) + dot(dy1[...], a1[...], TN)
        split_rows(share, at_ref, block, scratch_ref, keep_out, send_out)


def weight_grads(share, parity, h_pair, dpre_pair, dy_pair, act_pair, spare):
    rows, width = h_pair[0].shape
    span = act_pair[0].shape[1] // width

    def first(i, at):
        return (0, jnp.minimum(i, span - 1))

    def second(i, at):
        return (0, jnp.maximum(i - span, 0))

    def column(count, where):
        return pl.BlockSpec((count, width), where)

    plain = whole((rows, width))
    half = width // 2
    inner = shape_of((half, span * width), BF)
    outer = shape_of((half, span * width + spare), BF)
    return pl.pallas_call(
        functools.partial(weight_kernel, span, share),
        grid_spec=pltpu.PrefetchScalarGridSpec(
            num_scalar_prefetch=1,
            grid=(2 * span,),
            in_specs=[plain, plain, column(rows, first), column(rows, first)]
            + [plain, plain, column(rows, second), column(rows, second)],
            out_specs=[column(half, first)] * 2 + [column(half, second)] * 2,
            scratch_shapes=[pltpu.VMEM((width, width), F32)],
        ),
        out_shape=[inner, inner, outer, outer],
        compiler_params=params(),
        cost_estimate=cost(8),
        name="weight_grads",
    )(parity, *h_pair, *dpre_pair, *dy_pair, *act_pair)


def proj_kernel(share, at_ref, low_ref, o_ref, kept_ref, sent_ref, keep_ref, send_ref, scratch_ref):
    block = dot(low_ref[...], o_ref[...], TN)
    split_rows(share, at_ref, block, scratch_ref, keep_ref, send_ref)


def proj_grads(share, parity, low, o, keep, send):
    width = o.shape[1]
    last = keep.shape[1] // width - 1
    return pl.pallas_call(
        functools.partial(proj_kernel, share),
        grid_spec=pltpu.PrefetchScalarGridSpec(
            num_scalar_prefetch=1,
            grid=(1,),
            in_specs=[whole(low.shape), whole(o.shape)] + [pl.BlockSpec(memory_space=pl.ANY)] * 2,
            out_specs=[pl.BlockSpec((width // 2, width), lambda i, at: (0, last))] * 2,
            scratch_shapes=[pltpu.VMEM((width, width), F32)],
        ),
        out_shape=[shape_of(keep.shape, BF)] * 2,
        input_output_aliases={3: 0, 4: 1},
        compiler_params=params(),
        cost_estimate=cost(2),
        name="proj_grads",
    )(parity, low, o, keep, send)


def input_back_kernel(places, packed_ref, w_ref, x_ref, dmid_ref, norm_ref, out_ref, flat_ref):
    rows, _ = x_ref.shape
    half = rows // 2
    for h, place in enumerate(places):
        at = 3 * HD * h
        piece = packed_ref[place]
        flat_ref[:, at : at + 2 * HD] = piece[:rows]
        flat_ref[:half, at + 2 * HD : at + 3 * HD] = piece[rows:, :HD]
        flat_ref[half:, at + 2 * HD : at + 3 * HD] = piece[rows:, HD:]
    dh = dot(flat_ref[...], w_ref[...], NT)
    unit, scale = normalize(x_ref[...].astype(F32))
    out_ref[...] = (dmid_ref[...] + normalize_back(dh * norm_ref[0:1, :], unit, scale)).astype(BF)


def input_back(places, packed, weights, x, dmid, norms):
    rows, width = x.shape
    return pl.pallas_call(
        functools.partial(input_back_kernel, places),
        grid=(1,),
        in_specs=[whole(a.shape) for a in (packed, weights, x, dmid, norms)],
        out_specs=whole((rows, width)),
        out_shape=shape_of((rows, width), BF),
        scratch_shapes=[pltpu.VMEM((rows, 3 * HD * len(places)), BF)],
        compiler_params=params(),
        cost_estimate=cost(5),
        name="input_back",
    )(packed, weights, x, dmid, norms)


def adam_step(master, first_state, second_state, grad_term, step_rate, weight_decay):
    first_new = BETA_ONE * first_state + (1.0 - BETA_ONE) * grad_term
    second_new = BETA_TWO * second_state + (1.0 - BETA_TWO) * grad_term * grad_term
    first_hat = first_new / (1.0 - BETA_ONE**STEP)
    second_hat = second_new / (1.0 - BETA_TWO**STEP)
    master_new = master - step_rate * (
        first_hat / (jnp.sqrt(second_hat) + ADAM_EPS) + weight_decay * master
    )
    return (first_new, second_new, master_new)


def shards(
    tokens,
    cotangent,
    seq_lengths,
    slot_token,
    w_qkv,
    w_proj,
    w_inner,
    w_outer,
    norm_gains,
    norm_biases,
    qkv_first,
    qkv_second,
    proj_first,
    proj_second,
    inner_first,
    inner_second,
    outer_first,
    outer_second,
    norm_first,
    norm_second,
):
    side = lax.axis_index("ha")
    group = lax.axis_size("pb") * lax.axis_size("ka")
    rows, width = tokens.shape[1:]
    total = rows * group
    w_rows = w_qkv.shape[0]
    half_width = w_qkv.shape[2]
    heads = 2 * half_width // HD
    hidden_half = w_inner.shape[1]
    places = head_places(group, heads)
    head_at = [0] * group
    for h, place in enumerate(places):
        head_at[place] = h
    block = min(SCORE_BLOCK, total)

    def swap(a):
        return lax.ppermute(a, "ha", [(0, 1), (1, 0)])

    def ordered(own, other):
        return jnp.where(side == 0, own, other), jnp.where(side == 0, other, own)

    def own_micro(a):
        return lax.dynamic_index_in_dim(a, side, 0, False)

    def other_micro(a):
        return lax.dynamic_index_in_dim(a, 1 - side, 0, False)

    x = own_micro(tokens)
    along_z, along_ka = lax.axis_size("pb"), lax.axis_size("ka")
    stepped = along_z == 4 and along_ka == 4

    def flip(a, axis, size, bit):
        return lax.ppermute(a, axis, [(i, i ^ bit) for i in range(size)])

    if stepped:

        def z_flip(a, bit):
            return flip(a, "pb", along_z, bit)

        def x_flip(a):
            return flip(a, "ka", along_ka, 2)

        def c_flip(a):
            return flip(a, "ka", along_ka, 1)

        own = x[None]
        near, far, own_x, own_c = z_flip(own, 1), z_flip(own, 2), x_flip(own), c_flip(own)
    else:
        x_full = lax.all_gather(x, PLANE, axis=0, tiled=True)
    mine = jnp.concatenate(
        [w_qkv.astype(BF).reshape(w_rows, 3 * half_width), w_proj.astype(BF).T], axis=1
    )
    tok_row = own_micro(slot_token).reshape(1, total)
    mine_other, slot_row = swap(mine), slots_of_tokens(tok_row)
    if stepped:
        near, far = tie(near, far)
        mid_z = jnp.concatenate([near, far])
        last_z, mid_x, mid_c, own_xc = z_flip(far, 1), x_flip(mid_z), c_flip(mid_z), c_flip(own_x)
    low_half, high_half = ordered(mine, mine_other)
    qkv_rows = jnp.concatenate(
        [
            a[:, : 3 * half_width].reshape(w_rows, 3, heads // 2, HD).swapaxes(1, 2)
            for a in (low_half, high_half)
        ],
        axis=1,
    ).reshape(w_rows, heads, 3 * HD)
    proj_rows = jnp.concatenate(
        [a[:, 3 * half_width :] for a in (low_half, high_half)], axis=1
    )
    norm_master = jnp.concatenate([norm_gains, norm_biases], axis=0)
    head_rows = jnp.stack([qkv_rows[:, head_at[d]] for d in range(group)], axis=0)
    head_rows = jnp.concatenate(
        [
            head_rows,
            jnp.broadcast_to(norm_master.astype(BF).T[None], (group, w_rows, 4)),
            jnp.zeros((group, w_rows, HD - 4), BF),
        ],
        axis=2,
    )
    head_w = lax.all_to_all(head_rows, PLANE, 0, 0, tiled=True)
    ends = jnp.cumsum(own_micro(seq_lengths))
    starts = jnp.arange(total // block, dtype=jnp.int32) * block
    first_block = jnp.max(jnp.where(ends[None] <= starts[:, None], ends[None], 0), axis=1) // block
    last_block = jnp.min(jnp.where(ends[None] > starts[:, None], ends[None], total), axis=1) // block
    first_block = first_block.astype(jnp.int32)
    last_block = last_block.astype(jnp.int32)
    dy_own, dy_other = own_micro(cotangent), other_micro(cotangent)
    late_rows = qkv_rows.reshape(w_rows, -1)
    z, xc = lax.axis_index("pb"), lax.axis_index("ka")
    at_first = jnp.stack([z, 0 * z, xc // 2, xc % 2]).astype(jnp.int32)
    at_last = jnp.stack([z, 0 * z + 3, xc // 2, xc % 2]).astype(jnp.int32)
    ready = (dy_own, dy_other, late_rows, at_first, at_last, first_block, last_block, slot_row)
    if stepped:
        last_z, mid_x, mid_c, own_xc, head_w, *ready = tie(
            last_z, mid_x, mid_c, own_xc, head_w, *ready
        )
        last_x, last_c, mid_xc = x_flip(last_z), c_flip(last_z), c_flip(mid_x)
    else:
        head_w, *ready = tie(head_w, *ready)
    dy_own, dy_other, late_rows, at_first, at_last, first_block, last_block, slot_row = ready
    head_raw = head_w.reshape(width, 4 * HD)

    def turned(raw):
        return raw[:, : 3 * HD].T, raw[:, 3 * HD : 3 * HD + 4].astype(F32).T

    main_rows = jnp.concatenate(
        [
            w_inner.astype(BF),
            w_outer.astype(BF).T,
            proj_rows,
        ],
        axis=1,
    )
    if stepped:
        main_rows, mid_x = tie(main_rows, mid_x)
    else:
        main_rows, x_full = tie(main_rows, x_full)
    main_w = lax.all_gather(main_rows, PLANE, axis=0, tiled=True)
    proj_at = 2 * hidden_half // width

    if stepped:
        groups = ((own, own_x, own_c, own_xc), (mid_z, mid_x, mid_c, mid_xc))
        buffers = qkv_of_piece(at_first, groups, head_raw, total, ())
        last_x, last_c, *buffers = tie(last_x, last_c, *buffers)
        groups = ((last_z, last_x, last_c, c_flip(last_x)),)
        buffers = qkv_of_piece(at_last, groups, head_raw, total, buffers)
        unit, qkv = buffers
    else:
        unit, qkv = qkv_of_head(x_full, *turned(head_raw))
    q, qt, k, v, vt = sort_qkv(tok_row, qkv)
    o, o_low, lse = attend(first_block, qt, k, vt, block)
    late_rows, o_low = tie(late_rows, o_low)
    late_w = lax.all_gather(late_rows, PLANE, axis=0, tiled=True)
    o_packed, head_raw = tie(slots_out(slot_row, o_low, group), head_raw)
    o_packed = lax.all_to_all(o_packed, PLANE, 0, 0, tiled=True)
    head_w, norms = turned(head_raw)
    mid, h_own, o_own = middle(places, x, o_packed, main_w, proj_at, norms)
    h_other = swap(h_own)
    act_own, dpre_own, dh_own = hidden(h_own, dy_own, main_w, hidden_half, F32)
    h_other, dh_own = tie(h_other, dh_own)
    act_other, dpre_other, dh_send = hidden(h_other, dy_other, main_w, hidden_half, BF)
    dh_got = swap(dh_send)
    parity = (xc % 2).reshape(1).astype(jnp.int32)
    share = w_rows if stepped else 0
    halves = weight_grads(
        share, parity, (h_own, h_other), (dpre_own, dpre_other), (dy_own, dy_other), (act_own, act_other), width
    )
    dh_got, *halves = tie(dh_got, *halves)
    inner_halves, outer_halves = halves[:2], halves[2:]

    def pair_sum(halves, at):
        shape = (along_z, along_ka // 2, w_rows, halves[0].shape[1])
        parts = [lax.dynamic_index_in_dim(a.reshape(shape), at, 1, False) for a in halves]
        return parts[0].astype(F32) + parts[1].astype(F32)

    def scattered(halves, got):
        rest = (pair_sum(halves, xc // 2) + got.astype(F32)).astype(BF)
        return rest.reshape(-1, rest.shape[-1])

    if stepped:
        inner_halves = (inner_halves[0], c_flip(inner_halves[1]))
        inner_got = x_flip(pair_sum(inner_halves, 1 - xc // 2).astype(BF))

    dmid, dmid_low, g_packed, sums_two = middle_back(
        places, group, dh_own, dh_got, dy_own, mid, norms, main_w, proj_at
    )
    outer_halves = proj_grads(share, parity, dmid_low, o_own, *outer_halves)
    g_packed = lax.all_to_all(g_packed, PLANE, 0, 0, tiled=True)
    out_own, out_send = layer_terms(act_own, act_other, main_w)
    g_packed, out_own, out_send = tie(g_packed, out_own, out_send)
    if stepped:
        outer_halves = (outer_halves[0], c_flip(outer_halves[1]))
        outer_send = pair_sum(outer_halves, 1 - xc // 2).astype(BF)
        inner_rest = scattered(inner_halves, inner_got)
        outer_got = x_flip(outer_send)
    else:
        inner_sum = lax.psum_scatter(
            jnp.concatenate(inner_halves), PLANE, scatter_dimension=0, tiled=True
        )
    g, gt, delta = sort_grad(tok_row, g_packed, o)
    if stepped:
        g, inner_rest = tie(g, inner_rest)
        inner_sum = lax.psum_scatter(inner_rest, "pb", scatter_dimension=0, tiled=True)
    dqkv = attend_back(last_block, q, qt, k, v, g, gt, lse, delta, block)
    packed, dqkv_low = grads_out(slot_row, dqkv, group)
    if stepped:
        outer_rest = scattered(outer_halves, outer_got)
        dqkv_low, outer_rest, late_w, out_send, out_own, inner_sum = tie(
            dqkv_low, outer_rest, late_w, out_send, out_own, inner_sum
        )
    else:
        outer_sum = lax.psum_scatter(
            jnp.concatenate(outer_halves), PLANE, scatter_dimension=0, tiled=True
        )
    dqkv_own = lax.all_to_all(packed, PLANE, 0, 0, tiled=True)
    out_got = swap(out_send)
    layer_own = (mid + out_own + out_got.astype(F32)).astype(BF)
    layer_out = jnp.stack(ordered(layer_own, swap(layer_own)))

    head_grad = head_weight_grad(dqkv_low, unit, head_w, norms, sums_two)
    head_grad = head_grad.reshape(group, 2, w_rows // 2, 4 * HD)
    keep, send = ordered(head_grad[:, 0], head_grad[:, 1])
    keep = (keep.astype(F32) + swap(send).astype(F32)).astype(BF)
    keep, dqkv_own, layer_out = tie(keep, dqkv_own, layer_out)
    if stepped:
        dqkv_own, outer_rest = tie(dqkv_own, outer_rest)
        outer_sum = lax.psum_scatter(outer_rest, "pb", scatter_dimension=0, tiled=True)
    head_grad = lax.all_to_all(keep, PLANE, 0, 0, tiled=True)
    input_low = input_back(places, dqkv_own, late_w, x, dmid, norms)
    head_grad, outer_sum = tie(head_grad, outer_sum)
    input_grad = jnp.stack(ordered(input_low, swap(input_low))).astype(F32)

    norm_parts = head_grad[:, :, 3 * HD : 3 * HD + 8].astype(F32)
    norm_parts = norm_parts[:, :, :4] + norm_parts[:, :, 4:]
    first_sums = sum(norm_parts[place] for place in places)
    second_sums = jnp.sum(norm_parts, axis=0)
    norm_grad = jnp.stack(
        [first_sums[:, 0], second_sums[:, 1], first_sums[:, 2], second_sums[:, 3]]
    )
    norm_grad = jnp.concatenate(ordered(norm_grad, swap(norm_grad)), axis=1)
    qkv_part = jnp.stack([head_grad[place, :, : 3 * HD] for place in places], axis=1)
    qkv_part = qkv_part.reshape(w_rows // 2, 2, heads // 2, 3, HD)
    keep, send = ordered(qkv_part[:, 0], qkv_part[:, 1])
    qkv_grad = jnp.concatenate(ordered(keep, swap(send)), axis=0).astype(F32)
    qkv_grad = qkv_grad.swapaxes(1, 2).reshape(w_rows, 3, half_width)
    inner_grad = inner_sum.astype(F32)
    outer_grad = outer_sum[:, :hidden_half].astype(F32).T
    proj_part = outer_sum[:, hidden_half:]
    keep, send = ordered(proj_part[:, :half_width], proj_part[:, half_width:])
    proj_grad = (keep.astype(F32) + swap(send).astype(F32)).T

    qkv_out = adam_step(w_qkv, qkv_first, qkv_second, qkv_grad / MICRO, RATE_MATRIX, DECAY_RATE)
    proj_out = adam_step(w_proj, proj_first, proj_second, proj_grad / MICRO, RATE_PROJ, DECAY_RATE)
    inner_out = adam_step(
        w_inner, inner_first, inner_second, inner_grad / MICRO, RATE_MATRIX, DECAY_RATE
    )
    outer_out = adam_step(
        w_outer, outer_first, outer_second, outer_grad / MICRO, RATE_MATRIX, DECAY_RATE
    )
    norm_grad = norm_grad / MICRO
    norm_out = adam_step(norm_master, norm_first, norm_second, norm_grad, RATE_NORM, 0.0)
    norm_two_grad = jnp.stack([norm_grad[1], norm_grad[3]])
    return (
        layer_out,
        input_grad,
        *qkv_out,
        *proj_out,
        *inner_out,
        *outer_out,
        *norm_out,
        norm_two_grad,
    )


def solution(mesh):
    tok = P(None, PLANE, None)
    qkv = P(PLANE, None, "ha")
    down = P("ha", PLANE)
    inner = P(PLANE, "ha")
    norm = P(None, PLANE)
    in_specs = (
        (tok, tok, P(), P(), qkv, down, inner, down, norm, norm)
        + (qkv, qkv, down, down, inner, inner, down, down, norm, norm)
    )
    out_specs = (
        (tok, tok, qkv, qkv, qkv, down, down, down)
        + (inner, inner, inner, down, down, down, norm, norm, norm, norm)
    )
    return jax.shard_map(shards, mesh=mesh, in_specs=in_specs, out_specs=out_specs, check_vma=False)
```

```python
import functools

import jax
import jax.numpy as jnp
from jax import lax
from jax.experimental import pallas as pl
from jax.experimental.pallas import tpu as pltpu
from jax.sharding import PartitionSpec as P

HD = 64
MICRO = 2
STEP = 8
NORM_EPS = 1e-05
BETA_ONE = 0.9
BETA_TWO = 0.95
ADAM_EPS = 1e-08
DECAY_RATE = 0.1
RATE_MATRIX = 0.02
RATE_PROJ = 0.6
RATE_NORM = 0.1
BF = jnp.bfloat16
F32 = jnp.float32
PLANE = ("pb", "ka")
VMEM_LIMIT = 60 * 1024 * 1024
SCORE_BLOCK = 512
SHORT = 4096
STRAIGHT = 4
NT = (((1,), (1,)), ((), ()))
NN = (((1,), (0,)), ((), ()))
TN = (((0,), (0,)), ((), ()))


def dot(a, b, dims=NN):
    return lax.dot_general(a, b, dims, preferred_element_type=F32)


def params(steps=1):
    return pltpu.CompilerParams(
        dimension_semantics=("arbitrary",) * steps, vmem_limit_bytes=VMEM_LIMIT
    )


def cost(us):
    return pl.CostEstimate(flops=int(us * 2e8), bytes_accessed=int(us * 1e6), transcendentals=0)


def tie(*arrays):
    return lax.optimization_barrier(arrays)


def whole(shape):
    return pl.BlockSpec(shape, lambda *_: (0,) * len(shape))


def shape_of(shape, dtype):
    return jax.ShapeDtypeStruct(shape, dtype)


def head_places(group, heads):
    return tuple(h * group // heads for h in range(heads))


def normalize(x):
    center = x - jnp.mean(x, axis=-1, keepdims=True)
    spread = jnp.mean(center * center, axis=-1, keepdims=True)
    scale = lax.rsqrt(spread + NORM_EPS)
    return center * scale, scale


def normalize_back(grad, unit, scale):
    return scale * (
        grad
        - jnp.mean(grad, axis=-1, keepdims=True)
        - unit * jnp.mean(grad * unit, axis=-1, keepdims=True)
    )


def low_match(ids):
    low = lax.bitwise_and(ids, 255).astype(F32).astype(BF)
    line = lax.broadcasted_iota(jnp.int32, (256, 1), 0).astype(F32).astype(BF)
    return jnp.where(low == line, jnp.ones((), BF), jnp.zeros((), BF))


def moved(ids_ref, match_ref, source_ref, stack_ref, first):
    features = source_ref.shape[0]
    chunk = stack_ref.shape[1]
    total = None
    for part in range(source_ref.shape[1] // chunk):
        cut = slice(part * chunk, (part + 1) * chunk)
        high = lax.shift_right_logical(ids_ref[:, cut], 8)
        source = source_ref[:, cut]
        for block in range(stack_ref.shape[0] // features):
            stack_ref[block * features : (block + 1) * features, :] = jnp.where(
                high == first + block, source, jnp.zeros((), BF)
            )
        piece = dot(stack_ref[...], match_ref[:, cut], NT)
        total = piece if total is None else total + piece
    return total


def sort_block(total):
    return total if total <= SHORT else 1024


def stack_shape(features, columns, total):
    return pltpu.VMEM((features * columns // 256, min(3072, total)), BF)


def place_kernel(tok_ref, out_ref):
    total = tok_ref.shape[1]
    count = total // 256
    ids = tok_ref[...]
    high = lax.shift_right_logical(ids, 8)
    slot = lax.broadcasted_iota(jnp.int32, (1, total), 1)
    rows = lax.broadcasted_iota(jnp.int32, (count, 1), 0)
    match = low_match(ids)

    def part(values):
        picked = jnp.where(high == rows, values.astype(F32), 0.0).astype(BF)
        return dot(picked, match, NT)

    found = part(lax.shift_right_logical(slot, 8)) * 256.0 + part(lax.bitwise_and(slot, 255))
    found = found.astype(jnp.int32)
    for a in range(count):
        out_ref[:, a * 256 : (a + 1) * 256] = found[a : a + 1]


def slots_of_tokens(tok_row):
    return pl.pallas_call(
        place_kernel,
        grid=(1,),
        in_specs=[whole(tok_row.shape)],
        out_specs=whole(tok_row.shape),
        out_shape=shape_of(tok_row.shape, jnp.int32),
        compiler_params=params(),
        cost_estimate=cost(2),
        name="slots_of_tokens",
    )(tok_row)


def qkv_kernel(x_ref, w_ref, norm_ref, unit_ref, qkv_ref):
    unit, _ = normalize(x_ref[...].astype(F32))
    h = (unit * norm_ref[0:1, :] + norm_ref[2:3, :]).astype(BF)
    unit_ref[...] = unit.astype(BF)
    qkv_ref[...] = dot(w_ref[...], h, NT).astype(BF)


def qkv_piece_kernel(counts, at_ref, *refs):
    sources = refs[: 4 * len(counts)]
    raw_ref = refs[4 * len(counts)]
    unit_ref, qkv_ref, x_ref, w_ref, norm_ref = refs[-5:]

    @pl.when((pl.program_id(0) == 0) & (pl.program_id(1) == 0))
    def _():
        flat = raw_ref[...].astype(F32).T
        w_ref[...] = flat[: 3 * HD].astype(BF)
        norm_ref[...] = flat[3 * HD : 3 * HD + 8]

    rows = x_ref.shape[0] // 2
    even = at_ref[3] == 0
    slot = 0
    for group, count in enumerate(counts):
        for place in range(count):
            for side in range(2):

                @pl.when((pl.program_id(0) == slot) & (pl.program_id(1) == side))
                def _():
                    own = sources[4 * group + side][place]
                    other = sources[4 * group + 2 + side][place]
                    x_ref[:rows, :] = jnp.where(even, own, other)
                    x_ref[rows:, :] = jnp.where(even, other, own)

            slot += 1
    unit, _ = normalize(x_ref[...].astype(F32))
    h = (unit * norm_ref[0:1, :] + norm_ref[2:3, :]).astype(BF)
    unit_ref[...] = unit.astype(BF)
    qkv_ref[...] = dot(w_ref[...], h, NT).astype(BF)


def qkv_of_piece(at, groups, raw, total, buffers):
    counts = tuple(group[0].shape[0] for group in groups)
    pieces = [a for group in groups for a in group]
    _, rows, width = pieces[0].shape
    kept = [pl.BlockSpec(memory_space=pl.ANY)] * len(buffers)
    first = 1 + len(pieces) + 1

    def place(i, j, at):
        return (at[0] ^ (at[1] + i)) * 2 + (at[2] ^ j)

    return pl.pallas_call(
        functools.partial(qkv_piece_kernel, counts),
        grid_spec=pltpu.PrefetchScalarGridSpec(
            num_scalar_prefetch=1,
            grid=(sum(counts), 2),
            in_specs=[whole(a.shape) for a in (*pieces, raw)] + kept,
            out_specs=[
                pl.BlockSpec((2 * rows, width), lambda i, j, at: (place(i, j, at), 0)),
                pl.BlockSpec((3 * HD, 2 * rows), lambda i, j, at: (0, place(i, j, at))),
            ],
            scratch_shapes=[
                pltpu.VMEM((2 * rows, width), BF),
                pltpu.VMEM((3 * HD, width), BF),
                pltpu.VMEM((8, width), F32),
            ],
        ),
        out_shape=[shape_of((total, width), BF), shape_of((3 * HD, total), BF)],
        input_output_aliases={first: 0, first + 1: 1} if buffers else {},
        compiler_params=params(2),
        cost_estimate=cost(3 * sum(counts)),
        name="qkv_piece",
    )(at, *pieces, raw, *buffers)


def qkv_of_head(x_full, head_w, norms):
    rows, width = x_full.shape
    block = min(512, rows)
    return pl.pallas_call(
        qkv_kernel,
        grid=(rows // block,),
        in_specs=[
            pl.BlockSpec((block, width), lambda i: (i, 0)),
            whole(head_w.shape),
            whole(norms.shape),
        ],
        out_specs=[
            pl.BlockSpec((block, width), lambda i: (i, 0)),
            pl.BlockSpec((head_w.shape[0], block), lambda i: (0, i)),
        ],
        out_shape=[shape_of((rows, width), BF), shape_of((head_w.shape[0], rows), BF)],
        compiler_params=params(),
        cost_estimate=cost(8),
        name="qkv_head",
    )(x_full, head_w, norms)


def sort_kernel(tok_ref, qkv_ref, q_ref, qt_ref, k_ref, v_ref, vt_ref, match_ref, stack_ref):
    @pl.when(pl.program_id(0) == 0)
    def _():
        match_ref[...] = low_match(tok_ref[...])

    count = k_ref.shape[0] // 256
    found = moved(tok_ref, match_ref, qkv_ref, stack_ref, pl.program_id(0) * count)
    for part in range(count):
        cut = slice(part * 256, (part + 1) * 256)
        at = 3 * HD * part
        query = found[at : at + HD] * float(HD) ** -0.5
        value = found[at + 2 * HD : at + 3 * HD]
        qt_ref[:, cut] = query.astype(BF)
        q_ref[cut, :] = query.T.astype(BF)
        k_ref[cut, :] = found[at + HD : at + 2 * HD].T.astype(BF)
        v_ref[cut, :] = value.T.astype(BF)
        vt_ref[:, cut] = value.astype(BF)


def sort_qkv(tok_row, qkv):
    rows = qkv.shape[1]
    block = sort_block(rows)
    narrow = (pl.BlockSpec((block, HD), lambda i: (i, 0)), shape_of((rows, HD), BF))
    wide = (pl.BlockSpec((HD, block), lambda i: (0, i)), shape_of((HD, rows), BF))
    outs = (narrow, wide, narrow, narrow, wide)
    return pl.pallas_call(
        sort_kernel,
        grid=(rows // block,),
        in_specs=[whole(tok_row.shape), whole(qkv.shape)],
        out_specs=[spec for spec, _ in outs],
        out_shape=[shape for _, shape in outs],
        scratch_shapes=[pltpu.VMEM((256, rows), BF), stack_shape(3 * HD, block, rows)],
        compiler_params=params(),
        cost_estimate=cost(5),
        name="sort_qkv",
    )(tok_row, qkv)


def causal(keys, queries, ahead):
    return (
        lax.broadcasted_iota(jnp.int32, (keys, queries), 0)
        <= lax.broadcasted_iota(jnp.int32, (keys, queries), 1) + ahead
    )


def forward_kernel(first_ref, qt_ref, k_ref, vt_ref, o_ref, low_ref, lse_ref):
    block = qt_ref.shape[1]
    index = pl.program_id(0)
    half = block // 2

    def part(keys_at, count, query, state, ahead):
        top, total, acc = state
        scores = dot(k_ref[pl.ds(keys_at, count), :], query)
        square = scores * scores + 1.0
        inverse = lax.rsqrt(square)
        radius = square * inverse
        if ahead is not None:
            radius = jnp.where(causal(count, query.shape[1], ahead), radius, -1e30)
        new_top = jnp.maximum(top, jnp.max(radius, axis=0, keepdims=True))
        weights = jnp.exp(radius - new_top)
        shrink = jnp.exp(top - new_top)
        signed = (scores * inverse * weights).astype(BF)
        acc = acc * shrink + dot(vt_ref[:, pl.ds(keys_at, count)], signed)
        total = total * shrink + jnp.sum(weights, axis=0, keepdims=True)
        return (new_top, total, acc)

    def step(key_block, state):
        at = pl.multiple_of(key_block * block, block)
        return part(at, block, qt_ref[...], state, None)

    def diagonal():
        at = pl.multiple_of(index * block, block)
        empty = tuple(jnp.zeros((n, half), F32) for n in (1, 1, HD))
        low = part(at, half, qt_ref[:, :half], empty, 0)
        high = part(at, block, qt_ref[:, half:], empty, half)
        return tuple(jnp.concatenate([x, y], axis=1) for x, y in zip(low, high))

    def finish(state):
        top, total, acc = state
        out = acc * (1.0 / total)
        o_ref[...] = out
        low_ref[...] = out.astype(BF)
        lse_ref[...] = top + jnp.log(total)

    earlier = index - first_ref[index]
    for count in range(STRAIGHT):

        @pl.when(earlier == count)
        def _():
            state = diagonal()
            for back in range(1, count + 1):
                state = step(index - back, state)
            finish(state)

    @pl.when(earlier >= STRAIGHT)
    def _():
        finish(lax.fori_loop(first_ref[index], index, step, diagonal()))


def attend(first_block, qt, k, vt, block):
    rows = k.shape[0]
    return pl.pallas_call(
        forward_kernel,
        grid_spec=pltpu.PrefetchScalarGridSpec(
            num_scalar_prefetch=1,
            grid=(rows // block,),
            in_specs=[
                pl.BlockSpec((HD, block), lambda i, *_: (0, i)),
                whole(k.shape),
                whole(vt.shape),
            ],
            out_specs=[
                pl.BlockSpec((HD, block), lambda i, *_: (0, i)),
                pl.BlockSpec((HD, block), lambda i, *_: (0, i)),
                pl.BlockSpec((1, block), lambda i, *_: (0, i)),
            ],
        ),
        out_shape=[shape_of((HD, rows), F32), shape_of((HD, rows), BF), shape_of((1, rows), F32)],
        compiler_params=params(),
        cost_estimate=cost(13),
        name="attend_fwd",
    )(first_block, qt, k, vt)


def slots_out_kernel(rows, slot_ref, low_ref, out_ref, match_ref, stack_ref):
    half = rows // 2

    @pl.when(pl.program_id(0) == 0)
    def _():
        match_ref[...] = low_match(slot_ref[...])

    owners = out_ref.shape[0]
    count = owners * rows // 256
    found = moved(slot_ref, match_ref, low_ref, stack_ref, pl.program_id(0) * count)
    found = jnp.concatenate([found[p * HD : (p + 1) * HD].T for p in range(count)], axis=0)
    found = found.astype(BF)
    for d in range(owners):
        at = d * rows
        out_ref[d] = jnp.concatenate([found[at : at + half], found[at + half : at + rows]], axis=1)


def slots_out(slot_row, low, group):
    total = slot_row.shape[1]
    rows = total // group
    count = owners_per_step(group, rows)
    return pl.pallas_call(
        functools.partial(slots_out_kernel, rows),
        grid=(group // count,),
        in_specs=[whole(slot_row.shape), whole(low.shape)],
        out_specs=pl.BlockSpec((count, rows // 2, 2 * HD), lambda i: (i, 0, 0)),
        out_shape=shape_of((group, rows // 2, 2 * HD), BF),
        scratch_shapes=[pltpu.VMEM((256, total), BF), stack_shape(HD, count * rows, total)],
        compiler_params=params(),
        cost_estimate=cost(3),
        name="slots_out",
    )(slot_row, low)


def owners_per_step(group, rows, most=16):
    for count in (16, 8, 4, 2, 1):
        if count > (most if group * rows <= SHORT else 4):
            continue
        if group % count == 0 and count * rows % 256 == 0:
            return count
    return group


def sort_grad_kernel(
    tok_ref, packed_ref, o_ref, g_ref, gt_ref, delta_ref, slots_ref, match_ref, stack_ref
):
    group, half, _ = packed_ref.shape

    @pl.when(pl.program_id(0) == 0)
    def _():
        match_ref[...] = low_match(tok_ref[...])
        for d in range(group):
            piece = packed_ref[d].astype(F32).T.astype(BF)
            slots_ref[:, 2 * d * half : (2 * d + 1) * half] = piece[:HD]
            slots_ref[:, (2 * d + 1) * half : (2 * d + 2) * half] = piece[HD:]

    count = g_ref.shape[0] // 256
    found = moved(tok_ref, match_ref, slots_ref, stack_ref, pl.program_id(0) * count)
    for part in range(count):
        cut = slice(part * 256, (part + 1) * 256)
        grad = found[part * HD : (part + 1) * HD]
        gt_ref[:, cut] = grad.astype(BF)
        g_ref[cut, :] = grad.T.astype(BF)
        delta_ref[:, cut] = jnp.sum(grad * o_ref[:, cut], axis=0, keepdims=True)


def sort_grad(tok_row, packed, o):
    rows = o.shape[1]
    block = sort_block(rows)
    wide = pl.BlockSpec((HD, block), lambda i: (0, i))
    return pl.pallas_call(
        sort_grad_kernel,
        grid=(rows // block,),
        in_specs=[whole(tok_row.shape), whole(packed.shape), wide],
        out_specs=[
            pl.BlockSpec((block, HD), lambda i: (i, 0)),
            wide,
            pl.BlockSpec((1, block), lambda i: (0, i)),
        ],
        out_shape=[shape_of((rows, HD), BF), shape_of((HD, rows), BF), shape_of((1, rows), F32)],
        scratch_shapes=[
            pltpu.VMEM((HD, rows), BF),
            pltpu.VMEM((256, rows), BF),
            stack_shape(HD, block, rows),
        ],
        compiler_params=params(),
        cost_estimate=cost(4),
        name="sort_grad",
    )(tok_row, packed, o)


def backward_kernel(
    last_ref, q_ref, qt_ref, k_ref, v_ref, g_ref, gt_ref, lse_ref, delta_ref, out_ref, dq_ref, dk_ref, dv_ref
):
    block = k_ref.shape[0]
    index = pl.program_id(0)

    @pl.when(index == 0)
    def _():
        dq_ref[...] = jnp.zeros_like(dq_ref)

    key = k_ref[...]
    key_t = key.astype(F32).T.astype(BF)
    value = v_ref[...]

    half = block // 2

    def part(at, width, count, ahead):
        cut = pl.ds(at, width)
        scores = dot(key[:count], qt_ref[:, cut])
        square = scores * scores + 1.0
        inverse = lax.rsqrt(square)
        shifted = square * inverse - lse_ref[:, cut]
        if ahead is not None:
            shifted = jnp.where(causal(count, width, ahead), shifted, -1e30)
        weights = jnp.exp(shifted)
        slope = scores * inverse
        along = dot(value[:count], gt_ref[:, cut])
        bend = 1.0 + inverse * inverse * (inverse - 1.0)
        score_grad = weights * (bend * along - slope * delta_ref[:, cut])
        signed = (slope * weights).astype(BF)
        low_grad = score_grad.astype(BF)
        dv = dot(signed, g_ref[cut, :])
        dk = dot(low_grad, q_ref[cut, :])
        dq_ref[:, cut] += dot(key_t[:, :count], low_grad)
        return dk, dv

    def step(query_block):
        return part(pl.multiple_of(query_block * block, block), block, block, None)

    def diagonal():
        at = pl.multiple_of(index * block, block)
        low = part(at, half, half, 0)
        high = part(pl.multiple_of(at + half, half), half, block, half)
        return tuple(jnp.concatenate([x + y[:half], y[half:]], axis=0) for x, y in zip(low, high))

    def finish(dk, dv):
        at = pl.multiple_of(index * block, block)
        out_ref[:HD] = (dq_ref[:, pl.ds(at, block)] * float(HD) ** -0.5).astype(BF)
        out_ref[HD : 2 * HD] = dk.T.astype(BF)
        out_ref[2 * HD :] = dv.T.astype(BF)

    later = last_ref[index] - index
    for count in range(1, STRAIGHT + 1):

        @pl.when(later == count)
        def _():
            dk, dv = diagonal()
            for ahead in range(1, count):
                dk_more, dv_more = step(index + ahead)
                dk, dv = dk + dk_more, dv + dv_more
            finish(dk, dv)

    @pl.when(later > STRAIGHT)
    def _():
        dk_ref[...], dv_ref[...] = diagonal()

        def body(query_block, carry):
            dk_more, dv_more = step(query_block)
            dk_ref[...] += dk_more
            dv_ref[...] += dv_more
            return carry

        lax.fori_loop(index + 1, last_ref[index], body, 0)
        finish(dk_ref[...], dv_ref[...])


def attend_back(last_block, q, qt, k, v, g, gt, lse, delta, block):
    rows = q.shape[0]
    return pl.pallas_call(
        backward_kernel,
        grid_spec=pltpu.PrefetchScalarGridSpec(
            num_scalar_prefetch=1,
            grid=(rows // block,),
            in_specs=[
                whole(q.shape),
                whole(qt.shape),
                pl.BlockSpec((block, HD), lambda i, *_: (i, 0)),
                pl.BlockSpec((block, HD), lambda i, *_: (i, 0)),
                whole(g.shape),
                whole(gt.shape),
                whole(lse.shape),
                whole(delta.shape),
            ],
            out_specs=pl.BlockSpec((3 * HD, block), lambda i, *_: (0, i)),
            scratch_shapes=[
                pltpu.VMEM((HD, rows), F32),
                pltpu.VMEM((block, HD), F32),
                pltpu.VMEM((block, HD), F32),
            ],
        ),
        out_shape=shape_of((3 * HD, rows), BF),
        compiler_params=params(),
        cost_estimate=cost(19),
        name="attend_bwd",
    )(last_block, q, qt, k, v, g, gt, lse, delta)


def head_results(acc, column, w_ref, norm_ref, sums_ref):
    weights = w_ref[...].astype(F32)
    grad = acc * norm_ref[0:1, :] + column * norm_ref[2:3, :]
    sums = jnp.concatenate(
        [
            jnp.sum(weights * acc, axis=0, keepdims=True),
            sums_ref[0:1, :],
            jnp.sum(weights * column, axis=0, keepdims=True),
            sums_ref[1:2, :],
        ],
        axis=0,
    )
    top = sums.astype(BF).astype(F32)
    rest = jnp.concatenate([top, sums - top, jnp.zeros((HD - 8, sums.shape[1]), F32)], axis=0)
    return jnp.concatenate([grad, rest], axis=0).T.astype(BF)


def grads_out_kernel(rows, slot_ref, grad_ref, out_ref, low_ref, match_ref, stack_ref):
    half = rows // 2
    step = pl.program_id(0)

    @pl.when(step == 0)
    def _():
        match_ref[...] = low_match(slot_ref[...])

    count = out_ref.shape[0]
    parts = count * rows // 256
    found = moved(slot_ref, match_ref, grad_ref, stack_ref, step * parts)
    turned = []
    for p in range(parts):
        piece = found[3 * HD * p : 3 * HD * (p + 1)]
        low_ref[:, p * 256 : (p + 1) * 256] = piece.astype(BF)
        turned.append(piece.T)
    turned = jnp.concatenate(turned, axis=0).astype(BF)
    for d in range(count):
        at = d * rows
        out_ref[d, :rows, :] = turned[at : at + rows, : 2 * HD]
        out_ref[d, rows:, :] = jnp.concatenate(
            [turned[at : at + half, 2 * HD :], turned[at + half : at + rows, 2 * HD :]], axis=1
        )


def grads_out(slot_row, grads, group):
    total = slot_row.shape[1]
    rows = total // group
    out_rows = rows + rows // 2
    count = owners_per_step(group, rows, 8)
    return pl.pallas_call(
        functools.partial(grads_out_kernel, rows),
        grid=(group // count,),
        in_specs=[whole(slot_row.shape), whole(grads.shape)],
        out_specs=[
            pl.BlockSpec((count, out_rows, 2 * HD), lambda i: (i, 0, 0)),
            pl.BlockSpec((3 * HD, count * rows), lambda i: (0, i)),
        ],
        out_shape=[shape_of((group, out_rows, 2 * HD), BF), shape_of((3 * HD, total), BF)],
        scratch_shapes=[
            pltpu.VMEM((256, total), BF),
            stack_shape(3 * HD, count * rows, total),
        ],
        compiler_params=params(),
        cost_estimate=cost(7),
        name="grads_out",
    )(slot_row, grads)


def head_weight_kernel(grad_ref, unit_ref, w_ref, norm_ref, sums_ref, head_ref, acc_ref, line_ref):
    step = pl.program_id(0)
    term = dot(grad_ref[...], unit_ref[...])
    line = jnp.sum(grad_ref[...].astype(F32), axis=1, keepdims=True)

    @pl.when(step == 0)
    def _():
        acc_ref[...] = term
        line_ref[...] = line

    @pl.when(step > 0)
    def _():
        acc_ref[...] += term
        line_ref[...] += line

    @pl.when(step == pl.num_programs(0) - 1)
    def _():
        head_ref[...] = head_results(acc_ref[...], line_ref[...], w_ref, norm_ref, sums_ref)


def head_weight_grad(grads, unit, head_w, norms, sums_two):
    total, width = unit.shape
    block = 768 if total % 768 == 0 else total
    return pl.pallas_call(
        head_weight_kernel,
        grid=(total // block,),
        in_specs=[
            pl.BlockSpec((3 * HD, block), lambda i: (0, i)),
            pl.BlockSpec((block, width), lambda i: (i, 0)),
            whole(head_w.shape),
            whole(norms.shape),
            whole(sums_two.shape),
        ],
        out_specs=whole((width, 4 * HD)),
        out_shape=shape_of((width, 4 * HD), BF),
        scratch_shapes=[pltpu.VMEM((3 * HD, width), F32), pltpu.VMEM((3 * HD, 1), F32)],
        compiler_params=params(),
        cost_estimate=cost(5),
        name="head_weight",
    )(grads, unit, head_w, norms, sums_two)


def middle_kernel(places, x_ref, packed_ref, proj_ref, norm_ref, mid_ref, h_ref, o_ref):
    half = packed_ref.shape[1]
    for h, place in enumerate(places):
        piece = packed_ref[place]
        o_ref[:half, h * HD : (h + 1) * HD] = piece[:, :HD]
        o_ref[half:, h * HD : (h + 1) * HD] = piece[:, HD:]
    mid = x_ref[...].astype(F32) + dot(o_ref[...], proj_ref[...], NT)
    mid_ref[...] = mid
    unit, _ = normalize(mid)
    h_ref[...] = (unit * norm_ref[1:2, :] + norm_ref[3:4, :]).astype(BF)


def middle(places, x, packed, weights, proj_at, norms):
    rows, width = x.shape
    return pl.pallas_call(
        functools.partial(middle_kernel, places),
        grid=(1,),
        in_specs=[
            whole(x.shape),
            whole(packed.shape),
            pl.BlockSpec((width, width), lambda i: (0, proj_at)),
            whole(norms.shape),
        ],
        out_specs=[whole((rows, width))] * 3,
        out_shape=[
            shape_of((rows, width), F32),
            shape_of((rows, width), BF),
            shape_of((rows, width), BF),
        ],
        compiler_params=params(),
        cost_estimate=cost(3),
        name="middle",
    )(x, packed, weights, norms)


def hidden_kernel(h_ref, dy_ref, inner_ref, outer_ref, act_ref, dpre_ref, dh_ref, dh_acc):
    pre = dot(h_ref[...], inner_ref[...])
    root = 0.7978845608028654
    squared = pre * pre
    bend = jnp.tanh(root * (pre + 0.044715 * (squared * pre)))
    act_ref[...] = (0.5 * pre * (1.0 + bend)).astype(BF)
    slope = 0.5 * (1.0 + bend) + 0.5 * pre * (1.0 - bend * bend) * (
        root * (1.0 + 3.0 * 0.044715 * squared)
    )
    dpre = (dot(dy_ref[...], outer_ref[...]) * slope).astype(BF)
    dpre_ref[...] = dpre
    dh = dot(dpre, inner_ref[...], NT)

    @pl.when(pl.program_id(0) == 0)
    def _():
        dh_acc[...] = dh

    @pl.when(pl.program_id(0) > 0)
    def _():
        dh_acc[...] += dh

    @pl.when(pl.program_id(0) == pl.num_programs(0) - 1)
    def _():
        dh_ref[...] = dh_acc[...].astype(dh_ref.dtype)


def hidden(h, dy, weights, hidden_width, kind):
    rows, width = h.shape
    chunk = 512
    steps = hidden_width // chunk
    return pl.pallas_call(
        hidden_kernel,
        grid=(steps,),
        in_specs=[
            whole(h.shape),
            whole(dy.shape),
            pl.BlockSpec((width, chunk), lambda i: (0, i)),
            pl.BlockSpec((width, chunk), lambda i: (0, i + steps)),
        ],
        out_specs=[
            pl.BlockSpec((rows, chunk), lambda i: (0, i)),
            pl.BlockSpec((rows, chunk), lambda i: (0, i)),
            whole((rows, width)),
        ],
        out_shape=[
            shape_of((rows, hidden_width), BF),
            shape_of((rows, hidden_width), BF),
            shape_of((rows, width), kind),
        ],
        scratch_shapes=[pltpu.VMEM((rows, width), F32)],
        compiler_params=params(),
        cost_estimate=cost(6),
        name="hidden",
    )(h, dy, weights, weights)


def layer_kernel(own_ref, other_ref, outer_ref, out_ref, send_ref):
    out_ref[...] = dot(own_ref[...], outer_ref[...], NT)
    send_ref[...] = dot(other_ref[...], outer_ref[...], NT).astype(BF)


def layer_terms(act_own, act_other, weights):
    rows, span = act_own.shape
    width = weights.shape[0]
    return pl.pallas_call(
        layer_kernel,
        grid=(1,),
        in_specs=[
            whole(act_own.shape),
            whole(act_other.shape),
            pl.BlockSpec((width, span), lambda i: (0, 1)),
        ],
        out_specs=[whole((rows, width))] * 2,
        out_shape=[shape_of((rows, width), F32), shape_of((rows, width), BF)],
        compiler_params=params(),
        cost_estimate=cost(4),
        name="layer_terms",
    )(act_own, act_other, weights)


def middle_back_kernel(
    places, own_ref, other_ref, dy_ref, mid_ref, norm_ref, proj_ref, dmid_ref, low_ref, packed_ref, sums_ref
):
    half = packed_ref.shape[1]
    dh = own_ref[...] + other_ref[...].astype(F32)
    unit, scale = normalize(mid_ref[...])
    sums_ref[0:1, :] = jnp.sum(dh * unit, axis=0, keepdims=True)
    sums_ref[1:2, :] = jnp.sum(dh, axis=0, keepdims=True)
    dmid = dy_ref[...].astype(F32) + normalize_back(dh * norm_ref[1:2, :], unit, scale)
    dmid_ref[...] = dmid
    low = dmid.astype(BF)
    low_ref[...] = low
    grad = dot(low, proj_ref[...]).astype(BF)
    packed_ref[...] = jnp.zeros_like(packed_ref)
    for h, place in enumerate(places):
        cut = slice(h * HD, (h + 1) * HD)
        packed_ref[place] = jnp.concatenate([grad[:half, cut], grad[half:, cut]], axis=1)


def middle_back(places, group, own, other, dy, mid, norms, weights, proj_at):
    rows, width = mid.shape
    return pl.pallas_call(
        functools.partial(middle_back_kernel, places),
        grid=(1,),
        in_specs=[
            whole(own.shape),
            whole(other.shape),
            whole(dy.shape),
            whole(mid.shape),
            whole(norms.shape),
            pl.BlockSpec((width, width), lambda i: (0, proj_at)),
        ],
        out_specs=[
            whole((rows, width)),
            whole((rows, width)),
            whole((group, rows // 2, 2 * HD)),
            whole((2, width)),
        ],
        out_shape=[
            shape_of((rows, width), F32),
            shape_of((rows, width), BF),
            shape_of((group, rows // 2, 2 * HD), BF),
            shape_of((2, width), F32),
        ],
        compiler_params=params(),
        cost_estimate=cost(4),
        name="middle_back",
    )(own, other, dy, mid, norms, weights)


def split_rows(share, at_ref, block, scratch_ref, keep_ref, send_ref):
    if share == 0:
        half = keep_ref.shape[0]
        keep_ref[...] = block[:half].astype(BF)
        send_ref[...] = block[half:].astype(BF)
        return
    scratch_ref[...] = block
    for pair in range(keep_ref.shape[0] // share):
        cut = slice(pair * share, (pair + 1) * share)
        for target, parity in ((keep_ref, at_ref[0]), (send_ref, 1 - at_ref[0])):
            at = pl.multiple_of((2 * pair + parity) * share, share)
            target[cut, :] = scratch_ref[pl.ds(at, share), :].astype(BF)


def weight_kernel(
    span, share, at_ref, h0, h1, p0, p1, dy0, dy1, a0, a1, keep_in, send_in, keep_out, send_out, scratch_ref
):
    index = pl.program_id(0)

    @pl.when(index < span)
    def _():
        block = dot(h0[...], p0[...], TN) + dot(h1[...], p1[...], TN)
        split_rows(share, at_ref, block, scratch_ref, keep_in, send_in)

    @pl.when(index >= span)
    def _():
        block = dot(dy0[...], a0[...], TN) + dot(dy1[...], a1[...], TN)
        split_rows(share, at_ref, block, scratch_ref, keep_out, send_out)


def weight_grads(share, parity, h_pair, dpre_pair, dy_pair, act_pair, spare):
    rows, width = h_pair[0].shape
    span = act_pair[0].shape[1] // width

    def first(i, at):
        return (0, jnp.minimum(i, span - 1))

    def second(i, at):
        return (0, jnp.maximum(i - span, 0))

    def column(count, where):
        return pl.BlockSpec((count, width), where)

    plain = whole((rows, width))
    half = width // 2
    inner = shape_of((half, span * width), BF)
    outer = shape_of((half, span * width + spare), BF)
    return pl.pallas_call(
        functools.partial(weight_kernel, span, share),
        grid_spec=pltpu.PrefetchScalarGridSpec(
            num_scalar_prefetch=1,
            grid=(2 * span,),
            in_specs=[plain, plain, column(rows, first), column(rows, first)]
            + [plain, plain, column(rows, second), column(rows, second)],
            out_specs=[column(half, first)] * 2 + [column(half, second)] * 2,
            scratch_shapes=[pltpu.VMEM((width, width), F32)],
        ),
        out_shape=[inner, inner, outer, outer],
        compiler_params=params(),
        cost_estimate=cost(8),
        name="weight_grads",
    )(parity, *h_pair, *dpre_pair, *dy_pair, *act_pair)


def proj_kernel(share, at_ref, low_ref, o_ref, kept_ref, sent_ref, keep_ref, send_ref, scratch_ref):
    block = dot(low_ref[...], o_ref[...], TN)
    split_rows(share, at_ref, block, scratch_ref, keep_ref, send_ref)


def proj_grads(share, parity, low, o, keep, send):
    width = o.shape[1]
    last = keep.shape[1] // width - 1
    return pl.pallas_call(
        functools.partial(proj_kernel, share),
        grid_spec=pltpu.PrefetchScalarGridSpec(
            num_scalar_prefetch=1,
            grid=(1,),
            in_specs=[whole(low.shape), whole(o.shape)] + [pl.BlockSpec(memory_space=pl.ANY)] * 2,
            out_specs=[pl.BlockSpec((width // 2, width), lambda i, at: (0, last))] * 2,
            scratch_shapes=[pltpu.VMEM((width, width), F32)],
        ),
        out_shape=[shape_of(keep.shape, BF)] * 2,
        input_output_aliases={3: 0, 4: 1},
        compiler_params=params(),
        cost_estimate=cost(2),
        name="proj_grads",
    )(parity, low, o, keep, send)


def input_back_kernel(places, side_ref, packed_ref, own_ref, other_ref, x_ref, dmid_ref, norm_ref, out_ref, flat_ref):
    rows, _ = x_ref.shape
    half = rows // 2
    for h, place in enumerate(places):
        at = 3 * HD * h
        piece = packed_ref[place]
        flat_ref[:, at : at + 2 * HD] = piece[:rows]
        flat_ref[:half, at + 2 * HD : at + 3 * HD] = piece[rows:, :HD]
        flat_ref[half:, at + 2 * HD : at + 3 * HD] = piece[rows:, HD:]
    span = own_ref.shape[1]
    low, high = flat_ref[:, :span], flat_ref[:, span:]
    first = side_ref[0] == 0
    dh = dot(jnp.where(first, low, high), own_ref[...], NT)
    dh += dot(jnp.where(first, high, low), other_ref[...], NT)
    unit, scale = normalize(x_ref[...].astype(F32))
    out_ref[...] = (dmid_ref[...] + normalize_back(dh * norm_ref[0:1, :], unit, scale)).astype(BF)


def input_back(places, side, packed, own, other, x, dmid, norms):
    rows, width = x.shape
    arrays = (packed, own, other, x, dmid, norms)
    return pl.pallas_call(
        functools.partial(input_back_kernel, places),
        grid_spec=pltpu.PrefetchScalarGridSpec(
            num_scalar_prefetch=1,
            grid=(1,),
            in_specs=[whole(a.shape) for a in arrays],
            out_specs=whole((rows, width)),
            scratch_shapes=[pltpu.VMEM((rows, 3 * HD * len(places)), BF)],
        ),
        out_shape=shape_of((rows, width), BF),
        compiler_params=params(),
        cost_estimate=cost(5),
        name="input_back",
    )(side, *arrays)


def adam_step(master, first_state, second_state, grad_term, step_rate, weight_decay):
    first_new = BETA_ONE * first_state + (1.0 - BETA_ONE) * grad_term
    second_new = BETA_TWO * second_state + (1.0 - BETA_TWO) * grad_term * grad_term
    first_hat = first_new / (1.0 - BETA_ONE**STEP)
    second_hat = second_new / (1.0 - BETA_TWO**STEP)
    master_new = master - step_rate * (
        first_hat / (jnp.sqrt(second_hat) + ADAM_EPS) + weight_decay * master
    )
    return (first_new, second_new, master_new)


def shards(
    tokens,
    cotangent,
    seq_lengths,
    slot_token,
    w_qkv,
    w_proj,
    w_inner,
    w_outer,
    norm_gains,
    norm_biases,
    qkv_first,
    qkv_second,
    proj_first,
    proj_second,
    inner_first,
    inner_second,
    outer_first,
    outer_second,
    norm_first,
    norm_second,
):
    side = lax.axis_index("ha")
    group = lax.axis_size("pb") * lax.axis_size("ka")
    rows, width = tokens.shape[1:]
    total = rows * group
    w_rows = w_qkv.shape[0]
    half_width = w_qkv.shape[2]
    heads = 2 * half_width // HD
    hidden_half = w_inner.shape[1]
    places = head_places(group, heads)
    head_at = [0] * group
    for h, place in enumerate(places):
        head_at[place] = h
    block = min(SCORE_BLOCK, total)

    def swap(a):
        return lax.ppermute(a, "ha", [(0, 1), (1, 0)])

    def ordered(own, other):
        return jnp.where(side == 0, own, other), jnp.where(side == 0, other, own)

    def own_micro(a):
        return lax.dynamic_index_in_dim(a, side, 0, False)

    def other_micro(a):
        return lax.dynamic_index_in_dim(a, 1 - side, 0, False)

    x = own_micro(tokens)
    along_z, along_ka = lax.axis_size("pb"), lax.axis_size("ka")
    stepped = along_z == 4 and along_ka == 4

    def flip(a, axis, size, bit):
        return lax.ppermute(a, axis, [(i, i ^ bit) for i in range(size)])

    if stepped:

        def z_flip(a, bit):
            return flip(a, "pb", along_z, bit)

        def x_flip(a):
            return flip(a, "ka", along_ka, 2)

        def c_flip(a):
            return flip(a, "ka", along_ka, 1)

        own = x[None]
        near, far, own_x, own_c = z_flip(own, 1), z_flip(own, 2), x_flip(own), c_flip(own)
    else:
        x_full = lax.all_gather(x, PLANE, axis=0, tiled=True)
    mine = jnp.concatenate(
        [w_qkv.astype(BF).reshape(w_rows, 3 * half_width), w_proj.astype(BF).T], axis=1
    )
    tok_row = own_micro(slot_token).reshape(1, total)
    mine_other, slot_row = swap(mine), slots_of_tokens(tok_row)
    if stepped:
        near, far = tie(near, far)
        mid_z = jnp.concatenate([near, far])
        last_z, mid_x, mid_c, own_xc = z_flip(far, 1), x_flip(mid_z), c_flip(mid_z), c_flip(own_x)
    low_half, high_half = ordered(mine, mine_other)
    qkv_rows = jnp.concatenate(
        [
            a[:, : 3 * half_width].reshape(w_rows, 3, heads // 2, HD).swapaxes(1, 2)
            for a in (low_half, high_half)
        ],
        axis=1,
    ).reshape(w_rows, heads, 3 * HD)
    proj_rows = jnp.concatenate(
        [a[:, 3 * half_width :] for a in (low_half, high_half)], axis=1
    )
    norm_master = jnp.concatenate([norm_gains, norm_biases], axis=0)
    head_rows = jnp.stack([qkv_rows[:, head_at[d]] for d in range(group)], axis=0)
    head_rows = jnp.concatenate(
        [
            head_rows,
            jnp.broadcast_to(norm_master.astype(BF).T[None], (group, w_rows, 4)),
            jnp.zeros((group, w_rows, HD - 4), BF),
        ],
        axis=2,
    )
    head_w = lax.all_to_all(head_rows, PLANE, 0, 0, tiled=True)
    ends = jnp.cumsum(own_micro(seq_lengths))
    starts = jnp.arange(total // block, dtype=jnp.int32) * block
    first_block = jnp.max(jnp.where(ends[None] <= starts[:, None], ends[None], 0), axis=1) // block
    last_block = jnp.min(jnp.where(ends[None] > starts[:, None], ends[None], total), axis=1) // block
    first_block = first_block.astype(jnp.int32)
    last_block = last_block.astype(jnp.int32)
    dy_own, dy_other = own_micro(cotangent), other_micro(cotangent)
    late_rows = jnp.where(side == 0, qkv_rows[:, : heads // 2], qkv_rows[:, heads // 2 :])
    late_rows = late_rows.reshape(w_rows, -1)
    z, xc = lax.axis_index("pb"), lax.axis_index("ka")
    at_first = jnp.stack([z, 0 * z, xc // 2, xc % 2]).astype(jnp.int32)
    at_last = jnp.stack([z, 0 * z + 3, xc // 2, xc % 2]).astype(jnp.int32)
    ready = (dy_own, dy_other, late_rows, at_first, at_last, first_block, last_block, slot_row)
    if stepped:
        last_z, mid_x, mid_c, own_xc, head_w, *ready = tie(
            last_z, mid_x, mid_c, own_xc, head_w, *ready
        )
        last_x, last_c, mid_xc = x_flip(last_z), c_flip(last_z), c_flip(mid_x)
    else:
        head_w, *ready = tie(head_w, *ready)
    dy_own, dy_other, late_rows, at_first, at_last, first_block, last_block, slot_row = ready
    head_raw = head_w.reshape(width, 4 * HD)

    def turned(raw):
        return raw[:, : 3 * HD].T, raw[:, 3 * HD : 3 * HD + 4].astype(F32).T

    main_rows = jnp.concatenate(
        [
            w_inner.astype(BF),
            w_outer.astype(BF).T,
            proj_rows,
        ],
        axis=1,
    )
    if stepped:
        main_rows, mid_x = tie(main_rows, mid_x)
    else:
        main_rows, x_full = tie(main_rows, x_full)
    main_w = lax.all_gather(main_rows, PLANE, axis=0, tiled=True)
    proj_at = 2 * hidden_half // width

    if stepped:
        groups = ((own, own_x, own_c, own_xc), (mid_z, mid_x, mid_c, mid_xc))
        buffers = qkv_of_piece(at_first, groups, head_raw, total, ())
        last_x, last_c, *buffers = tie(last_x, last_c, *buffers)
        groups = ((last_z, last_x, last_c, c_flip(last_x)),)
        buffers = qkv_of_piece(at_last, groups, head_raw, total, buffers)
        unit, qkv = buffers
    else:
        unit, qkv = qkv_of_head(x_full, *turned(head_raw))
    q, qt, k, v, vt = sort_qkv(tok_row, qkv)
    o, o_low, lse = attend(first_block, qt, k, vt, block)
    late_rows, o_low = tie(late_rows, o_low)
    late_half = lax.all_gather(late_rows, PLANE, axis=0, tiled=True)
    o_packed, head_raw = tie(slots_out(slot_row, o_low, group), head_raw)
    o_packed = lax.all_to_all(o_packed, PLANE, 0, 0, tiled=True)
    head_w, norms = turned(head_raw)
    mid, h_own, o_own = middle(places, x, o_packed, main_w, proj_at, norms)
    h_other = swap(h_own)
    act_own, dpre_own, dh_own = hidden(h_own, dy_own, main_w, hidden_half, F32)
    h_other, dh_own = tie(h_other, dh_own)
    act_other, dpre_other, dh_send = hidden(h_other, dy_other, main_w, hidden_half, BF)
    dh_got = swap(dh_send)
    parity = (xc % 2).reshape(1).astype(jnp.int32)
    side_at = side.reshape(1).astype(jnp.int32)
    share = w_rows if stepped else 0
    halves = weight_grads(
        share, parity, (h_own, h_other), (dpre_own, dpre_other), (dy_own, dy_other), (act_own, act_other), width
    )
    dh_got, *halves = tie(dh_got, *halves)
    inner_halves, outer_halves = halves[:2], halves[2:]

    def pair_sum(halves, at):
        shape = (along_z, along_ka // 2, w_rows, halves[0].shape[1])
        parts = [lax.dynamic_index_in_dim(a.reshape(shape), at, 1, False) for a in halves]
        return parts[0].astype(F32) + parts[1].astype(F32)

    def scattered(halves, got):
        rest = (pair_sum(halves, xc // 2) + got.astype(F32)).astype(BF)
        return rest.reshape(-1, rest.shape[-1])

    if stepped:
        inner_halves = (inner_halves[0], c_flip(inner_halves[1]))
        inner_got = x_flip(pair_sum(inner_halves, 1 - xc // 2).astype(BF))

    dmid, dmid_low, g_packed, sums_two = middle_back(
        places, group, dh_own, dh_got, dy_own, mid, norms, main_w, proj_at
    )
    outer_halves = proj_grads(share, parity, dmid_low, o_own, *outer_halves)
    g_packed = lax.all_to_all(g_packed, PLANE, 0, 0, tiled=True)
    out_own, out_send = layer_terms(act_own, act_other, main_w)
    g_packed, out_own, out_send = tie(g_packed, out_own, out_send)
    if stepped:
        outer_halves = (outer_halves[0], c_flip(outer_halves[1]))
        outer_send = pair_sum(outer_halves, 1 - xc // 2).astype(BF)
        inner_rest = scattered(inner_halves, inner_got)
        outer_got = x_flip(outer_send)
    else:
        inner_sum = lax.psum_scatter(
            jnp.concatenate(inner_halves), PLANE, scatter_dimension=0, tiled=True
        )
    g, gt, delta = sort_grad(tok_row, g_packed, o)
    g, late_half = tie(g, late_half)
    late_w = swap(late_half)
    if stepped:
        g, inner_rest = tie(g, inner_rest)
        inner_sum = lax.psum_scatter(inner_rest, "pb", scatter_dimension=0, tiled=True)
    dqkv = attend_back(last_block, q, qt, k, v, g, gt, lse, delta, block)
    packed, dqkv_low = grads_out(slot_row, dqkv, group)
    if stepped:
        outer_rest = scattered(outer_halves, outer_got)
        dqkv_low, outer_rest, late_w, out_send, out_own, inner_sum = tie(
            dqkv_low, outer_rest, late_w, out_send, out_own, inner_sum
        )
    else:
        outer_sum = lax.psum_scatter(
            jnp.concatenate(outer_halves), PLANE, scatter_dimension=0, tiled=True
        )
    dqkv_own = lax.all_to_all(packed, PLANE, 0, 0, tiled=True)
    out_got = swap(out_send)
    layer_own = (mid + out_own + out_got.astype(F32)).astype(BF)
    layer_out = jnp.stack(ordered(layer_own, swap(layer_own)))

    head_grad = head_weight_grad(dqkv_low, unit, head_w, norms, sums_two)
    head_grad = head_grad.reshape(group, 2, w_rows // 2, 4 * HD)
    keep, send = ordered(head_grad[:, 0], head_grad[:, 1])
    keep = (keep.astype(F32) + swap(send).astype(F32)).astype(BF)
    keep, dqkv_own, layer_out = tie(keep, dqkv_own, layer_out)
    if stepped:
        dqkv_own, outer_rest = tie(dqkv_own, outer_rest)
        outer_sum = lax.psum_scatter(outer_rest, "pb", scatter_dimension=0, tiled=True)
    head_grad = lax.all_to_all(keep, PLANE, 0, 0, tiled=True)
    input_low = input_back(places, side_at, dqkv_own, late_half, late_w, x, dmid, norms)
    head_grad, outer_sum = tie(head_grad, outer_sum)
    input_grad = jnp.stack(ordered(input_low, swap(input_low))).astype(F32)

    norm_parts = head_grad[:, :, 3 * HD : 3 * HD + 8].astype(F32)
    norm_parts = norm_parts[:, :, :4] + norm_parts[:, :, 4:]
    first_sums = sum(norm_parts[place] for place in places)
    second_sums = jnp.sum(norm_parts, axis=0)
    norm_grad = jnp.stack(
        [first_sums[:, 0], second_sums[:, 1], first_sums[:, 2], second_sums[:, 3]]
    )
    norm_grad = jnp.concatenate(ordered(norm_grad, swap(norm_grad)), axis=1)
    qkv_part = jnp.stack([head_grad[place, :, : 3 * HD] for place in places], axis=1)
    qkv_part = qkv_part.reshape(w_rows // 2, 2, heads // 2, 3, HD)
    keep, send = ordered(qkv_part[:, 0], qkv_part[:, 1])
    qkv_grad = jnp.concatenate(ordered(keep, swap(send)), axis=0).astype(F32)
    qkv_grad = qkv_grad.swapaxes(1, 2).reshape(w_rows, 3, half_width)
    inner_grad = inner_sum.astype(F32)
    outer_grad = outer_sum[:, :hidden_half].astype(F32).T
    proj_part = outer_sum[:, hidden_half:]
    keep, send = ordered(proj_part[:, :half_width], proj_part[:, half_width:])
    proj_grad = (keep.astype(F32) + swap(send).astype(F32)).T

    qkv_out = adam_step(w_qkv, qkv_first, qkv_second, qkv_grad / MICRO, RATE_MATRIX, DECAY_RATE)
    proj_out = adam_step(w_proj, proj_first, proj_second, proj_grad / MICRO, RATE_PROJ, DECAY_RATE)
    inner_out = adam_step(
        w_inner, inner_first, inner_second, inner_grad / MICRO, RATE_MATRIX, DECAY_RATE
    )
    outer_out = adam_step(
        w_outer, outer_first, outer_second, outer_grad / MICRO, RATE_MATRIX, DECAY_RATE
    )
    norm_grad = norm_grad / MICRO
    norm_out = adam_step(norm_master, norm_first, norm_second, norm_grad, RATE_NORM, 0.0)
    norm_two_grad = jnp.stack([norm_grad[1], norm_grad[3]])
    return (
        layer_out,
        input_grad,
        *qkv_out,
        *proj_out,
        *inner_out,
        *outer_out,
        *norm_out,
        norm_two_grad,
    )


def solution(mesh):
    tok = P(None, PLANE, None)
    qkv = P(PLANE, None, "ha")
    down = P("ha", PLANE)
    inner = P(PLANE, "ha")
    norm = P(None, PLANE)
    in_specs = (
        (tok, tok, P(), P(), qkv, down, inner, down, norm, norm)
        + (qkv, qkv, down, down, inner, inner, down, down, norm, norm)
    )
    out_specs = (
        (tok, tok, qkv, qkv, qkv, down, down, down)
        + (inner, inner, inner, down, down, down, norm, norm, norm, norm)
    )
    return jax.shard_map(shards, mesh=mesh, in_specs=in_specs, out_specs=out_specs, check_vma=False)
```

```python
import functools

import jax
import jax.numpy as jnp
from jax import lax
from jax.experimental import pallas as pl
from jax.experimental.pallas import tpu as pltpu
from jax.sharding import PartitionSpec as P

HD = 64
MICRO = 2
STEP = 8
NORM_EPS = 1e-05
BETA_ONE = 0.9
BETA_TWO = 0.95
ADAM_EPS = 1e-08
DECAY_RATE = 0.1
RATE_MATRIX = 0.02
RATE_PROJ = 0.6
RATE_NORM = 0.1
BF = jnp.bfloat16
F32 = jnp.float32
PLANE = ("pb", "ka")
VMEM_LIMIT = 60 * 1024 * 1024
SCORE_BLOCK = 512
SHORT = 4096
STRAIGHT = 4
NT = (((1,), (1,)), ((), ()))
NN = (((1,), (0,)), ((), ()))
TN = (((0,), (0,)), ((), ()))


def dot(a, b, dims=NN):
    return lax.dot_general(a, b, dims, preferred_element_type=F32)


def params(steps=1):
    return pltpu.CompilerParams(
        dimension_semantics=("arbitrary",) * steps, vmem_limit_bytes=VMEM_LIMIT
    )


def cost(us):
    return pl.CostEstimate(flops=int(us * 2e8), bytes_accessed=int(us * 1e6), transcendentals=0)


def tie(*arrays):
    return lax.optimization_barrier(arrays)


def whole(shape):
    return pl.BlockSpec(shape, lambda *_: (0,) * len(shape))


def shape_of(shape, dtype):
    return jax.ShapeDtypeStruct(shape, dtype)


def head_places(group, heads):
    return tuple(h * group // heads for h in range(heads))


def normalize(x):
    center = x - jnp.mean(x, axis=-1, keepdims=True)
    spread = jnp.mean(center * center, axis=-1, keepdims=True)
    scale = lax.rsqrt(spread + NORM_EPS)
    return center * scale, scale


def normalize_back(grad, unit, scale):
    return scale * (
        grad
        - jnp.mean(grad, axis=-1, keepdims=True)
        - unit * jnp.mean(grad * unit, axis=-1, keepdims=True)
    )


def low_match(ids):
    low = lax.bitwise_and(ids, 255).astype(F32).astype(BF)
    line = lax.broadcasted_iota(jnp.int32, (256, 1), 0).astype(F32).astype(BF)
    return jnp.where(low == line, jnp.ones((), BF), jnp.zeros((), BF))


def moved(ids_ref, match_ref, source_ref, stack_ref, first):
    features = source_ref.shape[0]
    chunk = stack_ref.shape[1]
    total = None
    for part in range(source_ref.shape[1] // chunk):
        cut = slice(part * chunk, (part + 1) * chunk)
        high = lax.shift_right_logical(ids_ref[:, cut], 8)
        source = source_ref[:, cut]
        for block in range(stack_ref.shape[0] // features):
            stack_ref[block * features : (block + 1) * features, :] = jnp.where(
                high == first + block, source, jnp.zeros((), BF)
            )
        piece = dot(stack_ref[...], match_ref[:, cut], NT)
        total = piece if total is None else total + piece
    return total


def sort_block(total):
    return total if total <= SHORT else 1024


def stack_shape(features, columns, total):
    return pltpu.VMEM((features * columns // 256, min(3072, total)), BF)


def place_kernel(tok_ref, out_ref):
    total = tok_ref.shape[1]
    count = total // 256
    ids = tok_ref[...]
    high = lax.shift_right_logical(ids, 8)
    slot = lax.broadcasted_iota(jnp.int32, (1, total), 1)
    rows = lax.broadcasted_iota(jnp.int32, (count, 1), 0)
    match = low_match(ids)

    def part(values):
        picked = jnp.where(high == rows, values.astype(F32), 0.0).astype(BF)
        return dot(picked, match, NT)

    found = part(lax.shift_right_logical(slot, 8)) * 256.0 + part(lax.bitwise_and(slot, 255))
    found = found.astype(jnp.int32)
    for a in range(count):
        out_ref[:, a * 256 : (a + 1) * 256] = found[a : a + 1]


def slots_of_tokens(tok_row):
    return pl.pallas_call(
        place_kernel,
        grid=(1,),
        in_specs=[whole(tok_row.shape)],
        out_specs=whole(tok_row.shape),
        out_shape=shape_of(tok_row.shape, jnp.int32),
        compiler_params=params(),
        cost_estimate=cost(2),
        name="slots_of_tokens",
    )(tok_row)


def qkv_kernel(x_ref, w_ref, norm_ref, unit_ref, qkv_ref):
    unit, _ = normalize(x_ref[...].astype(F32))
    h = (unit * norm_ref[0:1, :] + norm_ref[2:3, :]).astype(BF)
    unit_ref[...] = unit.astype(BF)
    qkv_ref[...] = dot(w_ref[...], h, NT).astype(BF)


def qkv_piece_kernel(counts, at_ref, *refs):
    sources = refs[: 4 * len(counts)]
    raw_ref = refs[4 * len(counts)]
    unit_ref, qkv_ref, x_ref, w_ref, norm_ref = refs[-5:]

    @pl.when((pl.program_id(0) == 0) & (pl.program_id(1) == 0))
    def _():
        flat = raw_ref[...].astype(F32).T
        w_ref[...] = flat[: 3 * HD].astype(BF)
        norm_ref[...] = flat[3 * HD : 3 * HD + 8]

    rows = x_ref.shape[0] // 2
    even = at_ref[3] == 0
    slot = 0
    for group, count in enumerate(counts):
        for place in range(count):
            for side in range(2):

                @pl.when((pl.program_id(0) == slot) & (pl.program_id(1) == side))
                def _():
                    own = sources[4 * group + side][place]
                    other = sources[4 * group + 2 + side][place]
                    x_ref[:rows, :] = jnp.where(even, own, other)
                    x_ref[rows:, :] = jnp.where(even, other, own)

            slot += 1
    unit, _ = normalize(x_ref[...].astype(F32))
    h = (unit * norm_ref[0:1, :] + norm_ref[2:3, :]).astype(BF)
    unit_ref[...] = unit.astype(BF)
    qkv_ref[...] = dot(w_ref[...], h, NT).astype(BF)


def qkv_of_piece(at, groups, raw, total, buffers):
    counts = tuple(group[0].shape[0] for group in groups)
    pieces = [a for group in groups for a in group]
    _, rows, width = pieces[0].shape
    kept = [pl.BlockSpec(memory_space=pl.ANY)] * len(buffers)
    first = 1 + len(pieces) + 1

    def place(i, j, at):
        return (at[0] ^ (at[1] + i)) * 2 + (at[2] ^ j)

    return pl.pallas_call(
        functools.partial(qkv_piece_kernel, counts),
        grid_spec=pltpu.PrefetchScalarGridSpec(
            num_scalar_prefetch=1,
            grid=(sum(counts), 2),
            in_specs=[whole(a.shape) for a in (*pieces, raw)] + kept,
            out_specs=[
                pl.BlockSpec((2 * rows, width), lambda i, j, at: (place(i, j, at), 0)),
                pl.BlockSpec((3 * HD, 2 * rows), lambda i, j, at: (0, place(i, j, at))),
            ],
            scratch_shapes=[
                pltpu.VMEM((2 * rows, width), BF),
                pltpu.VMEM((3 * HD, width), BF),
                pltpu.VMEM((8, width), F32),
            ],
        ),
        out_shape=[shape_of((total, width), BF), shape_of((3 * HD, total), BF)],
        input_output_aliases={first: 0, first + 1: 1} if buffers else {},
        compiler_params=params(2),
        cost_estimate=cost(3 * sum(counts)),
        name="qkv_piece",
    )(at, *pieces, raw, *buffers)


def qkv_of_head(x_full, head_w, norms):
    rows, width = x_full.shape
    block = min(512, rows)
    return pl.pallas_call(
        qkv_kernel,
        grid=(rows // block,),
        in_specs=[
            pl.BlockSpec((block, width), lambda i: (i, 0)),
            whole(head_w.shape),
            whole(norms.shape),
        ],
        out_specs=[
            pl.BlockSpec((block, width), lambda i: (i, 0)),
            pl.BlockSpec((head_w.shape[0], block), lambda i: (0, i)),
        ],
        out_shape=[shape_of((rows, width), BF), shape_of((head_w.shape[0], rows), BF)],
        compiler_params=params(),
        cost_estimate=cost(8),
        name="qkv_head",
    )(x_full, head_w, norms)


def sort_kernel(tok_ref, qkv_ref, q_ref, qt_ref, k_ref, v_ref, vt_ref, match_ref, stack_ref):
    @pl.when(pl.program_id(0) == 0)
    def _():
        match_ref[...] = low_match(tok_ref[...])

    count = k_ref.shape[0] // 256
    found = moved(tok_ref, match_ref, qkv_ref, stack_ref, pl.program_id(0) * count)
    for part in range(count):
        cut = slice(part * 256, (part + 1) * 256)
        at = 3 * HD * part
        query = found[at : at + HD] * float(HD) ** -0.5
        value = found[at + 2 * HD : at + 3 * HD]
        qt_ref[:, cut] = query.astype(BF)
        q_ref[cut, :] = query.T.astype(BF)
        k_ref[cut, :] = found[at + HD : at + 2 * HD].T.astype(BF)
        v_ref[cut, :] = value.T.astype(BF)
        vt_ref[:, cut] = value.astype(BF)


def sort_qkv(tok_row, qkv):
    rows = qkv.shape[1]
    block = sort_block(rows)
    narrow = (pl.BlockSpec((block, HD), lambda i: (i, 0)), shape_of((rows, HD), BF))
    wide = (pl.BlockSpec((HD, block), lambda i: (0, i)), shape_of((HD, rows), BF))
    outs = (narrow, wide, narrow, narrow, wide)
    return pl.pallas_call(
        sort_kernel,
        grid=(rows // block,),
        in_specs=[whole(tok_row.shape), whole(qkv.shape)],
        out_specs=[spec for spec, _ in outs],
        out_shape=[shape for _, shape in outs],
        scratch_shapes=[pltpu.VMEM((256, rows), BF), stack_shape(3 * HD, block, rows)],
        compiler_params=params(),
        cost_estimate=cost(5),
        name="sort_qkv",
    )(tok_row, qkv)


def causal(keys, queries, ahead):
    return (
        lax.broadcasted_iota(jnp.int32, (keys, queries), 0)
        <= lax.broadcasted_iota(jnp.int32, (keys, queries), 1) + ahead
    )


def forward_kernel(first_ref, qt_ref, k_ref, vt_ref, o_ref, low_ref, lse_ref):
    block = qt_ref.shape[1]
    index = pl.program_id(0)
    half = block // 2

    def part(keys_at, count, query, state, ahead):
        top, total, acc = state
        scores = dot(k_ref[pl.ds(keys_at, count), :], query)
        square = scores * scores + 1.0
        inverse = lax.rsqrt(square)
        radius = square * inverse
        if ahead is not None:
            radius = jnp.where(causal(count, query.shape[1], ahead), radius, -1e30)
        new_top = jnp.maximum(top, jnp.max(radius, axis=0, keepdims=True))
        weights = jnp.exp(radius - new_top)
        shrink = jnp.exp(top - new_top)
        signed = (scores * inverse * weights).astype(BF)
        acc = acc * shrink + dot(vt_ref[:, pl.ds(keys_at, count)], signed)
        total = total * shrink + jnp.sum(weights, axis=0, keepdims=True)
        return (new_top, total, acc)

    def step(key_block, state):
        at = pl.multiple_of(key_block * block, block)
        return part(at, block, qt_ref[...], state, None)

    def diagonal():
        at = pl.multiple_of(index * block, block)
        empty = tuple(jnp.zeros((n, half), F32) for n in (1, 1, HD))
        low = part(at, half, qt_ref[:, :half], empty, 0)
        high = part(at, block, qt_ref[:, half:], empty, half)
        return tuple(jnp.concatenate([x, y], axis=1) for x, y in zip(low, high))

    def finish(state):
        top, total, acc = state
        out = acc * (1.0 / total)
        o_ref[...] = out
        low_ref[...] = out.astype(BF)
        lse_ref[...] = top + jnp.log(total)

    earlier = index - first_ref[index]
    for count in range(STRAIGHT):

        @pl.when(earlier == count)
        def _():
            state = diagonal()
            for back in range(1, count + 1):
                state = step(index - back, state)
            finish(state)

    @pl.when(earlier >= STRAIGHT)
    def _():
        finish(lax.fori_loop(first_ref[index], index, step, diagonal()))


def attend(first_block, qt, k, vt, block):
    rows = k.shape[0]
    return pl.pallas_call(
        forward_kernel,
        grid_spec=pltpu.PrefetchScalarGridSpec(
            num_scalar_prefetch=1,
            grid=(rows // block,),
            in_specs=[
                pl.BlockSpec((HD, block), lambda i, *_: (0, i)),
                whole(k.shape),
                whole(vt.shape),
            ],
            out_specs=[
                pl.BlockSpec((HD, block), lambda i, *_: (0, i)),
                pl.BlockSpec((HD, block), lambda i, *_: (0, i)),
                pl.BlockSpec((1, block), lambda i, *_: (0, i)),
            ],
        ),
        out_shape=[shape_of((HD, rows), F32), shape_of((HD, rows), BF), shape_of((1, rows), F32)],
        compiler_params=params(),
        cost_estimate=cost(13),
        name="attend_fwd",
    )(first_block, qt, k, vt)


def slots_out_kernel(rows, slot_ref, low_ref, out_ref, match_ref, stack_ref):
    half = rows // 2

    @pl.when(pl.program_id(0) == 0)
    def _():
        match_ref[...] = low_match(slot_ref[...])

    owners = out_ref.shape[0]
    count = owners * rows // 256
    found = moved(slot_ref, match_ref, low_ref, stack_ref, pl.program_id(0) * count)
    found = jnp.concatenate([found[p * HD : (p + 1) * HD].T for p in range(count)], axis=0)
    found = found.astype(BF)
    for d in range(owners):
        at = d * rows
        out_ref[d] = jnp.concatenate([found[at : at + half], found[at + half : at + rows]], axis=1)


def slots_out(slot_row, low, group):
    total = slot_row.shape[1]
    rows = total // group
    count = owners_per_step(group, rows)
    return pl.pallas_call(
        functools.partial(slots_out_kernel, rows),
        grid=(group // count,),
        in_specs=[whole(slot_row.shape), whole(low.shape)],
        out_specs=pl.BlockSpec((count, rows // 2, 2 * HD), lambda i: (i, 0, 0)),
        out_shape=shape_of((group, rows // 2, 2 * HD), BF),
        scratch_shapes=[pltpu.VMEM((256, total), BF), stack_shape(HD, count * rows, total)],
        compiler_params=params(),
        cost_estimate=cost(3),
        name="slots_out",
    )(slot_row, low)


def owners_per_step(group, rows, most=16):
    for count in (16, 8, 4, 2, 1):
        if count > (most if group * rows <= SHORT else 4):
            continue
        if group % count == 0 and count * rows % 256 == 0:
            return count
    return group


def sort_grad_kernel(
    tok_ref, packed_ref, o_ref, g_ref, gt_ref, delta_ref, slots_ref, match_ref, stack_ref
):
    group, half, _ = packed_ref.shape

    @pl.when(pl.program_id(0) == 0)
    def _():
        match_ref[...] = low_match(tok_ref[...])
        for d in range(group):
            piece = packed_ref[d].astype(F32).T.astype(BF)
            slots_ref[:, 2 * d * half : (2 * d + 1) * half] = piece[:HD]
            slots_ref[:, (2 * d + 1) * half : (2 * d + 2) * half] = piece[HD:]

    count = g_ref.shape[0] // 256
    found = moved(tok_ref, match_ref, slots_ref, stack_ref, pl.program_id(0) * count)
    for part in range(count):
        cut = slice(part * 256, (part + 1) * 256)
        grad = found[part * HD : (part + 1) * HD]
        gt_ref[:, cut] = grad.astype(BF)
        g_ref[cut, :] = grad.T.astype(BF)
        delta_ref[:, cut] = jnp.sum(grad * o_ref[:, cut], axis=0, keepdims=True)


def sort_grad(tok_row, packed, o):
    rows = o.shape[1]
    block = sort_block(rows)
    wide = pl.BlockSpec((HD, block), lambda i: (0, i))
    return pl.pallas_call(
        sort_grad_kernel,
        grid=(rows // block,),
        in_specs=[whole(tok_row.shape), whole(packed.shape), wide],
        out_specs=[
            pl.BlockSpec((block, HD), lambda i: (i, 0)),
            wide,
            pl.BlockSpec((1, block), lambda i: (0, i)),
        ],
        out_shape=[shape_of((rows, HD), BF), shape_of((HD, rows), BF), shape_of((1, rows), F32)],
        scratch_shapes=[
            pltpu.VMEM((HD, rows), BF),
            pltpu.VMEM((256, rows), BF),
            stack_shape(HD, block, rows),
        ],
        compiler_params=params(),
        cost_estimate=cost(4),
        name="sort_grad",
    )(tok_row, packed, o)


def backward_kernel(
    last_ref, q_ref, qt_ref, k_ref, v_ref, g_ref, gt_ref, lse_ref, delta_ref, out_ref, dq_ref, dk_ref, dv_ref
):
    block = k_ref.shape[0]
    index = pl.program_id(0)

    @pl.when(index == 0)
    def _():
        dq_ref[...] = jnp.zeros_like(dq_ref)

    key = k_ref[...]
    key_t = key.astype(F32).T.astype(BF)
    value = v_ref[...]

    half = block // 2

    def part(at, width, count, ahead):
        cut = pl.ds(at, width)
        scores = dot(key[:count], qt_ref[:, cut])
        square = scores * scores + 1.0
        inverse = lax.rsqrt(square)
        shifted = square * inverse - lse_ref[:, cut]
        if ahead is not None:
            shifted = jnp.where(causal(count, width, ahead), shifted, -1e30)
        weights = jnp.exp(shifted)
        slope = scores * inverse
        along = dot(value[:count], gt_ref[:, cut])
        bend = 1.0 + inverse * inverse * (inverse - 1.0)
        score_grad = weights * (bend * along - slope * delta_ref[:, cut])
        signed = (slope * weights).astype(BF)
        low_grad = score_grad.astype(BF)
        dv = dot(signed, g_ref[cut, :])
        dk = dot(low_grad, q_ref[cut, :])
        dq_ref[:, cut] += dot(key_t[:, :count], low_grad)
        return dk, dv

    def step(query_block):
        return part(pl.multiple_of(query_block * block, block), block, block, None)

    def diagonal():
        at = pl.multiple_of(index * block, block)
        low = part(at, half, half, 0)
        high = part(pl.multiple_of(at + half, half), half, block, half)
        return tuple(jnp.concatenate([x + y[:half], y[half:]], axis=0) for x, y in zip(low, high))

    def finish(dk, dv):
        at = pl.multiple_of(index * block, block)
        out_ref[:HD] = (dq_ref[:, pl.ds(at, block)] * float(HD) ** -0.5).astype(BF)
        out_ref[HD : 2 * HD] = dk.T.astype(BF)
        out_ref[2 * HD :] = dv.T.astype(BF)

    later = last_ref[index] - index
    for count in range(1, STRAIGHT + 1):

        @pl.when(later == count)
        def _():
            dk, dv = diagonal()
            for ahead in range(1, count):
                dk_more, dv_more = step(index + ahead)
                dk, dv = dk + dk_more, dv + dv_more
            finish(dk, dv)

    @pl.when(later > STRAIGHT)
    def _():
        dk_ref[...], dv_ref[...] = diagonal()

        def body(query_block, carry):
            dk_more, dv_more = step(query_block)
            dk_ref[...] += dk_more
            dv_ref[...] += dv_more
            return carry

        lax.fori_loop(index + 1, last_ref[index], body, 0)
        finish(dk_ref[...], dv_ref[...])


def attend_back(last_block, q, qt, k, v, g, gt, lse, delta, block):
    rows = q.shape[0]
    return pl.pallas_call(
        backward_kernel,
        grid_spec=pltpu.PrefetchScalarGridSpec(
            num_scalar_prefetch=1,
            grid=(rows // block,),
            in_specs=[
                whole(q.shape),
                whole(qt.shape),
                pl.BlockSpec((block, HD), lambda i, *_: (i, 0)),
                pl.BlockSpec((block, HD), lambda i, *_: (i, 0)),
                whole(g.shape),
                whole(gt.shape),
                whole(lse.shape),
                whole(delta.shape),
            ],
            out_specs=pl.BlockSpec((3 * HD, block), lambda i, *_: (0, i)),
            scratch_shapes=[
                pltpu.VMEM((HD, rows), F32),
                pltpu.VMEM((block, HD), F32),
                pltpu.VMEM((block, HD), F32),
            ],
        ),
        out_shape=shape_of((3 * HD, rows), BF),
        compiler_params=params(),
        cost_estimate=cost(19),
        name="attend_bwd",
    )(last_block, q, qt, k, v, g, gt, lse, delta)


def head_results(acc, column, w_ref, norm_ref, sums_ref):
    weights = w_ref[...].astype(F32)
    grad = acc * norm_ref[0:1, :] + column * norm_ref[2:3, :]
    sums = jnp.concatenate(
        [
            jnp.sum(weights * acc, axis=0, keepdims=True),
            sums_ref[0:1, :],
            jnp.sum(weights * column, axis=0, keepdims=True),
            sums_ref[1:2, :],
        ],
        axis=0,
    )
    top = sums.astype(BF).astype(F32)
    rest = jnp.concatenate([top, sums - top, jnp.zeros((HD - 8, sums.shape[1]), F32)], axis=0)
    return jnp.concatenate([grad, rest], axis=0).T.astype(BF)


def grads_out_kernel(rows, slot_ref, grad_ref, out_ref, low_ref, match_ref, stack_ref):
    half = rows // 2
    step = pl.program_id(0)

    @pl.when(step == 0)
    def _():
        match_ref[...] = low_match(slot_ref[...])

    count = out_ref.shape[0]
    parts = count * rows // 256
    found = moved(slot_ref, match_ref, grad_ref, stack_ref, step * parts)
    turned = []
    for p in range(parts):
        piece = found[3 * HD * p : 3 * HD * (p + 1)]
        low_ref[:, p * 256 : (p + 1) * 256] = piece.astype(BF)
        turned.append(piece.T)
    turned = jnp.concatenate(turned, axis=0).astype(BF)
    for d in range(count):
        at = d * rows
        out_ref[d, :rows, :] = turned[at : at + rows, : 2 * HD]
        out_ref[d, rows:, :] = jnp.concatenate(
            [turned[at : at + half, 2 * HD :], turned[at + half : at + rows, 2 * HD :]], axis=1
        )


def grads_out(slot_row, grads, group):
    total = slot_row.shape[1]
    rows = total // group
    out_rows = rows + rows // 2
    count = owners_per_step(group, rows)
    return pl.pallas_call(
        functools.partial(grads_out_kernel, rows),
        grid=(group // count,),
        in_specs=[whole(slot_row.shape), whole(grads.shape)],
        out_specs=[
            pl.BlockSpec((count, out_rows, 2 * HD), lambda i: (i, 0, 0)),
            pl.BlockSpec((3 * HD, count * rows), lambda i: (0, i)),
        ],
        out_shape=[shape_of((group, out_rows, 2 * HD), BF), shape_of((3 * HD, total), BF)],
        scratch_shapes=[
            pltpu.VMEM((256, total), BF),
            stack_shape(3 * HD, count * rows, total),
        ],
        compiler_params=params(),
        cost_estimate=cost(7),
        name="grads_out",
    )(slot_row, grads)


def head_weight_kernel(grad_ref, unit_ref, w_ref, norm_ref, sums_ref, head_ref, acc_ref, line_ref):
    step = pl.program_id(0)
    term = dot(grad_ref[...], unit_ref[...])
    line = jnp.sum(grad_ref[...].astype(F32), axis=1, keepdims=True)

    @pl.when(step == 0)
    def _():
        acc_ref[...] = term
        line_ref[...] = line

    @pl.when(step > 0)
    def _():
        acc_ref[...] += term
        line_ref[...] += line

    @pl.when(step == pl.num_programs(0) - 1)
    def _():
        head_ref[...] = head_results(acc_ref[...], line_ref[...], w_ref, norm_ref, sums_ref)


def head_weight_grad(grads, unit, head_w, norms, sums_two):
    total, width = unit.shape
    block = 768 if total % 768 == 0 else total
    return pl.pallas_call(
        head_weight_kernel,
        grid=(total // block,),
        in_specs=[
            pl.BlockSpec((3 * HD, block), lambda i: (0, i)),
            pl.BlockSpec((block, width), lambda i: (i, 0)),
            whole(head_w.shape),
            whole(norms.shape),
            whole(sums_two.shape),
        ],
        out_specs=whole((width, 4 * HD)),
        out_shape=shape_of((width, 4 * HD), BF),
        scratch_shapes=[pltpu.VMEM((3 * HD, width), F32), pltpu.VMEM((3 * HD, 1), F32)],
        compiler_params=params(),
        cost_estimate=cost(5),
        name="head_weight",
    )(grads, unit, head_w, norms, sums_two)


def middle_kernel(places, x_ref, packed_ref, proj_ref, norm_ref, mid_ref, h_ref, o_ref):
    half = packed_ref.shape[1]
    for h, place in enumerate(places):
        piece = packed_ref[place]
        o_ref[:half, h * HD : (h + 1) * HD] = piece[:, :HD]
        o_ref[half:, h * HD : (h + 1) * HD] = piece[:, HD:]
    mid = x_ref[...].astype(F32) + dot(o_ref[...], proj_ref[...], NT)
    mid_ref[...] = mid
    unit, _ = normalize(mid)
    h_ref[...] = (unit * norm_ref[1:2, :] + norm_ref[3:4, :]).astype(BF)


def middle(places, x, packed, weights, proj_at, norms):
    rows, width = x.shape
    return pl.pallas_call(
        functools.partial(middle_kernel, places),
        grid=(1,),
        in_specs=[
            whole(x.shape),
            whole(packed.shape),
            pl.BlockSpec((width, width), lambda i: (0, proj_at)),
            whole(norms.shape),
        ],
        out_specs=[whole((rows, width))] * 3,
        out_shape=[
            shape_of((rows, width), F32),
            shape_of((rows, width), BF),
            shape_of((rows, width), BF),
        ],
        compiler_params=params(),
        cost_estimate=cost(3),
        name="middle",
    )(x, packed, weights, norms)


def hidden_kernel(h_ref, dy_ref, inner_ref, outer_ref, act_ref, dpre_ref, dh_ref, dh_acc):
    pre = dot(h_ref[...], inner_ref[...])
    root = 0.7978845608028654
    squared = pre * pre
    bend = jnp.tanh(root * (pre + 0.044715 * (squared * pre)))
    act_ref[...] = (0.5 * pre * (1.0 + bend)).astype(BF)
    slope = 0.5 * (1.0 + bend) + 0.5 * pre * (1.0 - bend * bend) * (
        root * (1.0 + 3.0 * 0.044715 * squared)
    )
    dpre = (dot(dy_ref[...], outer_ref[...]) * slope).astype(BF)
    dpre_ref[...] = dpre
    dh = dot(dpre, inner_ref[...], NT)

    @pl.when(pl.program_id(0) == 0)
    def _():
        dh_acc[...] = dh

    @pl.when(pl.program_id(0) > 0)
    def _():
        dh_acc[...] += dh

    @pl.when(pl.program_id(0) == pl.num_programs(0) - 1)
    def _():
        dh_ref[...] = dh_acc[...].astype(dh_ref.dtype)


def hidden(h, dy, weights, hidden_width, kind):
    rows, width = h.shape
    chunk = 768
    steps = hidden_width // chunk
    return pl.pallas_call(
        hidden_kernel,
        grid=(steps,),
        in_specs=[
            whole(h.shape),
            whole(dy.shape),
            pl.BlockSpec((width, chunk), lambda i: (0, i)),
            pl.BlockSpec((width, chunk), lambda i: (0, i + steps)),
        ],
        out_specs=[
            pl.BlockSpec((rows, chunk), lambda i: (0, i)),
            pl.BlockSpec((rows, chunk), lambda i: (0, i)),
            whole((rows, width)),
        ],
        out_shape=[
            shape_of((rows, hidden_width), BF),
            shape_of((rows, hidden_width), BF),
            shape_of((rows, width), kind),
        ],
        scratch_shapes=[pltpu.VMEM((rows, width), F32)],
        compiler_params=params(),
        cost_estimate=cost(6),
        name="hidden",
    )(h, dy, weights, weights)


def layer_kernel(own_ref, other_ref, outer_ref, out_ref, send_ref):
    out_ref[...] = dot(own_ref[...], outer_ref[...], NT)
    send_ref[...] = dot(other_ref[...], outer_ref[...], NT).astype(BF)


def layer_terms(act_own, act_other, weights):
    rows, span = act_own.shape
    width = weights.shape[0]
    return pl.pallas_call(
        layer_kernel,
        grid=(1,),
        in_specs=[
            whole(act_own.shape),
            whole(act_other.shape),
            pl.BlockSpec((width, span), lambda i: (0, 1)),
        ],
        out_specs=[whole((rows, width))] * 2,
        out_shape=[shape_of((rows, width), F32), shape_of((rows, width), BF)],
        compiler_params=params(),
        cost_estimate=cost(4),
        name="layer_terms",
    )(act_own, act_other, weights)


def middle_back_kernel(
    places, own_ref, other_ref, dy_ref, mid_ref, norm_ref, proj_ref, dmid_ref, low_ref, packed_ref, sums_ref
):
    half = packed_ref.shape[1]
    dh = own_ref[...] + other_ref[...].astype(F32)
    unit, scale = normalize(mid_ref[...])
    sums_ref[0:1, :] = jnp.sum(dh * unit, axis=0, keepdims=True)
    sums_ref[1:2, :] = jnp.sum(dh, axis=0, keepdims=True)
    dmid = dy_ref[...].astype(F32) + normalize_back(dh * norm_ref[1:2, :], unit, scale)
    dmid_ref[...] = dmid
    low = dmid.astype(BF)
    low_ref[...] = low
    grad = dot(low, proj_ref[...]).astype(BF)
    packed_ref[...] = jnp.zeros_like(packed_ref)
    for h, place in enumerate(places):
        cut = slice(h * HD, (h + 1) * HD)
        packed_ref[place] = jnp.concatenate([grad[:half, cut], grad[half:, cut]], axis=1)


def middle_back(places, group, own, other, dy, mid, norms, weights, proj_at):
    rows, width = mid.shape
    return pl.pallas_call(
        functools.partial(middle_back_kernel, places),
        grid=(1,),
        in_specs=[
            whole(own.shape),
            whole(other.shape),
            whole(dy.shape),
            whole(mid.shape),
            whole(norms.shape),
            pl.BlockSpec((width, width), lambda i: (0, proj_at)),
        ],
        out_specs=[
            whole((rows, width)),
            whole((rows, width)),
            whole((group, rows // 2, 2 * HD)),
            whole((2, width)),
        ],
        out_shape=[
            shape_of((rows, width), F32),
            shape_of((rows, width), BF),
            shape_of((group, rows // 2, 2 * HD), BF),
            shape_of((2, width), F32),
        ],
        compiler_params=params(),
        cost_estimate=cost(4),
        name="middle_back",
    )(own, other, dy, mid, norms, weights)


def split_rows(share, at_ref, block, scratch_ref, keep_ref, send_ref):
    if share == 0:
        half = keep_ref.shape[0]
        keep_ref[...] = block[:half].astype(BF)
        send_ref[...] = block[half:].astype(BF)
        return
    scratch_ref[...] = block
    for pair in range(keep_ref.shape[0] // share):
        cut = slice(pair * share, (pair + 1) * share)
        for target, parity in ((keep_ref, at_ref[0]), (send_ref, 1 - at_ref[0])):
            at = pl.multiple_of((2 * pair + parity) * share, share)
            target[cut, :] = scratch_ref[pl.ds(at, share), :].astype(BF)


def weight_kernel(
    span, share, at_ref, h0, h1, p0, p1, dy0, dy1, a0, a1, keep_in, send_in, keep_out, send_out, scratch_ref
):
    index = pl.program_id(0)

    @pl.when(index < span)
    def _():
        block = dot(h0[...], p0[...], TN) + dot(h1[...], p1[...], TN)
        split_rows(share, at_ref, block, scratch_ref, keep_in, send_in)

    @pl.when(index >= span)
    def _():
        block = dot(dy0[...], a0[...], TN) + dot(dy1[...], a1[...], TN)
        split_rows(share, at_ref, block, scratch_ref, keep_out, send_out)


def weight_grads(share, parity, h_pair, dpre_pair, dy_pair, act_pair, spare):
    rows, width = h_pair[0].shape
    span = act_pair[0].shape[1] // width

    def first(i, at):
        return (0, jnp.minimum(i, span - 1))

    def second(i, at):
        return (0, jnp.maximum(i - span, 0))

    def column(count, where):
        return pl.BlockSpec((count, width), where)

    plain = whole((rows, width))
    half = width // 2
    inner = shape_of((half, span * width), BF)
    outer = shape_of((half, span * width + spare), BF)
    return pl.pallas_call(
        functools.partial(weight_kernel, span, share),
        grid_spec=pltpu.PrefetchScalarGridSpec(
            num_scalar_prefetch=1,
            grid=(2 * span,),
            in_specs=[plain, plain, column(rows, first), column(rows, first)]
            + [plain, plain, column(rows, second), column(rows, second)],
            out_specs=[column(half, first)] * 2 + [column(half, second)] * 2,
            scratch_shapes=[pltpu.VMEM((width, width), F32)],
        ),
        out_shape=[inner, inner, outer, outer],
        compiler_params=params(),
        cost_estimate=cost(8),
        name="weight_grads",
    )(parity, *h_pair, *dpre_pair, *dy_pair, *act_pair)


def proj_kernel(share, at_ref, low_ref, o_ref, kept_ref, sent_ref, keep_ref, send_ref, scratch_ref):
    block = dot(low_ref[...], o_ref[...], TN)
    split_rows(share, at_ref, block, scratch_ref, keep_ref, send_ref)


def proj_grads(share, parity, low, o, keep, send):
    width = o.shape[1]
    last = keep.shape[1] // width - 1
    return pl.pallas_call(
        functools.partial(proj_kernel, share),
        grid_spec=pltpu.PrefetchScalarGridSpec(
            num_scalar_prefetch=1,
            grid=(1,),
            in_specs=[whole(low.shape), whole(o.shape)] + [pl.BlockSpec(memory_space=pl.ANY)] * 2,
            out_specs=[pl.BlockSpec((width // 2, width), lambda i, at: (0, last))] * 2,
            scratch_shapes=[pltpu.VMEM((width, width), F32)],
        ),
        out_shape=[shape_of(keep.shape, BF)] * 2,
        input_output_aliases={3: 0, 4: 1},
        compiler_params=params(),
        cost_estimate=cost(2),
        name="proj_grads",
    )(parity, low, o, keep, send)


def input_back_kernel(places, side_ref, packed_ref, own_ref, other_ref, x_ref, dmid_ref, norm_ref, out_ref, flat_ref):
    rows, _ = x_ref.shape
    half = rows // 2
    for h, place in enumerate(places):
        at = 3 * HD * h
        piece = packed_ref[place]
        flat_ref[:, at : at + 2 * HD] = piece[:rows]
        flat_ref[:half, at + 2 * HD : at + 3 * HD] = piece[rows:, :HD]
        flat_ref[half:, at + 2 * HD : at + 3 * HD] = piece[rows:, HD:]
    span = own_ref.shape[1]
    low, high = flat_ref[:, :span], flat_ref[:, span:]
    first = side_ref[0] == 0
    dh = dot(jnp.where(first, low, high), own_ref[...], NT)
    dh += dot(jnp.where(first, high, low), other_ref[...], NT)
    unit, scale = normalize(x_ref[...].astype(F32))
    out_ref[...] = (dmid_ref[...] + normalize_back(dh * norm_ref[0:1, :], unit, scale)).astype(BF)


def input_back(places, side, packed, own, other, x, dmid, norms):
    rows, width = x.shape
    arrays = (packed, own, other, x, dmid, norms)
    return pl.pallas_call(
        functools.partial(input_back_kernel, places),
        grid_spec=pltpu.PrefetchScalarGridSpec(
            num_scalar_prefetch=1,
            grid=(1,),
            in_specs=[whole(a.shape) for a in arrays],
            out_specs=whole((rows, width)),
            scratch_shapes=[pltpu.VMEM((rows, 3 * HD * len(places)), BF)],
        ),
        out_shape=shape_of((rows, width), BF),
        compiler_params=params(),
        cost_estimate=cost(5),
        name="input_back",
    )(side, *arrays)


def adam_step(master, first_state, second_state, grad_term, step_rate, weight_decay):
    first_new = BETA_ONE * first_state + (1.0 - BETA_ONE) * grad_term
    second_new = BETA_TWO * second_state + (1.0 - BETA_TWO) * grad_term * grad_term
    first_hat = first_new / (1.0 - BETA_ONE**STEP)
    second_hat = second_new / (1.0 - BETA_TWO**STEP)
    master_new = master - step_rate * (
        first_hat / (jnp.sqrt(second_hat) + ADAM_EPS) + weight_decay * master
    )
    return (first_new, second_new, master_new)


def shards(
    tokens,
    cotangent,
    seq_lengths,
    slot_token,
    w_qkv,
    w_proj,
    w_inner,
    w_outer,
    norm_gains,
    norm_biases,
    qkv_first,
    qkv_second,
    proj_first,
    proj_second,
    inner_first,
    inner_second,
    outer_first,
    outer_second,
    norm_first,
    norm_second,
):
    side = lax.axis_index("ha")
    group = lax.axis_size("pb") * lax.axis_size("ka")
    rows, width = tokens.shape[1:]
    total = rows * group
    w_rows = w_qkv.shape[0]
    half_width = w_qkv.shape[2]
    heads = 2 * half_width // HD
    hidden_half = w_inner.shape[1]
    places = head_places(group, heads)
    head_at = [0] * group
    for h, place in enumerate(places):
        head_at[place] = h
    block = min(SCORE_BLOCK, total)

    def swap(a):
        return lax.ppermute(a, "ha", [(0, 1), (1, 0)])

    def ordered(own, other):
        return jnp.where(side == 0, own, other), jnp.where(side == 0, other, own)

    def own_micro(a):
        return lax.dynamic_index_in_dim(a, side, 0, False)

    def other_micro(a):
        return lax.dynamic_index_in_dim(a, 1 - side, 0, False)

    x = own_micro(tokens)
    along_z, along_ka = lax.axis_size("pb"), lax.axis_size("ka")
    stepped = along_z == 4 and along_ka == 4

    def flip(a, axis, size, bit):
        return lax.ppermute(a, axis, [(i, i ^ bit) for i in range(size)])

    if stepped:

        def z_flip(a, bit):
            return flip(a, "pb", along_z, bit)

        def x_flip(a):
            return flip(a, "ka", along_ka, 2)

        def c_flip(a):
            return flip(a, "ka", along_ka, 1)

        own = x[None]
        near, far, own_x, own_c = z_flip(own, 1), z_flip(own, 2), x_flip(own), c_flip(own)
    else:
        x_full = lax.all_gather(x, PLANE, axis=0, tiled=True)
    mine = jnp.concatenate(
        [w_qkv.astype(BF).reshape(w_rows, 3 * half_width), w_proj.astype(BF).T], axis=1
    )
    tok_row = own_micro(slot_token).reshape(1, total)
    mine_other, slot_row = swap(mine), slots_of_tokens(tok_row)
    if stepped:
        near, far = tie(near, far)
        mid_z = jnp.concatenate([near, far])
        last_z, mid_x, mid_c, own_xc = z_flip(far, 1), x_flip(mid_z), c_flip(mid_z), c_flip(own_x)
    low_half, high_half = ordered(mine, mine_other)
    qkv_rows = jnp.concatenate(
        [
            a[:, : 3 * half_width].reshape(w_rows, 3, heads // 2, HD).swapaxes(1, 2)
            for a in (low_half, high_half)
        ],
        axis=1,
    ).reshape(w_rows, heads, 3 * HD)
    proj_rows = jnp.concatenate(
        [a[:, 3 * half_width :] for a in (low_half, high_half)], axis=1
    )
    norm_master = jnp.concatenate([norm_gains, norm_biases], axis=0)
    head_rows = jnp.stack([qkv_rows[:, head_at[d]] for d in range(group)], axis=0)
    head_rows = jnp.concatenate(
        [
            head_rows,
            jnp.broadcast_to(norm_master.astype(BF).T[None], (group, w_rows, 4)),
            jnp.zeros((group, w_rows, HD - 4), BF),
        ],
        axis=2,
    )
    head_w = lax.all_to_all(head_rows, PLANE, 0, 0, tiled=True)
    ends = jnp.cumsum(own_micro(seq_lengths))
    starts = jnp.arange(total // block, dtype=jnp.int32) * block
    first_block = jnp.max(jnp.where(ends[None] <= starts[:, None], ends[None], 0), axis=1) // block
    last_block = jnp.min(jnp.where(ends[None] > starts[:, None], ends[None], total), axis=1) // block
    first_block = first_block.astype(jnp.int32)
    last_block = last_block.astype(jnp.int32)
    dy_own, dy_other = own_micro(cotangent), other_micro(cotangent)
    late_rows = jnp.where(side == 0, qkv_rows[:, : heads // 2], qkv_rows[:, heads // 2 :])
    late_rows = late_rows.reshape(w_rows, -1)
    z, xc = lax.axis_index("pb"), lax.axis_index("ka")
    at_first = jnp.stack([z, 0 * z, xc // 2, xc % 2]).astype(jnp.int32)
    at_last = jnp.stack([z, 0 * z + 3, xc // 2, xc % 2]).astype(jnp.int32)
    ready = (dy_own, dy_other, late_rows, at_first, at_last, first_block, last_block, slot_row)
    if stepped:
        last_z, mid_x, mid_c, own_xc, head_w, *ready = tie(
            last_z, mid_x, mid_c, own_xc, head_w, *ready
        )
        last_x, last_c, mid_xc = x_flip(last_z), c_flip(last_z), c_flip(mid_x)
    else:
        head_w, *ready = tie(head_w, *ready)
    dy_own, dy_other, late_rows, at_first, at_last, first_block, last_block, slot_row = ready
    head_raw = head_w.reshape(width, 4 * HD)

    def turned(raw):
        return raw[:, : 3 * HD].T, raw[:, 3 * HD : 3 * HD + 4].astype(F32).T

    main_rows = jnp.concatenate(
        [
            w_inner.astype(BF),
            w_outer.astype(BF).T,
            proj_rows,
        ],
        axis=1,
    )
    if stepped:
        main_rows, mid_x = tie(main_rows, mid_x)
    else:
        main_rows, x_full = tie(main_rows, x_full)
    main_w = lax.all_gather(main_rows, PLANE, axis=0, tiled=True)
    proj_at = 2 * hidden_half // width

    if stepped:
        groups = ((own, own_x, own_c, own_xc), (mid_z, mid_x, mid_c, mid_xc))
        buffers = qkv_of_piece(at_first, groups, head_raw, total, ())
        last_x, last_c, *buffers = tie(last_x, last_c, *buffers)
        groups = ((last_z, last_x, last_c, c_flip(last_x)),)
        buffers = qkv_of_piece(at_last, groups, head_raw, total, buffers)
        unit, qkv = buffers
    else:
        unit, qkv = qkv_of_head(x_full, *turned(head_raw))
    q, qt, k, v, vt = sort_qkv(tok_row, qkv)
    o, o_low, lse = attend(first_block, qt, k, vt, block)
    late_rows, o_low = tie(late_rows, o_low)
    late_half = lax.all_gather(late_rows, PLANE, axis=0, tiled=True)
    o_packed, head_raw = tie(slots_out(slot_row, o_low, group), head_raw)
    o_packed = lax.all_to_all(o_packed, PLANE, 0, 0, tiled=True)
    head_w, norms = turned(head_raw)
    mid, h_own, o_own = middle(places, x, o_packed, main_w, proj_at, norms)
    h_other = swap(h_own)
    act_own, dpre_own, dh_own = hidden(h_own, dy_own, main_w, hidden_half, F32)
    h_other, dh_own = tie(h_other, dh_own)
    act_other, dpre_other, dh_send = hidden(h_other, dy_other, main_w, hidden_half, BF)
    dh_got = swap(dh_send)
    parity = (xc % 2).reshape(1).astype(jnp.int32)
    side_at = side.reshape(1).astype(jnp.int32)
    share = w_rows if stepped else 0
    halves = weight_grads(
        share, parity, (h_own, h_other), (dpre_own, dpre_other), (dy_own, dy_other), (act_own, act_other), width
    )
    dh_got, *halves = tie(dh_got, *halves)
    inner_halves, outer_halves = halves[:2], halves[2:]

    def pair_sum(halves, at):
        shape = (along_z, along_ka // 2, w_rows, halves[0].shape[1])
        parts = [lax.dynamic_index_in_dim(a.reshape(shape), at, 1, False) for a in halves]
        return parts[0].astype(F32) + parts[1].astype(F32)

    def scattered(halves, got):
        rest = (pair_sum(halves, xc // 2) + got.astype(F32)).astype(BF)
        return rest.reshape(-1, rest.shape[-1])

    if stepped:
        inner_halves = (inner_halves[0], c_flip(inner_halves[1]))
        inner_got = x_flip(pair_sum(inner_halves, 1 - xc // 2).astype(BF))

    dmid, dmid_low, g_packed, sums_two = middle_back(
        places, group, dh_own, dh_got, dy_own, mid, norms, main_w, proj_at
    )
    outer_halves = proj_grads(share, parity, dmid_low, o_own, *outer_halves)
    g_packed = lax.all_to_all(g_packed, PLANE, 0, 0, tiled=True)
    out_own, out_send = layer_terms(act_own, act_other, main_w)
    g_packed, out_own, out_send = tie(g_packed, out_own, out_send)
    if stepped:
        outer_halves = (outer_halves[0], c_flip(outer_halves[1]))
        outer_send = pair_sum(outer_halves, 1 - xc // 2).astype(BF)
        inner_rest = scattered(inner_halves, inner_got)
        outer_got = x_flip(outer_send)
    else:
        inner_sum = lax.psum_scatter(
            jnp.concatenate(inner_halves), PLANE, scatter_dimension=0, tiled=True
        )
    g, gt, delta = sort_grad(tok_row, g_packed, o)
    g, late_half = tie(g, late_half)
    late_w = swap(late_half)
    if stepped:
        g, inner_rest = tie(g, inner_rest)
        inner_sum = lax.psum_scatter(inner_rest, "pb", scatter_dimension=0, tiled=True)
    dqkv = attend_back(last_block, q, qt, k, v, g, gt, lse, delta, block)
    packed, dqkv_low = grads_out(slot_row, dqkv, group)
    if stepped:
        outer_rest = scattered(outer_halves, outer_got)
        dqkv_low, outer_rest, late_w, out_send, out_own, inner_sum = tie(
            dqkv_low, outer_rest, late_w, out_send, out_own, inner_sum
        )
    else:
        outer_sum = lax.psum_scatter(
            jnp.concatenate(outer_halves), PLANE, scatter_dimension=0, tiled=True
        )
    dqkv_own = lax.all_to_all(packed, PLANE, 0, 0, tiled=True)
    out_got = swap(out_send)
    layer_own = (mid + out_own + out_got.astype(F32)).astype(BF)
    layer_out = jnp.stack(ordered(layer_own, swap(layer_own)))

    head_grad = head_weight_grad(dqkv_low, unit, head_w, norms, sums_two)
    head_grad = head_grad.reshape(group, 2, w_rows // 2, 4 * HD)
    keep, send = ordered(head_grad[:, 0], head_grad[:, 1])
    keep = (keep.astype(F32) + swap(send).astype(F32)).astype(BF)
    keep, dqkv_own, layer_out = tie(keep, dqkv_own, layer_out)
    if stepped:
        dqkv_own, outer_rest = tie(dqkv_own, outer_rest)
        outer_sum = lax.psum_scatter(outer_rest, "pb", scatter_dimension=0, tiled=True)
    head_grad = lax.all_to_all(keep, PLANE, 0, 0, tiled=True)
    input_low = input_back(places, side_at, dqkv_own, late_half, late_w, x, dmid, norms)
    head_grad, outer_sum = tie(head_grad, outer_sum)
    input_grad = jnp.stack(ordered(input_low, swap(input_low))).astype(F32)

    norm_parts = head_grad[:, :, 3 * HD : 3 * HD + 8].astype(F32)
    norm_parts = norm_parts[:, :, :4] + norm_parts[:, :, 4:]
    first_sums = sum(norm_parts[place] for place in places)
    second_sums = jnp.sum(norm_parts, axis=0)
    norm_grad = jnp.stack(
        [first_sums[:, 0], second_sums[:, 1], first_sums[:, 2], second_sums[:, 3]]
    )
    norm_grad = jnp.concatenate(ordered(norm_grad, swap(norm_grad)), axis=1)
    qkv_part = jnp.stack([head_grad[place, :, : 3 * HD] for place in places], axis=1)
    qkv_part = qkv_part.reshape(w_rows // 2, 2, heads // 2, 3, HD)
    keep, send = ordered(qkv_part[:, 0], qkv_part[:, 1])
    qkv_grad = jnp.concatenate(ordered(keep, swap(send)), axis=0).astype(F32)
    qkv_grad = qkv_grad.swapaxes(1, 2).reshape(w_rows, 3, half_width)
    inner_grad = inner_sum.astype(F32)
    outer_grad = outer_sum[:, :hidden_half].astype(F32).T
    proj_part = outer_sum[:, hidden_half:]
    keep, send = ordered(proj_part[:, :half_width], proj_part[:, half_width:])
    proj_grad = (keep.astype(F32) + swap(send).astype(F32)).T

    qkv_out = adam_step(w_qkv, qkv_first, qkv_second, qkv_grad / MICRO, RATE_MATRIX, DECAY_RATE)
    proj_out = adam_step(w_proj, proj_first, proj_second, proj_grad / MICRO, RATE_PROJ, DECAY_RATE)
    inner_out = adam_step(
        w_inner, inner_first, inner_second, inner_grad / MICRO, RATE_MATRIX, DECAY_RATE
    )
    outer_out = adam_step(
        w_outer, outer_first, outer_second, outer_grad / MICRO, RATE_MATRIX, DECAY_RATE
    )
    norm_grad = norm_grad / MICRO
    norm_out = adam_step(norm_master, norm_first, norm_second, norm_grad, RATE_NORM, 0.0)
    norm_two_grad = jnp.stack([norm_grad[1], norm_grad[3]])
    return (
        layer_out,
        input_grad,
        *qkv_out,
        *proj_out,
        *inner_out,
        *outer_out,
        *norm_out,
        norm_two_grad,
    )


def solution(mesh):
    tok = P(None, PLANE, None)
    qkv = P(PLANE, None, "ha")
    down = P("ha", PLANE)
    inner = P(PLANE, "ha")
    norm = P(None, PLANE)
    in_specs = (
        (tok, tok, P(), P(), qkv, down, inner, down, norm, norm)
        + (qkv, qkv, down, down, inner, inner, down, down, norm, norm)
    )
    out_specs = (
        (tok, tok, qkv, qkv, qkv, down, down, down)
        + (inner, inner, inner, down, down, down, norm, norm, norm, norm)
    )
    return jax.shard_map(shards, mesh=mesh, in_specs=in_specs, out_specs=out_specs, check_vma=False)
```
